32 devices in a mesh: gx: 8 (over z, x), gy: 4 (over y, core).
Axes of the slice: x: 2, y: 2, z: 4, core: 2. Of those that a mesh axis runs over, the one named last changes fastest.
Arguments:
- tokens: int32 [65536], P(('gx', 'gy')), may hold values from 0 to 26
- timesteps: int32 [256], P(('gx', 'gy')), may hold values from 0 to 999
- cotangent: bfloat16 [65536, 512], P(('gx', 'gy')), may hold values from -6 to 6
- char_table: bfloat16 [27, 512], P(None, ('gx', 'gy')), may hold values from -6 to 6
- time_weight: bfloat16 [512, 512], P(('gx', 'gy')), may hold values from -0.25 to 0.25
- ln1_gain: bfloat16 [512], P(('gx', 'gy')), may hold values from 0.5 to 1.5
- ln1_bias: bfloat16 [512], P(('gx', 'gy')), may hold values from -4 to 4
- w_qkv: bfloat16 [512, 1536], P(('gx', 'gy')), may hold values from -0.25 to 0.25
- w_attn_out: bfloat16 [512, 512], P(('gx', 'gy')), may hold values from -2 to 2
- ln2_gain: bfloat16 [512], P(('gx', 'gy')), may hold values from 0.5 to 1.5
- ln2_bias: bfloat16 [512], P(('gx', 'gy')), may hold values from -4 to 4
- w_up: bfloat16 [512, 2048], P(('gx', 'gy')), may hold values from -0.25 to 0.25
- w_down: bfloat16 [2048, 512], P(('gx', 'gy')), may hold values from -0.125 to 0.125
Outputs:
- result: float32 [65536, 512], P(('gx', 'gy'))
- d_input: float32 [65536, 512], P(('gx', 'gy'))
- d_char_table: float32 [27, 512], P(None, ('gx', 'gy'))
- d_time_weight: float32 [512, 512], P(('gx', 'gy'))
- d_ln1_gain: float32 [512], P(('gx', 'gy'))
- d_ln1_bias: float32 [512], P(('gx', 'gy'))
- d_w_qkv: float32 [512, 1536], P(('gx', 'gy'))
- d_w_attn_out: float32 [512, 512], P(('gx', 'gy'))
- d_ln2_gain: float32 [512], P(('gx', 'gy'))
- d_ln2_bias: float32 [512], P(('gx', 'gy'))
- d_w_up: float32 [512, 2048], P(('gx', 'gy'))
- d_w_down: float32 [2048, 512], P(('gx', 'gy'))
The draws below stay inside these ranges and needn't reach their ends.
All inputs are finite; a program needn't handle non-finite values.
Results may differ from the reference program's by a relative error of at most 0.013.
Values may be sent and summed in bfloat16 or wider, within the bound.
A program may use at most 192 MiB of HBM per device.

```python
import math
import jax
import jax.numpy as jnp
import numpy as np
from jax import lax

D = 512
HEADS = 8
HEAD_DIM = 64
FF = 2048
VOCAB = 27
TSTEPS = 1000
SEQ_LEN = 256
SEQS = 256
TOKENS = 65536


def set_ends(values, own_key, low, largest):
    longest = values.shape.index(max(values.shape))
    spots = []
    for shift in (0, 1):
        where = [jax.random.randint(jax.random.fold_in(own_key, axis), (), 0, length) for axis, length in enumerate(values.shape)]
        where[longest] = (where[longest] + shift) % values.shape[longest]
        spots.append(tuple(where))
    return values.at[spots[0]].set(low).at[spots[1]].set(largest)


def raised(entries, rng, source, target, shards_of, factor):
    def block_of(position):
        return (jnp.arange(entries.shape[position]) // (entries.shape[position] // shards_of)).reshape((-1,) + (1,) * (entries.ndim - 1 - position))

    first = jax.random.permutation(rng, shards_of)[block_of(target)]
    far = (block_of(target) + shards_of // 2) % shards_of
    return jnp.where((block_of(source) == first) | (block_of(source) == far), factor * entries, entries)


def block_levels(rng, dims, shards, low, largest):
    level = 1.0
    for axis_at, shards_of in shards:
        draws = jax.random.uniform(jax.random.fold_in(jax.random.fold_in(rng, 6), axis_at), (shards_of,), jnp.float32, low / len(shards), largest / len(shards))
        level = level * jnp.repeat(jnp.exp(draws), dims[axis_at] // shards_of).reshape((-1,) + (1,) * (len(dims) - 1 - axis_at))
    return level


def cumulative_ranks(count, lean):
    weights = [(1 << 20) // math.isqrt(rank ** lean) + 1 for rank in range(1, count + 1)]
    scale = 1 + sum(weights) // (1 << 30)
    return np.cumsum(np.array([max(1, weight // scale) for weight in weights]))


def skewed_ids(stream_key, extent, count, lean):
    table = cumulative_ranks(count, lean)
    lot = jax.random.randint(jax.random.fold_in(stream_key, 1), extent, 0, int(table[count - 1]))
    grade = jnp.searchsorted(jnp.asarray(table, jnp.int32), lot, side="right")
    return jax.random.permutation(jax.random.fold_in(stream_key, 2), count)[grade].astype(jnp.int32)


def gaussian(key, extent, scale, most, shards=(), kind=jnp.bfloat16):
    loudness = block_levels(key, extent, shards, -0.22, 0.18) if shards else 1.0
    array = jax.random.normal(key, extent, jnp.float32) * scale * loudness
    return jnp.minimum(jnp.maximum(array, -most), most).astype(kind)


def bell_draw_with(own_key, extent, scale, reach, split, heavy, kind=jnp.bfloat16):
    entries = scale * jax.random.normal(own_key, extent, jnp.float32)
    if split:
        entries = entries * block_levels(own_key, extent, split, -0.22, 0.18)
    return jnp.clip(raised(entries, jax.random.fold_in(own_key, 3), *heavy), -reach, reach).astype(kind)


def setup_inputs(seed: int = 0) -> dict:
    keys = jax.random.split(jax.random.key(seed), 14)
    return {
        "tokens": set_ends(skewed_ids(keys[0], (TOKENS,), VOCAB, 1), jax.random.fold_in(keys[0], 3), 0, VOCAB - 1).astype(jnp.int32),
        "timesteps": set_ends(jax.random.randint(keys[1], (SEQS,), 0, TSTEPS), jax.random.fold_in(keys[1], 1), 0, TSTEPS - 1).astype(jnp.int32),
        "cotangent": bell_draw_with(keys[2], (TOKENS, D), 1.0, 6.0, ((0, 32),), (0, 1, 32, 2.75)),
        "char_table": gaussian(keys[3], (VOCAB, D), 1.0, 6.0, ((1, 32),)),
        "time_weight": gaussian(keys[4], (D, D), D ** -0.5, 0.25, ((0, 32),)),
        "ln1_gain": jnp.clip(1.0 + 0.1 * jax.random.normal(keys[5], (D,), jnp.float32), 0.5, 1.5).astype(jnp.bfloat16),
        "ln1_bias": gaussian(keys[6], (D,), 0.3, 4.0, ((0, 32),)),
        "w_qkv": gaussian(keys[7], (D, 3 * D), D ** -0.5, 0.25, ((0, 32),)),
        "w_attn_out": gaussian(keys[8], (D, D), (D // 64) ** -0.5, 2.0, ((0, 32),)),
        "ln2_gain": jnp.clip(1.0 + 0.1 * jax.random.normal(keys[9], (D,), jnp.float32), 0.5, 1.5).astype(jnp.bfloat16),
        "ln2_bias": gaussian(keys[10], (D,), 0.3, 4.0, ((0, 32),)),
        "w_up": gaussian(keys[11], (D, FF), D ** -0.5, 0.25, ((0, 32),)),
        "w_down": gaussian(keys[12], (FF, D), FF ** -0.5, 0.125, ((0, 32),)),
    }


EPSILON = 1e-05
full_precision = lax.Precision.HIGHEST

@jax.custom_vjp
def low(v):
    return lax.optimization_barrier(v.astype(jnp.bfloat16)).astype(jnp.float32)

@jax.custom_vjp
def low_back(v):
    return v

def low_keep(v):
    return (low(v), None)

def low_pass(kept, grad):
    return (grad,)

def back_keep(v):
    return (v, None)

def back_low(kept, grad):
    return (low(grad),)
low.defvjp(low_keep, low_pass)
low_back.defvjp(back_keep, back_low)

def layer_norm(values, gain, offset):
    center = lax.optimization_barrier(jnp.mean(values, axis=-1, keepdims=True))
    shifted = values - center
    spread = lax.optimization_barrier(jnp.mean(shifted * shifted, axis=-1, keepdims=True))
    return shifted * lax.rsqrt(spread + EPSILON) * gain + offset

def sinusoid(steps, features):
    half_width = features // 2
    frequency = jnp.exp(-math.log(10000.0) * jnp.arange(half_width, dtype=jnp.float32) / half_width)
    angles = steps.astype(jnp.float32)[:, None] * frequency[None, :]
    return jnp.concatenate([jnp.sin(angles), jnp.cos(angles)], axis=1)

def block(start, weights):
    gain_one, bias_one, qkv_weight, proj_weight, gain_two, bias_two, up_weight, down_weight = weights
    row_count = start.shape[0]
    seq_count = row_count // SEQ_LEN
    normed = low(layer_norm(start, gain_one, bias_one))
    project = low(low_back(jnp.dot(normed, qkv_weight, precision=full_precision)))
    shaped = project.reshape(seq_count, SEQ_LEN, 3, HEADS, HEAD_DIM)
    scores = low_back(jnp.einsum('sqhd,skhd->shqk', shaped[:, :, 0], shaped[:, :, 1], precision=full_precision) * (1.0 / math.sqrt(HEAD_DIM)))
    probabilities = low(jax.nn.softmax(scores, axis=-1))
    mixed = jnp.einsum('shqk,skhd->sqhd', probabilities, shaped[:, :, 2], precision=full_precision)
    mixed = low(low_back(mixed.reshape(row_count, HEADS * HEAD_DIM)))
    middle = start + low_back(jnp.dot(mixed, proj_weight, precision=full_precision))
    normed_two = low(layer_norm(middle, gain_two, bias_two))
    hidden = low_back(jnp.dot(normed_two, up_weight, precision=full_precision))
    active = low(low_back(jax.nn.gelu(hidden, approximate=False)))
    return middle + low_back(jnp.dot(active, down_weight, precision=full_precision))

def embed(table, stamp_weight, tokens, timesteps):
    waves = low(sinusoid(timesteps, D))
    stamps = low_back(jnp.dot(waves, stamp_weight, precision=full_precision))
    return table[tokens] + jnp.repeat(stamps, SEQ_LEN, axis=0)

def reference(tokens, timesteps, cotangent, char_table, time_weight, ln1_gain, ln1_bias, w_qkv, w_attn_out, ln2_gain, ln2_bias, w_up, w_down):
    weights = tuple((item.astype(jnp.float32) for item in (ln1_gain, ln1_bias, w_qkv, w_attn_out, ln2_gain, ln2_bias, w_up, w_down)))
    table = char_table.astype(jnp.float32)
    stamp_weight = time_weight.astype(jnp.float32)
    start, embed_pull = jax.vjp(lambda first, second: embed(first, second, tokens, timesteps), table, stamp_weight)
    group_size = math.gcd(SEQS, 16)

    def whole(values, params):
        pieces = values.reshape(SEQS // group_size, group_size * SEQ_LEN, D)
        stepper = jax.checkpoint(block)

        def scan_step(carry, piece):
            return (carry, stepper(piece, params))
        _, outputs = lax.scan(scan_step, jnp.zeros((), jnp.float32), pieces)
        return outputs.reshape(TOKENS, D)
    result, block_pull = jax.vjp(whole, start, weights)
    grad_start, grad_weights = block_pull(cotangent.astype(jnp.float32))
    grad_table, grad_stamp = embed_pull(grad_start)
    return (result, grad_start, grad_table, grad_stamp, grad_weights[0], grad_weights[1], grad_weights[2], grad_weights[3], grad_weights[4], grad_weights[5], grad_weights[6], grad_weights[7])
```

```python
import functools
import math

import jax
import jax.numpy as jnp
from jax import lax
from jax.experimental import pallas as pl
from jax.experimental.pallas import tpu as pltpu
from jax.sharding import PartitionSpec as P

F32, BF16 = jnp.float32, jnp.bfloat16

MESH = pl.DeviceIdType.MESH


def place():
    gx, gy = lax.axis_index("gx"), lax.axis_index("gy")
    return gx // 2, gx % 2, gy // 2, gy % 2


def device(z, x, y, c):
    return (z * 2 + x, y * 2 + c)


def greet(nz):
    z, x, y, c = place()
    barrier = pltpu.get_barrier_semaphore()

    def hello(*where):
        pl.semaphore_signal(barrier, inc=1, device_id=device(*where), device_id_type=MESH)

    hello(z, x, y, 1 - c)
    hello(z, 1 - x, y, c)
    hello(z, x, 1 - y, c)

    @pl.when(z > 0)
    def _():
        hello(z - 1, x, y, c)

    @pl.when(z < nz - 1)
    def _():
        hello(z + 1, x, y, c)

    pl.semaphore_wait(barrier, 3 + jnp.minimum(z, 1) + jnp.minimum(nz - 1 - z, 1))


def send(src, dst, sems, slot, where):
    send_sems, recv_sems = sems
    return pltpu.make_async_remote_copy(
        src_ref=src, dst_ref=dst, send_sem=send_sems.at[slot], recv_sem=recv_sems.at[slot],
        device_id=device(*where), device_id_type=MESH)


def middle_of(width):
    return width // 256 * 128


GATHER_SLOTS = lambda nz: 2 * (nz - 1) + 4 + 5


class Gather:
    def __init__(self, nz, out, sems):
        self.nz, self.out, self.sems = nz, out, sems
        self.base = 2 * (nz - 1)

    def own(self, value):
        z, x, y, c = place()
        self.out[z, x, y, c] = value

    def along(self, step, act):
        nz = self.nz
        z, x, y, c = place()
        for way, slot in ((1, 2 * (step - 1)), (-1, 2 * (step - 1) + 1)):
            origin = z - way * (step - 1)
            to = z + way
            can_send = (origin >= 0) & (origin < nz) & (to >= 0) & (to < nz)
            arrives = (z - way * step >= 0) & (z - way * step < nz)
            if act == "start":
                @pl.when(can_send)
                def _():
                    send(self.out.at[origin, x, y, c], self.out.at[origin, x, y, c], self.sems, slot, (to, x, y, c)).start()
            elif act == "recv":
                come = z - way * step

                @pl.when(arrives)
                def _():
                    send(self.out.at[come, x, y, c], self.out.at[come, x, y, c], self.sems, slot, (z - way, x, y, c)).wait_recv()
            else:
                @pl.when(can_send)
                def _():
                    send(self.out.at[origin, x, y, c], self.out.at[origin, x, y, c], self.sems, slot, (to, x, y, c)).wait_send()

    def copy(self, name, comes=False):
        z, x, y, c = place()
        half = middle_of(self.out.shape[-1])
        cuts = {"": slice(None), "lo": pl.ds(0, half), "hi": pl.ds(half, self.out.shape[-1] - half)}
        to, a, b, k, cut, slot = {
            "x": ("x", x, y, c, "", 0), "y": ("y", x, y, c, "", 1),
            "xd": ("x", x, 1 - y, c, "lo", 2), "yd": ("y", 1 - x, y, c, "hi", 3),
            "c0": ("c", x, y, c, "", 4), "c1": ("c", 1 - x, y, c, "", 5), "c2": ("c", x, 1 - y, c, "", 6),
            "c3": ("c", 1 - x, 1 - y, c, "lo", 7), "c4": ("c", 1 - x, 1 - y, c, "hi", 8)}[name]
        if comes:
            a, b, k = (1 - a, b, k) if to == "x" else (a, 1 - b, k) if to == "y" else (a, b, 1 - k)
        where = {"x": (z, 1 - x, y, c), "y": (z, x, 1 - y, c), "c": (z, x, y, 1 - c)}[to]
        ref = self.out.at[pl.ds(0, self.nz), a, b, k]
        if cut:
            ref = ref.at[:, :, cuts[cut]]
        return send(ref, ref, self.sems, self.base + slot, where)

    def start(self, *names):
        for name in names:
            self.copy(name).start()

    def arrive(self, *names):
        for name in names:
            self.copy(name, comes=True).wait_recv()

    def along_z(self):
        self.along(1, "start")
        for step in range(1, self.nz):
            self.along(step, "recv")
            if step < self.nz - 1:
                self.along(step + 1, "start")

    def finish(self):
        for step in range(1, self.nz):
            self.along(step, "sent")
        for name in ("x", "y", "xd", "yd", "c0", "c1", "c2", "c3", "c4"):
            self.copy(name).wait_send()


def gather_kernel(nz, count, *refs):
    ins, outs, sems = refs[:count], refs[count:2 * count], refs[2 * count:]
    groups = [Gather(nz, outs[i], (sems[2 * i], sems[2 * i + 1])) for i in range(count)]
    for group, ref in zip(groups, ins):
        group.own(ref[...])
    greet(nz)
    for i, group in enumerate(groups):
        group.along_z()
        group.start("x", "y", "c0")
        if i > 0:
            before = groups[i - 1]
            before.arrive("x", "y")
            before.start("xd", "yd", "c1", "c2")
        if i > 1:
            before = groups[i - 2]
            before.arrive("xd", "yd")
            before.start("c3", "c4")
    last = groups[-1]
    last.arrive("x", "y")
    last.start("xd", "yd", "c1", "c2")
    for group in groups[-2:]:
        group.arrive("xd", "yd")
        group.start("c3", "c4")
    for group in groups:
        group.arrive("c0", "c1", "c2", "c3", "c4")
        group.finish()


def gather(nz, shards):
    count = len(shards)
    sems = []
    for _ in shards:
        sems += [pltpu.SemaphoreType.DMA((GATHER_SLOTS(nz),)), pltpu.SemaphoreType.DMA((GATHER_SLOTS(nz),))]
    vmem = pl.BlockSpec(memory_space=pltpu.VMEM)
    return pl.pallas_call(
        functools.partial(gather_kernel, nz, count),
        out_shape=[jax.ShapeDtypeStruct((nz, 2, 2, 2) + s.shape, s.dtype) for s in shards],
        in_specs=[vmem] * count, out_specs=[vmem] * count, scratch_shapes=sems,
        compiler_params=pltpu.CompilerParams(collective_id=0, has_side_effects=True, vmem_limit_bytes=60 * 2**20),
        name="gather_weights",
    )(*shards)


SCATTER_SLOTS = lambda nz: 2 * (nz - 1) + 5


class Scatter:
    def __init__(self, nz, mine, own, far, near, line, sems):
        self.nz, self.mine, self.own, self.far, self.near, self.line, self.sems = nz, mine, own, far, near, line, sems
        self.width = mine.shape[-1]
        self.half = middle_of(self.width)
        self.base = 2 * (nz - 1)

    def cuts(self):
        return pl.ds(0, self.half), pl.ds(self.half, self.width - self.half)

    def copy(self, name):
        z, x, y, c = place()
        nz, own, sems, base = self.nz, self.own, self.sems, self.base
        lo, hi = self.cuts()
        all_z = pl.ds(0, nz)
        xp, yp, cp = (z, 1 - x, y, c), (z, x, 1 - y, c), (z, x, y, 1 - c)
        if name == "c":
            return send(self.mine.at[all_z, :, :, 1 - c], own, sems, base, cp)
        if name == "xd":
            return send(own.at[all_z, 1 - x, 1 - y, :, lo], self.far.at[:, :, lo], sems, base + 1, xp)
        if name == "yd":
            return send(own.at[all_z, 1 - x, 1 - y, :, hi], self.far.at[:, :, hi], sems, base + 2, yp)
        if name == "x":
            return send(own.at[all_z, 1 - x, y], self.near.at[0], sems, base + 3, xp)
        return send(own.at[all_z, x, 1 - y], self.near.at[1], sems, base + 4, yp)

    def add(self, a, b, value, cols=None):
        cols = cols if cols is not None else pl.ds(0, self.width)

        def one(k, _):
            spot = (k, a, b, slice(None), cols)
            self.own[spot] = (self.own[spot].astype(jnp.float32) + value(k, cols)).astype(self.own.dtype)
            return 0
        lax.fori_loop(0, self.nz, one, 0)

    def cores(self):
        self.copy("c").start()

    def corner(self):
        z, x, y, c = place()
        self.copy("c").wait()
        for a, b in ((1 - x, 1 - y), (1 - x, y), (x, 1 - y), (x, y)):
            self.add(a, b, lambda k, cols, a=a, b=b: self.mine[k, a, b, c, :, cols].astype(jnp.float32))
            if a is not x and b is not y:
                self.copy("xd").start()
                self.copy("yd").start()

    def sides(self):
        z, x, y, c = place()
        lo, hi = self.cuts()
        self.copy("xd").wait()
        self.add(x, 1 - y, lambda k, cols: self.far[k, :, cols].astype(jnp.float32), lo)
        self.copy("y").start()
        self.copy("yd").wait()
        self.add(1 - x, y, lambda k, cols: self.far[k, :, cols].astype(jnp.float32), hi)
        self.copy("x").start()

    def column(self):
        z, x, y, c = place()
        self.copy("x").wait()
        self.copy("y").wait()
        self.add(x, y, lambda k, cols: self.near[0, k, :, cols].astype(jnp.float32) + self.near[1, k, :, cols].astype(jnp.float32))

    def along(self, step, act):
        nz = self.nz
        z, x, y, c = place()
        far = nz - step
        for way, slot in ((1, 2 * (step - 1)), (-1, 2 * (step - 1) + 1)):
            goes = z + way * far
            can_send = (goes >= 0) & (goes < nz)
            comes = z + way * (far - 1)
            back = z - way
            arrives = (back >= 0) & (back < nz) & (comes >= 0) & (comes < nz)
            landing = self.line.at[slot]
            if act == "start":
                @pl.when(can_send)
                def _():
                    send(self.own.at[goes, x, y], landing, self.sems, slot, (z + way, x, y, c)).start()
            elif act == "recv":
                @pl.when(arrives)
                def _():
                    send(self.own.at[comes, x, y], landing, self.sems, slot, (back, x, y, c)).wait_recv()
                    spot = (comes, x, y)
                    self.own[spot] = (self.own[spot].astype(jnp.float32) + self.line[slot].astype(jnp.float32)).astype(self.own.dtype)
            else:
                @pl.when(can_send)
                def _():
                    send(self.own.at[goes, x, y], landing, self.sems, slot, (z + way, x, y, c)).wait_send()

    def total(self):
        z, x, y, c = place()
        for step in range(1, self.nz):
            self.along(step, "sent")
        return self.own[z, x, y].astype(jnp.float32)


def scatter_kernel(nz, count, *refs):
    ins, outs = refs[:count], refs[count:2 * count]
    rest = refs[2 * count:]
    groups = [Scatter(nz, ins[i], *rest[6 * i:6 * i + 4], rest[6 * i + 4:6 * i + 6]) for i in range(count)]
    greet(nz)
    for group in groups:
        group.cores()
    for i in range(count + 3):
        for stage, act in ((3, "line"), (2, "column"), (1, "sides"), (0, "corner")):
            k = i - stage
            if 0 <= k < count:
                if act == "corner":
                    groups[k].corner()
                elif act == "sides":
                    groups[k].sides()
                elif act == "column":
                    groups[k].column()
                    groups[k].along(1, "start")
                else:
                    for step in range(1, nz):
                        groups[k].along(step, "recv")
                        if step < nz - 1:
                            groups[k].along(step + 1, "start")
    for group, out in zip(groups, outs):
        out[...] = group.total()


def scatter_scratch(nz, tail, dtype):
    return [
        pltpu.VMEM((nz, 2, 2) + tail, dtype), pltpu.VMEM((nz,) + tail, dtype), pltpu.VMEM((2, nz) + tail, dtype),
        pltpu.VMEM((2 * (nz - 1),) + tail, dtype),
        pltpu.SemaphoreType.DMA((SCATTER_SLOTS(nz),)), pltpu.SemaphoreType.DMA((SCATTER_SLOTS(nz),))]


def scatter(nz, partials):
    count = len(partials)
    scratch = []
    for p in partials:
        scratch += scatter_scratch(nz, p.shape[4:], p.dtype)
    vmem = pl.BlockSpec(memory_space=pltpu.VMEM)
    return pl.pallas_call(
        functools.partial(scatter_kernel, nz, count),
        out_shape=[jax.ShapeDtypeStruct(p.shape[4:], jnp.float32) for p in partials],
        in_specs=[vmem] * count, out_specs=[vmem] * count, scratch_shapes=scratch,
        compiler_params=pltpu.CompilerParams(collective_id=1, has_side_effects=True, vmem_limit_bytes=60 * 2**20),
        name="scatter_grads",
    )(*partials)


HEADS = 8
EPSILON = 1e-05
VMEM_LIMIT = 60 * 2**20


def dot(left, right):
    return jnp.dot(left, right, preferred_element_type=F32)


def dot_nt(left, right):
    return lax.dot_general(left, right, (((1,), (1,)), ((), ())), preferred_element_type=F32)


def norm_rows(values):
    count = values.shape[0]
    shifted = values - jnp.sum(values, axis=0, keepdims=True) * (1.0 / count)
    inverse = lax.rsqrt(jnp.sum(shifted * shifted, axis=0, keepdims=True) * (1.0 / count) + EPSILON)
    return shifted * inverse, inverse


def norm_rows_back(grad, gain, normed, inverse):
    count = grad.shape[0]
    scaled = grad * gain
    lean = jnp.sum(scaled, axis=0, keepdims=True) * (1.0 / count)
    turn = jnp.sum(scaled * normed, axis=0, keepdims=True) * (1.0 / count)
    return inverse * (scaled - lean - normed * turn)


def fold(values):
    total = values[:, :128]
    for k in range(1, values.shape[1] // 128):
        total = total + values[:, 128 * k:128 * (k + 1)]
    return total


def param(small, column):
    return small[:, column:column + 1].astype(F32)


def attention_forward(tokens, waves, small, time_w, w_qkv, w_out):
    seqs, _, length = tokens.shape
    feat = time_w.shape[0]
    head = feat // HEADS
    turn = math.log2(math.e) / math.sqrt(head)

    def kernel(tok_ref, waves_ref, small_ref, time_ref, qkv_ref, out_ref, start_o, middle_o, project_o, powers_o, inv_o, mixed_o, qkv_t, out_t, stamps):
        i = pl.program_id(0)

        @pl.when(i == 0)
        def _():
            qkv_t[...] = qkv_ref[...].T
            out_t[...] = out_ref[...].T
            stamps[...] = dot(time_ref[...].T, waves_ref[...])

        tok = tok_ref[0]
        one_hot = (lax.broadcasted_iota(jnp.int32, (128, length), 0) == tok).astype(BF16)
        lane = lax.broadcasted_iota(jnp.int32, stamps.shape, 1)
        stamp = jnp.sum(jnp.where(lane == i, stamps[...], 0.0), axis=1, keepdims=True)
        start = dot(small_ref[...], one_hot) + stamp
        start_o[...] = start
        normed, _ = norm_rows(start)
        low = (normed * param(small_ref[...], 27) + param(small_ref[...], 28)).astype(BF16)
        project_o[...] = dot(qkv_t[...], low).astype(BF16)
        for h in range(HEADS):
            rows = pl.ds(h * head, head)
            keys = project_o[pl.ds(feat + h * head, head), :].T
            scores = dot(keys, project_o[rows, :])
            top = jnp.max(scores, axis=0, keepdims=True)
            powers = jnp.exp2((scores - top) * turn)
            inverse = 1.0 / jnp.sum(powers, axis=0, keepdims=True)
            low_powers = powers.astype(BF16)
            powers_o[0, h] = low_powers
            inv_o[0, h:h + 1, :] = inverse
            mixed_o[rows, :] = (dot(project_o[pl.ds(2 * feat + h * head, head), :], low_powers) * inverse).astype(BF16)
        middle_o[...] = start + dot(out_t[...], mixed_o[...])

    whole = lambda a: pl.BlockSpec(a.shape, lambda i: (0,) * a.ndim)
    block = lambda rows: pl.BlockSpec((rows, length), lambda i: (0, i))
    n = seqs * length
    return pl.pallas_call(
        kernel, grid=(seqs,),
        in_specs=[pl.BlockSpec((1, 1, length), lambda i: (i, 0, 0))] + [whole(a) for a in (waves, small, time_w, w_qkv, w_out)],
        out_specs=[block(feat), block(feat), block(3 * feat), pl.BlockSpec((1, HEADS, length, length), lambda i: (i, 0, 0, 0)),
                   pl.BlockSpec((1, HEADS, length), lambda i: (i, 0, 0)), block(feat)],
        out_shape=[jax.ShapeDtypeStruct((feat, n), F32), jax.ShapeDtypeStruct((feat, n), F32), jax.ShapeDtypeStruct((3 * feat, n), BF16),
                   jax.ShapeDtypeStruct((seqs, HEADS, length, length), BF16), jax.ShapeDtypeStruct((seqs, HEADS, length), F32),
                   jax.ShapeDtypeStruct((feat, n), BF16)],
        scratch_shapes=[pltpu.VMEM((3 * feat, feat), BF16), pltpu.VMEM((feat, feat), BF16), pltpu.VMEM((feat, 128), F32)],
        compiler_params=pltpu.CompilerParams(vmem_limit_bytes=VMEM_LIMIT), name="attention_forward",
    )(tokens, waves, small, time_w, w_qkv, w_out)


def feed_forward(middle, cotangent, small, w_up, w_down, chunk=256):
    feat, n = middle.shape
    ff = w_up.shape[1]
    steps = n // chunk
    tile = 256

    def kernel(mid_ref, cot_ref, small_ref, up_ref, down_ref, result_o, grad_o, ln_o, dup_o, ddown_o,
               up_t, down_t, act, gh, cot_f, low_f):
        i = pl.program_id(0)

        @pl.when(i == 0)
        def _():
            up_t[...] = up_ref[...].T
            down_t[...] = down_ref[...].T
            ln_o[...] = jnp.zeros_like(ln_o)

        cols = pl.ds(pl.multiple_of(i * chunk, chunk), chunk)
        middle = mid_ref[...]
        normed, inverse = norm_rows(middle)
        gain = param(small_ref[...], 29)
        low = (normed * gain + param(small_ref[...], 30)).astype(BF16)
        low_f[:, cols] = low
        cot = cot_ref[...].T
        cot_f[:, cols] = cot
        for j in range(ff // tile):
            rows = pl.ds(j * tile, tile)
            hidden = dot(up_t[rows, :], low)
            grad_active = dot(down_ref[rows, :], cot).astype(BF16).astype(F32)
            cdf = 0.5 + 0.5 * lax.erf(hidden * math.sqrt(0.5))
            bell = jnp.exp2(hidden * hidden * (-0.5 * math.log2(math.e))) * (1.0 / math.sqrt(2.0 * math.pi))
            act[rows, cols] = (hidden * cdf).astype(BF16)
            gh[rows, cols] = (grad_active * (cdf + hidden * bell)).astype(BF16)
        result_o[...] = (middle + dot(down_t[...], act[:, cols])).T
        grad_normed = dot(up_ref[...], gh[:, cols])
        grad_o[...] = cot.astype(F32) + norm_rows_back(grad_normed, gain, normed, inverse)
        ln_o[0] += fold(grad_normed * normed)
        ln_o[1] += fold(grad_normed)

        @pl.when(i == steps - 1)
        def _():
            def up(j, _):
                rows = pl.ds(pl.multiple_of(j * tile, tile), tile)
                dup_o[:, rows] = dot_nt(low_f[...], gh[rows, :]).astype(BF16)
                ddown_o[rows, :] = dot_nt(act[rows, :], cot_f[...]).astype(BF16)
                return 0
            lax.fori_loop(0, ff // tile, up, 0)

    whole = lambda shape: pl.BlockSpec(shape, lambda i: (0,) * len(shape))
    return pl.pallas_call(
        kernel, grid=(steps,),
        in_specs=[pl.BlockSpec((feat, chunk), lambda i: (0, i)), pl.BlockSpec((chunk, feat), lambda i: (i, 0)),
                  whole(small.shape), whole(w_up.shape), whole(w_down.shape)],
        out_specs=[pl.BlockSpec((chunk, feat), lambda i: (i, 0)), pl.BlockSpec((feat, chunk), lambda i: (0, i)), whole((2, feat, 128)),
                   whole((feat, ff)), whole((ff, feat))],
        out_shape=[jax.ShapeDtypeStruct((n, feat), F32), jax.ShapeDtypeStruct((feat, n), F32), jax.ShapeDtypeStruct((2, feat, 128), F32),
                   jax.ShapeDtypeStruct((feat, ff), BF16), jax.ShapeDtypeStruct((ff, feat), BF16)],
        scratch_shapes=[pltpu.VMEM((ff, feat), BF16), pltpu.VMEM((feat, ff), BF16), pltpu.VMEM((ff, n), BF16), pltpu.VMEM((ff, n), BF16),
                        pltpu.VMEM((feat, n), BF16), pltpu.VMEM((feat, n), BF16)],
        compiler_params=pltpu.CompilerParams(vmem_limit_bytes=VMEM_LIMIT), name="feed_forward",
    )(middle, cotangent, small, w_up, w_down)


def attention_backward(tokens, waves, small, w_qkv, w_out, start, grad_middle, project, powers, inverses, mixed):
    seqs, _, length = tokens.shape
    feat, n = start.shape
    head = feat // HEADS
    scale = 1.0 / math.sqrt(head)

    def kernel(tok_ref, waves_ref, small_ref, qkv_ref, out_ref, start_ref, grad_ref, project_ref, powers_ref, inv_ref, mixed_ref,
               din_o, dqkv_o, dout_o, dtime_o, ln_o, dchar_o, ga_f, mix_f, low_f, gp_f, gs_f):
        i = pl.program_id(0)

        @pl.when(i == 0)
        def _():
            ln_o[...] = jnp.zeros_like(ln_o)
            dchar_o[...] = jnp.zeros_like(dchar_o)
            gs_f[...] = jnp.zeros_like(gs_f)

        cols = pl.ds(pl.multiple_of(i * length, length), length)
        grad_low = grad_ref[...].astype(BF16)
        ga_f[:, cols] = grad_low
        mix_f[:, cols] = mixed_ref[...]
        grad_mixed = dot(out_ref[...], grad_low).astype(BF16).astype(F32)
        for h in range(HEADS):
            rows = pl.ds(h * head, head)
            krows, vrows = pl.ds(feat + h * head, head), pl.ds(2 * feat + h * head, head)
            scaled = grad_mixed[h * head:(h + 1) * head] * inv_ref[0, h:h + 1, :]
            lean = jnp.sum(scaled * mixed_ref[rows, :].astype(F32), axis=0, keepdims=True)
            scaled = scaled.astype(BF16)
            low_powers = powers_ref[0, h]
            grad_probs = dot(project_ref[vrows, :].T, scaled)
            grad_scores = (low_powers.astype(F32) * (grad_probs - lean)).astype(BF16)
            gp_f[vrows, cols] = dot_nt(scaled, low_powers).astype(BF16)
            gp_f[rows, cols] = (dot(project_ref[krows, :], grad_scores) * scale).astype(BF16)
            gp_f[krows, cols] = (dot_nt(project_ref[rows, :], grad_scores) * scale).astype(BF16)
        normed, inverse = norm_rows(start_ref[...])
        gain = param(small_ref[...], 27)
        low_f[:, cols] = (normed * gain + param(small_ref[...], 28)).astype(BF16)
        grad_normed = dot(qkv_ref[...], gp_f[:, cols])
        din = grad_ref[...] + norm_rows_back(grad_normed, gain, normed, inverse)
        din_o[...] = din.T
        ln_o[0] += fold(grad_normed * normed)
        ln_o[1] += fold(grad_normed)
        lane = lax.broadcasted_iota(jnp.int32, gs_f.shape, 1)
        gs_f[...] += jnp.where(lane == i, jnp.sum(din, axis=1, keepdims=True), 0.0)
        one_hot = (lax.broadcasted_iota(jnp.int32, (128, length), 0) == tok_ref[0]).astype(BF16)
        high = din.astype(BF16)
        rest = (din - high.astype(F32)).astype(BF16)
        dchar_o[...] += dot_nt(high, one_hot) + dot_nt(rest, one_hot)

        @pl.when(i == seqs - 1)
        def _():
            dtime_o[...] = dot_nt(waves_ref[...], gs_f[...].astype(BF16)).astype(BF16)
            dout_o[...] = dot_nt(mix_f[...], ga_f[...]).astype(BF16)

            def one(j, _):
                rows = pl.ds(pl.multiple_of(j * 256, 256), 256)
                dqkv_o[:, rows] = dot_nt(low_f[...], gp_f[rows, :]).astype(BF16)
                return 0
            lax.fori_loop(0, 3 * feat // 256, one, 0)

    whole = lambda shape: pl.BlockSpec(shape, lambda i: (0,) * len(shape))
    block = lambda rows: pl.BlockSpec((rows, length), lambda i: (0, i))
    return pl.pallas_call(
        kernel, grid=(seqs,),
        in_specs=[pl.BlockSpec((1, 1, length), lambda i: (i, 0, 0)), whole(waves.shape), whole(small.shape), whole(w_qkv.shape), whole(w_out.shape),
                  block(feat), block(feat), block(3 * feat), pl.BlockSpec((1, HEADS, length, length), lambda i: (i, 0, 0, 0)),
                  pl.BlockSpec((1, HEADS, length), lambda i: (i, 0, 0)), block(feat)],
        out_specs=[pl.BlockSpec((length, feat), lambda i: (i, 0)), whole((feat, 3 * feat)), whole((feat, feat)), whole((feat, feat)),
                   whole((2, feat, 128)), whole((feat, 128))],
        out_shape=[jax.ShapeDtypeStruct((n, feat), F32), jax.ShapeDtypeStruct((feat, 3 * feat), BF16), jax.ShapeDtypeStruct((feat, feat), BF16),
                   jax.ShapeDtypeStruct((feat, feat), BF16), jax.ShapeDtypeStruct((2, feat, 128), F32), jax.ShapeDtypeStruct((feat, 128), F32)],
        scratch_shapes=[pltpu.VMEM((feat, n), BF16), pltpu.VMEM((feat, n), BF16), pltpu.VMEM((feat, n), BF16), pltpu.VMEM((3 * feat, n), BF16),
                        pltpu.VMEM((feat, 128), F32)],
        compiler_params=pltpu.CompilerParams(vmem_limit_bytes=VMEM_LIMIT), name="attention_backward",
    )(tokens, waves, small, w_qkv, w_out, start, grad_middle, project, powers, inverses, mixed)


def sinusoid(steps, features):
    half = features // 2
    frequency = jnp.exp(-math.log(10000.0) * jnp.arange(half, dtype=F32) / half)
    angles = frequency[:, None] * steps.astype(F32)[None, :]
    waves = jnp.concatenate([jnp.sin(angles), jnp.cos(angles)], axis=0).astype(BF16)
    return jnp.pad(waves, ((0, 0), (0, 128 - steps.shape[0])))


def pack_small(char_table, g1, b1, g2, b2):
    cols = jnp.concatenate([char_table.T, g1[:, None], b1[:, None], g2[:, None], b2[:, None]], axis=1)
    return jnp.pad(cols, ((0, 0), (0, 128 - cols.shape[1])))


def layer(tokens, timesteps, cotangent, small, time_w, w_qkv, w_out, w_up, w_down):
    seqs = timesteps.shape[0]
    tok = tokens.reshape(seqs, 1, tokens.shape[0] // seqs)
    waves = sinusoid(timesteps, time_w.shape[0])
    start, middle, project, powers, inv, mixed = attention_forward(tok, waves, small, time_w, w_qkv, w_out)
    result, grad_mid, ln2, dup, ddown = feed_forward(middle, cotangent, small, w_up, w_down)
    din, dqkv, dout, dtime, ln1, dchar = attention_backward(tok, waves, small, w_qkv, w_out, start, grad_mid, project, powers, inv, mixed)
    lns = jnp.sum(jnp.concatenate([ln1, ln2]), axis=-1)
    dsmall = jnp.concatenate([dchar[:, :27], lns.T, dchar[:, 31:]], axis=1)
    return result, din, dsmall, dtime, dqkv, dout, dup, ddown

AXES = ("gx", "gy")


def gather_all(mesh_shape, packed):
    count = mesh_shape[0] * mesh_shape[1]
    if mesh_shape[1] == 4 and mesh_shape[0] % 2 == 0 and all(p.shape[0] % 16 == 0 for p in packed):
        got = gather(mesh_shape[0] // 2, packed)
    else:
        got = [lax.all_gather(p, AXES, axis=0) for p in packed]
    return [g.reshape(count * p.shape[0], p.shape[1]) for g, p in zip(got, packed)]


def scatter_all(mesh_shape, parts):
    count = mesh_shape[0] * mesh_shape[1]
    rows = [p.shape[0] // count for p in parts]
    if mesh_shape[1] == 4 and mesh_shape[0] % 2 == 0 and all(r % 16 == 0 for r in rows):
        nz = mesh_shape[0] // 2
        return scatter(nz, [p.reshape(nz, 2, 2, 2, r, p.shape[1]) for p, r in zip(parts, rows)])
    return [lax.psum_scatter(p.astype(F32), AXES, scatter_dimension=0, tiled=True) for p in parts]


def make_body(mesh_shape):
    def body(tokens, timesteps, cotangent, char_table, time_weight, ln1_gain, ln1_bias, w_qkv, w_attn_out, ln2_gain, ln2_bias, w_up, w_down):
        feat = w_up.shape[0] * mesh_shape[0] * mesh_shape[1]
        ff = w_up.shape[1]
        chars = char_table.shape[0]
        small = pack_small(char_table, ln1_gain, ln1_bias, ln2_gain, ln2_bias)
        first, second, down = gather_all(mesh_shape, [
            jnp.concatenate([small, time_weight, w_qkv], axis=1), jnp.concatenate([w_attn_out, w_up], axis=1), w_down])
        result, din, dsmall, dtime, dqkv, dout, dup, ddown = layer(
            tokens, timesteps, cotangent, first[:, :128], first[:, 128:128 + feat], first[:, 128 + feat:], second[:, :feat], second[:, feat:], down)
        dup, ddown, rest = scatter_all(mesh_shape, [
            dup, ddown, jnp.concatenate([dsmall.astype(BF16), dtime, dqkv, dout], axis=1)])
        ln = rest[:, chars:chars + 4].T
        return (result, din, rest[:, :chars].T, rest[:, 128:128 + feat], ln[0], ln[1], rest[:, 128 + feat:128 + 4 * feat], rest[:, 128 + 4 * feat:],
                ln[2], ln[3], dup, ddown)
    return body


def solution(mesh):
    every = P(AXES)
    rows, cols = P(AXES, None), P(None, AXES)
    return jax.shard_map(
        make_body((mesh.shape["gx"], mesh.shape["gy"])),
        mesh=mesh,
        in_specs=(every, every, rows, cols, rows, every, every, rows, rows, every, every, rows, rows),
        out_specs=(rows, rows, cols, rows, every, every, rows, rows, every, every, rows, rows),
        check_vma=False,
    )
```

```python
import types
import math

import jax
import jax.numpy as jnp
from jax import lax
from jax.experimental import pallas as pl
from jax.experimental.pallas import tpu as pltpu
from jax.sharding import PartitionSpec as P

F32, BF16 = jnp.float32, jnp.bfloat16

MESH = pl.DeviceIdType.MESH


def place():
    gx, gy = lax.axis_index("gx"), lax.axis_index("gy")
    return gx // 2, gx % 2, gy // 2, gy % 2


def device(z, x, y, c):
    return (z * 2 + x, y * 2 + c)


def greet(nz):
    z, x, y, c = place()
    barrier = pltpu.get_barrier_semaphore()
    for where in [(z, x, y, 1 - c), (z, 1 - x, y, c), (z, x, 1 - y, c)] + [((z + d) % nz, x, y, c) for d in range(1, nz)]:
        pl.semaphore_signal(barrier, inc=1, device_id=device(*where), device_id_type=MESH)


def greeted(nz):
    pl.semaphore_wait(pltpu.get_barrier_semaphore(), 3 + nz - 1)


def send(src, dst, sems, slot, where):
    return pltpu.make_async_remote_copy(
        src_ref=src, dst_ref=dst, send_sem=sems.at[0, slot], recv_sem=sems.at[1, slot],
        device_id=device(*where), device_id_type=MESH)


def middle_of(width):
    return width // 256 * 128


class Gather:
    NAMES = ("x", "y", "xd", "yd", "c0", "c1", "c2", "c3", "c4")

    @staticmethod
    def scratch(nz):
        return pltpu.SemaphoreType.DMA((2, nz - 1 + 9))

    def __init__(self, nz, shard, out, sems):
        self.nz, self.shard, self.out, self.sems = nz, shard, out, sems

    def along(self, d, comes=False):
        z, x, y, c = place()
        come = (z + self.nz - d) % self.nz
        return send(self.shard, self.out.at[come if comes else z, x, y, c], self.sems, d - 1, ((z + d) % self.nz, x, y, c))

    def copy(self, name, comes=False):
        z, x, y, c = place()
        width = self.out.shape[-1]
        lo, hi = pl.ds(0, middle_of(width)), pl.ds(middle_of(width), width - middle_of(width))
        to, a, b, k, cut, slot = {
            "x": ("x", x, y, c, None, 0), "y": ("y", x, y, c, None, 1),
            "xd": ("x", x, 1 - y, c, lo, 2), "yd": ("y", 1 - x, y, c, hi, 3),
            "c0": ("c", x, y, c, None, 4), "c1": ("c", 1 - x, y, c, None, 5), "c2": ("c", x, 1 - y, c, None, 6),
            "c3": ("c", 1 - x, 1 - y, c, lo, 7), "c4": ("c", 1 - x, 1 - y, c, hi, 8)}[name]
        if comes:
            a, b, k = (1 - a, b, k) if to == "x" else (a, 1 - b, k) if to == "y" else (a, b, 1 - k)
        where = {"x": (z, 1 - x, y, c), "y": (z, x, 1 - y, c), "c": (z, x, y, 1 - c)}[to]
        ref = self.out.at[pl.ds(0, self.nz), a, b, k]
        if cut is not None:
            ref = ref.at[:, :, cut]
        return send(ref, ref, self.sems, self.nz - 1 + slot, where)

    def start(self, *names):
        for name in names:
            self.copy(name).start()

    def arrive(self, *names):
        for name in names:
            self.copy(name, comes=True).wait_recv()

    def lines(self):
        for d in range(1, self.nz):
            self.along(d).start()

    def sides(self):
        for d in range(1, self.nz):
            self.along(d, comes=True).wait_recv()
        self.start("x", "y", "c0")

    def corners(self):
        self.arrive("x", "y")
        self.start("xd", "yd", "c1", "c2")

    def cores(self):
        self.arrive("xd", "yd")
        self.start("c3", "c4")

    def whole(self):
        self.arrive("c0", "c1", "c2", "c3", "c4")

    def finish(self):
        for d in range(1, self.nz):
            self.along(d).wait_send()
        for name in self.NAMES:
            self.copy(name).wait_send()


class Scatter:
    @staticmethod
    def scratch(nz, tail, dtype):
        return [pltpu.VMEM((nz, 2, 2) + tail, dtype), pltpu.VMEM((nz,) + tail, dtype), pltpu.VMEM((2, nz) + tail, dtype),
                pltpu.VMEM((nz - 1,) + tail, dtype), pltpu.SemaphoreType.DMA((2, nz - 1 + 5))]

    def __init__(self, nz, mine, kept, own, far, near, line, sems):
        self.nz, self.mine, self.kept, self.own, self.far, self.near, self.line, self.sems = nz, mine, kept, own, far, near, line, sems
        self.width = own.shape[-1]

    def copy(self, name):
        z, x, y, c = place()
        nz, own, sems, base = self.nz, self.own, self.sems, self.nz - 1
        half = middle_of(self.width)
        lo, hi = pl.ds(0, half), pl.ds(half, self.width - half)
        all_z = pl.ds(0, nz)
        xp, yp, cp = (z, 1 - x, y, c), (z, x, 1 - y, c), (z, x, y, 1 - c)
        if name == "c":
            return send(self.mine.at[all_z, :, :, 1 - c], own, sems, base, cp)
        if name == "xd":
            return send(own.at[all_z, 1 - x, 1 - y, :, lo], self.far.at[:, :, lo], sems, base + 1, xp)
        if name == "yd":
            return send(own.at[all_z, 1 - x, 1 - y, :, hi], self.far.at[:, :, hi], sems, base + 2, yp)
        if name == "x":
            return send(own.at[all_z, 1 - x, y], self.near.at[0], sems, base + 3, xp)
        return send(own.at[all_z, x, 1 - y], self.near.at[1], sems, base + 4, yp)

    def along(self, d):
        z, x, y, c = place()
        to = (z + d) % self.nz
        return send(self.own.at[to, x, y], self.line.at[d - 1], self.sems, d - 1, (to, x, y, c))

    def add(self, a, b, *values, cut=None):
        cols = cut if cut is not None else pl.ds(0, self.width)

        def one(k, _):
            spot = (k, a, b, slice(None), cols)
            total = self.own[spot]
            for value in values:
                total = total + value(k, cols)
            self.own[spot] = total
            return 0
        lax.fori_loop(0, self.nz, one, 0)

    def cores(self):
        self.copy("c").start()

    def corners(self):
        z, x, y, c = place()
        self.copy("c").wait()
        for a, b in ((1 - x, 1 - y), (1 - x, y), (x, 1 - y), (x, y)):
            self.add(a, b, lambda k, cols, a=a, b=b: self.kept(k, a, b, cols))
            if a is not x and b is not y:
                self.copy("xd").start()
                self.copy("yd").start()

    def sides(self):
        z, x, y, c = place()
        half = middle_of(self.width)
        self.copy("xd").wait()
        self.add(x, 1 - y, lambda k, cols: self.far[k, :, cols], cut=pl.ds(0, half))
        self.copy("y").start()
        self.copy("yd").wait()
        self.add(1 - x, y, lambda k, cols: self.far[k, :, cols], cut=pl.ds(half, self.width - half))
        self.copy("x").start()

    def lines(self):
        z, x, y, c = place()
        self.copy("x").wait()
        self.copy("y").wait()
        self.add(x, y, lambda k, cols: self.near[0, k, :, cols], lambda k, cols: self.near[1, k, :, cols])
        for d in range(1, self.nz):
            self.along(d).start()

    def total(self):
        z, x, y, c = place()
        for d in range(1, self.nz):
            self.along(d).wait()
        total = self.own[z, x, y].astype(F32)
        for d in range(1, self.nz):
            total = total + self.line[d - 1].astype(F32)
        return total

HEADS = 8
EPSILON = 1e-05
VMEM_LIMIT = 62 * 2**20
BLOCKS = (2, 2, 2)


def dot(left, right):
    return jnp.dot(left, right, preferred_element_type=F32)


def dot_nt(left, right):
    return lax.dot_general(left, right, (((1,), (1,)), ((), ())), preferred_element_type=F32)


def norm_rows(values):
    count = values.shape[0]
    shifted = values - jnp.sum(values, axis=0, keepdims=True) * (1.0 / count)
    inverse = lax.rsqrt(jnp.sum(shifted * shifted, axis=0, keepdims=True) * (1.0 / count) + EPSILON)
    return shifted * inverse, inverse


def norm_rows_back(grad, gain, normed, inverse):
    count = grad.shape[0]
    scaled = grad * gain
    lean = jnp.sum(scaled, axis=0, keepdims=True) * (1.0 / count)
    turn = jnp.sum(scaled * normed, axis=0, keepdims=True) * (1.0 / count)
    return inverse * (scaled - lean - normed * turn)


def fold(values):
    total = values[:, :128]
    for k in range(1, values.shape[1] // 128):
        total = total + values[:, 128 * k:128 * (k + 1)]
    return total


def flat(ref, cols=slice(None)):
    value = ref[(slice(None),) * (len(ref.shape) - 1) + (cols,)]
    return value.reshape(-1, value.shape[-1])


class Call:
    def __init__(self):
        self.ins, self.outs, self.scratch = [], [], []

    def arg(self, name, array, spec):
        self.ins.append((name, array, spec))

    def out(self, name, shape, dtype, spec):
        self.outs.append((name, jax.ShapeDtypeStruct(shape, dtype), spec))

    def temp(self, name, kind):
        self.scratch.append((name, kind))

    def run(self, kernel, name, grid, collective=None):
        names = [n for n, *_ in self.ins + self.outs + self.scratch]

        def body(*refs):
            kernel(types.SimpleNamespace(**dict(zip(names, refs))))
        extra = {} if collective is None else dict(collective_id=collective, has_side_effects=True)
        got = pl.pallas_call(
            body, grid=grid, in_specs=[s for *_, s in self.ins], out_specs=[s for *_, s in self.outs],
            out_shape=[s for _, s, _ in self.outs], scratch_shapes=[k for _, k in self.scratch],
            compiler_params=pltpu.CompilerParams(vmem_limit_bytes=VMEM_LIMIT, **extra), name=name,
        )(*[a for _, a, _ in self.ins])
        return dict(zip([n for n, *_ in self.outs], got))


def whole(shape):
    return pl.BlockSpec(tuple(shape), lambda i: (0,) * len(shape))


def lanes(rows, width, first=0):
    return pl.BlockSpec((rows, width), lambda i: (0, jnp.maximum(i - first, 0)))


ANYWHERE = pl.BlockSpec(memory_space=pl.ANY)


def fill_waves(r, feat):
    half = feat // 2
    r.steps_row[...] = jnp.zeros_like(r.steps_row)
    r.steps_row[:, :r.steps.shape[1]] = r.steps[...].astype(F32)
    rate = jnp.exp(lax.broadcasted_iota(jnp.int32, (half, 128), 0).astype(F32) * (-math.log(10000.0) / half))
    angles = rate * r.steps_row[...]
    r.waves[:half, :] = jnp.sin(angles).astype(BF16)
    r.waves[half:, :] = jnp.cos(angles).astype(BF16)


def fill_small(r, chars):
    r.square[...] = jnp.zeros_like(r.square)
    count = r.char.shape[1]
    r.square[:chars, :count] = r.char[...].astype(F32)
    for k, ref in enumerate((r.g1, r.b1, r.g2, r.b2)):
        r.square[chars + k:chars + k + 1, :count] = ref[...].astype(F32)
    r.small_shard[...] = r.square[...].T[:count].astype(BF16)


def param(r, column):
    return r[:, column:column + 1].astype(F32)


def embed(r, i, tok, small):
    one_hot = (lax.broadcasted_iota(jnp.int32, (128, tok.shape[1]), 0) == tok).astype(BF16)
    lane = lax.broadcasted_iota(jnp.int32, r.stamps.shape, 1)
    stamp = jnp.sum(jnp.where(lane == i, r.stamps[...], 0.0), axis=1, keepdims=True)
    return dot(small, one_hot) + stamp


def heads_forward(r, feat):
    head = feat // HEADS
    turn = math.log2(math.e) / math.sqrt(head)
    rows = [pl.ds(h * head, head) for h in range(HEADS)]
    for h in range(HEADS):
        r.scores[h] = dot(r.project[pl.ds(feat + h * head, head), :].T, r.project[rows[h], :])
    for h in range(HEADS):
        scores = r.scores[h]
        powers = jnp.exp2((scores - jnp.max(scores, axis=0, keepdims=True)) * turn)
        r.inv[0, h:h + 1, :] = 1.0 / jnp.sum(powers, axis=0, keepdims=True)
        r.powers[0, h] = powers.astype(BF16)
    for h in range(HEADS):
        mixed = dot(r.project[pl.ds(2 * feat + h * head, head), :], r.powers[0, h])
        r.mixed[rows[h], :] = (mixed * r.inv[0, h:h + 1, :]).astype(BF16)


def attention_forward(nz, tokens, timesteps, shards):
    char, g1, b1, g2, b2, time_w, w_qkv, w_out, w_up, w_down = shards
    seqs = timesteps.shape[0]
    n = tokens.shape[0]
    length = n // seqs
    feat = time_w.shape[1]
    ff = w_up.shape[1]
    chars = char.shape[0]
    count = char.shape[1]
    call = Call()
    call.arg("tok", tokens.reshape(seqs, 1, length), whole((seqs, 1, length)))
    call.arg("steps", timesteps.reshape(1, seqs), whole((1, seqs)))
    call.arg("char", char, whole(char.shape))
    for name, value in (("g1", g1), ("b1", b1), ("g2", g2), ("b2", b2)):
        call.arg(name, value.reshape(1, count), whole((1, count)))
    call.arg("time_w", time_w, whole(time_w.shape))
    call.arg("w_qkv", w_qkv, whole(w_qkv.shape))
    call.arg("w_out", w_out, whole(w_out.shape))
    if nz:
        call.arg("w_up", w_up, ANYWHERE)
        call.arg("w_down", w_down, ANYWHERE)
    for name, rows, kind in (("start", feat, F32), ("middle", feat, F32), ("project", 3 * feat, BF16), ("mixed", feat, BF16)):
        call.out(name, (rows, n), kind, lanes(rows, length))
    call.out("powers", (seqs, HEADS, length, length), BF16, pl.BlockSpec((1, HEADS, length, length), lambda i: (i, 0, 0, 0)))
    call.out("inv", (seqs, HEADS, length), F32, pl.BlockSpec((1, HEADS, length), lambda i: (i, 0, 0)))
    call.out("waves", (feat, 128), BF16, whole((feat, 128)))
    parts = 3
    if nz:
        blocks = lambda a: (nz,) + BLOCKS + a
        kept = {"first": (count, 128 + feat), "out": w_out.shape}
        kept.update({f"qkv{p}": (count, feat) for p in range(parts)})
        for name, tail in kept.items():
            call.temp(name, pltpu.VMEM(blocks(tail), BF16))
            call.temp(name + "_sems", Gather.scratch(nz))
        for name, tail in (("up", w_up.shape), ("down", w_down.shape)):
            call.out(name, blocks(tail), BF16, ANYWHERE)
            call.temp(name + "_sems", Gather.scratch(nz))
        for name, tail in (("first_o", kept["first"]), ("out_o", kept["out"]), ("qkv_o", w_qkv.shape)):
            call.out(name, blocks(tail), BF16, ANYWHERE)
        call.temp("first_shard", pltpu.VMEM((count, 128 + feat), BF16))
        call.temp("place_sems", pltpu.SemaphoreType.DMA((2,)))
        call.temp("save_sems", pltpu.SemaphoreType.DMA((2 + parts,)))
    else:
        call.out("small", (count, 128), BF16, whole((count, 128)))
    call.temp("small_shard", pltpu.VMEM((count, 128), BF16))
    call.temp("square", pltpu.VMEM((128, max(count, 128)), F32))
    call.temp("steps_row", pltpu.VMEM((1, 128), F32))
    call.temp("stamps", pltpu.VMEM((feat, 128), F32))
    call.temp("qkv_t", pltpu.VMEM((3 * feat, feat), BF16))
    call.temp("out_t", pltpu.VMEM((feat, feat), BF16))
    call.temp("starts", pltpu.VMEM((seqs, feat, length), F32))
    call.temp("low", pltpu.VMEM((seqs, feat, length), BF16))
    call.temp("scores", pltpu.VMEM((HEADS, length, length), F32))

    def kernel(r):
        i = pl.program_id(0)
        if nz:
            z, x, y, c = place()
            first = Gather(nz, r.first_shard, r.first, r.first_sems)
            qkv = [Gather(nz, r.w_qkv.at[:, pl.ds(p * feat, feat)], getattr(r, f"qkv{p}"), getattr(r, f"qkv{p}_sems")) for p in range(parts)]
            out = Gather(nz, r.w_out, r.out, r.out_sems)
            up = Gather(nz, r.w_up, r.up, r.up_sems)
            down = Gather(nz, r.w_down, r.down, r.down_sems)
            put = [pltpu.make_async_copy(g.shard, g.out.at[z, x, y, c], r.place_sems.at[k]) for k, g in enumerate((up, down))]
            every = (pl.ds(0, nz), slice(None), slice(None), slice(None), slice(None))
            save = [pltpu.make_async_copy(r.first, r.first_o, r.save_sems.at[0]), pltpu.make_async_copy(r.out, r.out_o, r.save_sems.at[1])]
            save += [pltpu.make_async_copy(g.out, r.qkv_o.at[every + (pl.ds(p * feat, feat),)], r.save_sems.at[2 + p]) for p, g in enumerate(qkv)]

        def small():
            return flat(r.first, slice(0, 128)) if nz else r.small[...]

        def begin(some):
            table = small()
            for k in some:
                start = embed(r, k, r.tok[k], table)
                r.starts[k] = start
                normed, _ = norm_rows(start)
                r.low[k] = (normed * param(table, chars) + param(table, chars + 1)).astype(BF16)

        @pl.when(i == 0)
        def _():
            if nz:
                greet(nz)
                for copy in put:
                    copy.start()
            fill_small(r, chars)
            if nz:
                q, k, v = qkv
                r.first_shard[:, :128] = r.small_shard[...]
                r.first_shard[:, 128:] = r.time_w[...]
                for g in (first, out, q, k, v):
                    g.out[z, x, y, c] = g.shard[...]
                greeted(nz)
                first.lines()
                q.lines()
                fill_waves(r, feat)
                first.sides()
                k.lines()
                q.sides()
                v.lines()
                first.corners()
                k.sides()
                out.lines()
                q.corners()
                first.cores()
                v.sides()
                k.corners()
                q.cores()
                first.whole()
                r.stamps[...] = dot(flat(r.first, slice(128, 128 + feat)).T, r.waves[...])
                out.sides()
                v.corners()
                k.cores()
                begin(range(0, seqs // 2))
                out.corners()
                v.cores()
                q.whole()
                r.qkv_t[:feat] = flat(r.qkv0).T
                up.lines()
                begin(range(seqs // 2, seqs))
                out.cores()
                k.whole()
                r.qkv_t[feat:2 * feat] = flat(r.qkv1).T
                v.whole()
                r.qkv_t[2 * feat:] = flat(r.qkv2).T
            else:
                r.small[...] = r.small_shard[...]
                fill_waves(r, feat)
                r.stamps[...] = dot(r.time_w[...].T, r.waves[...])
                r.qkv_t[...] = r.w_qkv[...].T
                r.out_t[...] = r.w_out[...].T
                begin(range(seqs))

        r.project[...] = dot(r.qkv_t[...], r.low[i]).astype(BF16)
        heads_forward(r, feat)
        if nz:
            @pl.when(i == 0)
            def _():
                out.whole()
                r.out_t[...] = flat(r.out).T
                for copy in put:
                    copy.wait()
                up.sides()
                down.lines()
                for copy in save:
                    copy.start()

            @pl.when(i == 2)
            def _():
                down.sides()

            @pl.when(i == 3)
            def _():
                up.corners()

            @pl.when(i == 5)
            def _():
                up.cores()
                down.corners()

            @pl.when(i == seqs - 1)
            def _():
                down.cores()
                for copy in save:
                    copy.wait()
                for g in (up, down):
                    g.whole()
                for g in (first, *qkv, out, up, down):
                    g.finish()
        start = r.starts[i]
        r.start[...] = start
        r.middle[...] = start + dot(r.out_t[...], r.mixed[...])

    return call.run(kernel, "attention_forward", (seqs,), 0 if nz else None)


def feed_forward(chars, middle, cotangent, mixed, small, w_up, w_down, chunk=512):
    feat, n = middle.shape
    ff = w_up.shape[1]
    steps = n // chunk
    tile = 256
    call = Call()
    call.arg("middle", middle, lanes(feat, chunk))
    call.arg("cot", cotangent, pl.BlockSpec((chunk, feat), lambda i: (i, 0)))
    call.arg("mixed", mixed, whole(mixed.shape))
    call.arg("small", small, whole((feat, 128)))
    call.arg("w_up", w_up, whole(w_up.shape))
    call.arg("w_down", w_down, whole(w_down.shape))
    call.out("result", (n, feat), F32, pl.BlockSpec((chunk, feat), lambda i: (i, 0)))
    call.out("grad", (feat, n), F32, lanes(feat, chunk))
    call.out("ln", (2, feat, 128), F32, whole((2, feat, 128)))
    call.out("d_up", (feat, ff + feat), BF16, whole((feat, ff + feat)))
    call.out("d_down", (ff, feat), BF16, whole((ff, feat)))
    call.temp("up_t", pltpu.VMEM((ff, feat), BF16))
    call.temp("down_t", pltpu.VMEM((feat, ff), BF16))
    call.temp("act", pltpu.VMEM((ff, n), BF16))
    call.temp("gh", pltpu.VMEM((ff, n), BF16))
    call.temp("cot_f", pltpu.VMEM((feat, n), BF16))
    call.temp("low_f", pltpu.VMEM((feat, n), BF16))
    call.temp("ga_f", pltpu.VMEM((feat, n), BF16))

    def kernel(r):
        i = pl.program_id(0)

        @pl.when(i == 0)
        def _():
            r.up_t[...] = r.w_up[...].T
            r.down_t[...] = r.w_down[...].T
            r.ln[...] = jnp.zeros_like(r.ln)

        cols = pl.ds(pl.multiple_of(i * chunk, chunk), chunk)
        middle = r.middle[...]
        normed, inverse = norm_rows(middle)
        gain = param(r.small, chars + 2)
        low = (normed * gain + param(r.small, chars + 3)).astype(BF16)
        r.low_f[:, cols] = low
        cot = r.cot[...].T
        r.cot_f[:, cols] = cot
        for j in range(ff // tile):
            rows = pl.ds(j * tile, tile)
            hidden = dot(r.up_t[rows, :], low)
            grad_active = dot(r.w_down[rows, :], cot).astype(BF16).astype(F32)
            cdf = 0.5 + 0.5 * lax.erf(hidden * math.sqrt(0.5))
            bell = jnp.exp2(hidden * hidden * (-0.5 * math.log2(math.e))) * (1.0 / math.sqrt(2.0 * math.pi))
            r.act[rows, cols] = (hidden * cdf).astype(BF16)
            r.gh[rows, cols] = (grad_active * (cdf + hidden * bell)).astype(BF16)
        r.result[...] = (middle + dot(r.down_t[...], r.act[:, cols])).T
        grad_normed = dot(r.w_up[...], r.gh[:, cols])
        grad = cot.astype(F32) + norm_rows_back(grad_normed, gain, normed, inverse)
        r.grad[...] = grad
        r.ga_f[:, cols] = grad.astype(BF16)
        r.ln[0] += fold(grad_normed * normed)
        r.ln[1] += fold(grad_normed)

        @pl.when(i == steps - 1)
        def _():
            big = 512

            def one(j, _):
                rows = pl.ds(pl.multiple_of(j * big, big), big)
                r.d_up[:, rows] = dot_nt(r.low_f[...], r.gh[rows, :]).astype(BF16)
                r.d_down[rows, :] = dot_nt(r.act[rows, :], r.cot_f[...]).astype(BF16)
                return 0
            lax.fori_loop(0, ff // big, one, 0)
            r.d_up[:, ff:] = dot_nt(r.mixed[...], r.ga_f[...]).astype(BF16)

    return call.run(kernel, "feed_forward", (steps,))


def heads_backward(r, feat, cols):
    head = feat // HEADS
    scale = 1.0 / math.sqrt(head)
    rows = [pl.ds(h * head, head) for h in range(HEADS)]
    krows = [pl.ds(feat + h * head, head) for h in range(HEADS)]
    vrows = [pl.ds(2 * feat + h * head, head) for h in range(HEADS)]
    for h in range(HEADS):
        scaled = r.grad_mixed[rows[h], :] * r.inv[0, h:h + 1, :]
        r.lean[h:h + 1, :] = jnp.sum(scaled * r.mixed[rows[h], :].astype(F32), axis=0, keepdims=True)
        r.scaled[rows[h], :] = scaled.astype(BF16)
    for h in range(HEADS):
        r.scores[h] = dot(r.project[vrows[h], :].T, r.scaled[rows[h], :])
    for h in range(HEADS):
        r.grad_scores[h] = (r.powers[0, h].astype(F32) * (r.scores[h] - r.lean[h:h + 1, :])).astype(BF16)
    for h in range(HEADS):
        r.gp_f[vrows[h], cols] = dot_nt(r.scaled[rows[h], :], r.powers[0, h]).astype(BF16)
        r.gp_f[rows[h], cols] = (dot(r.project[krows[h], :], r.grad_scores[h]) * scale).astype(BF16)
        r.gp_f[krows[h], cols] = (dot_nt(r.project[rows[h], :], r.grad_scores[h]) * scale).astype(BF16)


def attention_backward(nz, chars, tokens, waves, small, w_qkv, w_out, saved, ff):
    feat, n = saved["start"].shape
    seqs = saved["powers"].shape[0]
    length = n // seqs
    call = Call()
    late = lambda i: jnp.maximum(i - seqs, 0)
    soon = lambda i: jnp.minimum(i, seqs - 1)
    call.arg("tok", tokens.reshape(seqs, 1, length), pl.BlockSpec((1, 1, length), lambda i: (late(i), 0, 0)))
    call.arg("waves", waves, whole(waves.shape))
    call.arg("small", small, whole((feat, 128)))
    call.arg("w_qkv", w_qkv, whole(w_qkv.shape))
    call.arg("w_out", w_out, whole(w_out.shape))
    call.arg("start", saved["start"], pl.BlockSpec((feat, length), lambda i: (0, i % seqs)))
    call.arg("grad", saved["grad"], pl.BlockSpec((feat, length), lambda i: (0, i % seqs)))
    for name, rows in (("project", 3 * feat), ("mixed", feat)):
        call.arg(name, saved[name], pl.BlockSpec((rows, length), lambda i: (0, soon(i))))
    call.arg("powers", saved["powers"], pl.BlockSpec((1, HEADS, length, length), lambda i: (soon(i), 0, 0, 0)))
    call.arg("inv", saved["inv"], pl.BlockSpec((1, HEADS, length), lambda i: (soon(i), 0, 0)))
    call.arg("ln2", saved["ln"], whole((2, feat, 128)))
    call.out("d_in", (feat, n), F32, pl.BlockSpec((feat, length), lambda i: (0, late(i))))
    call.temp("ln1", pltpu.VMEM((2, feat, 128), F32))
    call.temp("d_char", pltpu.VMEM((feat, 128), F32))
    call.temp("low_f", pltpu.VMEM((feat, n), BF16))
    call.temp("gp_f", pltpu.VMEM((3 * feat, n), BF16))
    call.temp("scores", pltpu.VMEM((HEADS, length, length), F32))
    call.temp("grad_scores", pltpu.VMEM((HEADS, length, length), BF16))
    call.temp("grad_mixed", pltpu.VMEM((feat, length), F32))
    call.temp("scaled", pltpu.VMEM((feat, length), BF16))
    call.temp("lean", pltpu.VMEM((HEADS, length), F32))
    call.temp("gs_f", pltpu.VMEM((feat, 128), F32))
    if nz:
        devices = nz * 8
        per, down_per = feat // devices, ff // devices
        blocks = (nz,) + BLOCKS
        call.arg("d_up", saved["d_up"].reshape(blocks + (per, ff + feat)), ANYWHERE)
        call.arg("d_down", saved["d_down"].reshape(blocks + (down_per, feat)), ANYWHERE)
        for name, shape in (("o_up", (per, ff)), ("o_out", (per, feat)), ("o_down", (down_per, feat)), ("o_qkv", (per, 3 * feat)),
                            ("o_time", (per, feat)), ("o_char", (chars, per)), ("o_ln", (4, per))):
            call.out(name, shape, F32, whole(shape))
        tails = {"up": (per, ff + feat), "down": (down_per, feat), "qkv": (per, 3 * feat), "rest": (per, 128 + feat)}
        for name, tail in tails.items():
            for part, kind in zip(("own", "far", "near", "line", "sems"), Scatter.scratch(nz, tail, BF16)):
                call.temp(f"{name}_{part}", kind)
        for name in ("up", "down"):
            call.temp(f"{name}_kept", pltpu.VMEM((nz, 2, 2) + tails[name], BF16))
        call.temp("kept_sems", pltpu.SemaphoreType.DMA((2,)))
        call.temp("d_qkv", pltpu.VMEM(blocks + (per, 3 * feat), BF16))
        call.temp("d_rest", pltpu.VMEM(blocks + (per, 128 + feat), BF16))
    else:
        call.out("d_qkv", (feat, 3 * feat), BF16, whole((feat, 3 * feat)))
        call.out("d_rest", (feat, 128 + feat), BF16, whole((feat, 128 + feat)))

    def kernel(r):
        i = pl.program_id(0)
        if nz:
            z, x, y, c = place()
            group = lambda name, mine, kept: Scatter(nz, mine, kept, *[getattr(r, f"{name}_{p}") for p in ("own", "far", "near", "line", "sems")])
            up = group("up", r.d_up, lambda k, a, b, cols: r.up_kept[k, a, b, :, cols])
            down = group("down", r.d_down, lambda k, a, b, cols: r.down_kept[k, a, b, :, cols])
            qkv = group("qkv", r.d_qkv, lambda k, a, b, cols: r.d_qkv[k, a, b, c, :, cols])
            rest = group("rest", r.d_rest, lambda k, a, b, cols: r.d_rest[k, a, b, c, :, cols])
            keep = [pltpu.make_async_copy(g.mine.at[pl.ds(0, nz), :, :, c], kept, r.kept_sems.at[k])
                    for k, (g, kept) in enumerate(((up, r.up_kept), (down, r.down_kept)))]

        @pl.when(i == 0)
        def _():
            if nz:
                greet(nz)
                for copy in keep:
                    copy.start()
            r.ln1[...] = jnp.zeros_like(r.ln1)
            r.d_char[...] = jnp.zeros_like(r.d_char)
            r.gs_f[...] = jnp.zeros_like(r.gs_f)

        @pl.when(i < seqs)
        def _():
            cols = pl.ds(pl.multiple_of(i * length, length), length)
            grad_low = r.grad[...].astype(BF16)
            r.grad_mixed[...] = dot(r.w_out[...], grad_low).astype(BF16).astype(F32)
            heads_backward(r, feat, cols)
            normed, _ = norm_rows(r.start[...])
            r.low_f[:, cols] = (normed * param(r.small, chars) + param(r.small, chars + 1)).astype(BF16)

        def at(step, *acts):
            @pl.when(i == step)
            def _():
                for act in acts:
                    act()

        if nz:
            at(0, lambda: greeted(nz), up.cores, down.cores, lambda: [copy.wait() for copy in keep])
            at(1, up.corners)
            at(2, down.corners)
            at(4, up.sides)
            at(5, down.sides)
            at(seqs - 1, up.lines)
            at(seqs + 1, qkv.corners)
            at(seqs + 2, down.lines)
            at(seqs + 4, qkv.sides)
            at(seqs + 6, qkv.lines)

        tall = lambda value: value.astype(BF16).reshape(r.d_qkv.shape[:-1] + (value.shape[-1],))

        @pl.when(i == seqs)
        def _():
            for p in range(3):
                rows = pl.ds(p * feat, feat)
                r.d_qkv[..., rows] = tall(dot_nt(r.low_f[...], r.gp_f[rows, :]))
            if nz:
                qkv.cores()

        @pl.when(i >= seqs)
        def _():
            k = i - seqs
            cols = pl.ds(pl.multiple_of(k * length, length), length)
            normed, inverse = norm_rows(r.start[...])
            gain = param(r.small, chars)
            grad_normed = dot(r.w_qkv[...], r.gp_f[:, cols])
            d_in = r.grad[...] + norm_rows_back(grad_normed, gain, normed, inverse)
            r.d_in[...] = d_in
            r.ln1[0] += fold(grad_normed * normed)
            r.ln1[1] += fold(grad_normed)
            lane = lax.broadcasted_iota(jnp.int32, r.gs_f.shape, 1)
            r.gs_f[...] += jnp.where(lane == k, jnp.sum(d_in, axis=1, keepdims=True), 0.0)
            one_hot = (lax.broadcasted_iota(jnp.int32, (128, length), 0) == r.tok[0]).astype(BF16)
            high = d_in.astype(BF16)
            low = (d_in - high.astype(F32)).astype(BF16)
            r.d_char[...] += dot_nt(high, one_hot) + dot_nt(low, one_hot)

        @pl.when(i == 2 * seqs - 1)
        def _():
            lane = lax.broadcasted_iota(jnp.int32, r.d_char.shape, 1)
            small = jnp.where(lane < chars, r.d_char[...], 0.0)
            for k, ref in enumerate((r.ln1.at[0], r.ln1.at[1], r.ln2.at[0], r.ln2.at[1])):
                small = jnp.where(lane == chars + k, jnp.sum(ref[...], axis=1, keepdims=True), small)
            r.d_rest[..., :128] = tall(small)
            r.d_rest[..., 128:] = tall(dot_nt(r.waves[...], r.gs_f[...].astype(BF16)))
            if nz:
                rest.cores()
                total = up.total()
                r.o_up[...] = total[:, :ff]
                r.o_out[...] = total[:, ff:]
                r.o_down[...] = down.total()
                rest.corners()
                rest.sides()
                rest.lines()
                r.o_qkv[...] = qkv.total()
                total = rest.total()
                r.o_time[...] = total[:, 128:]
                turned = total[:, :128].T
                r.o_char[...] = turned[:chars]
                r.o_ln[...] = turned[chars:chars + 4]

    return call.run(kernel, "attention_backward", (2 * seqs,), 1 if nz else None)


def hand_over(d_in, parts, width=512):
    feat, n = d_in.shape
    call = Call()
    call.arg("d_in", d_in, lanes(feat, width))
    call.out("o_d_in", (n, feat), F32, pl.BlockSpec((width, feat), lambda i: (i, 0)))
    for name, part in parts.items():
        call.arg(name, part, whole(part.shape))
        if name == "ln":
            for k in range(part.shape[0]):
                call.out(f"o_ln{k}", (1, part.shape[1]), F32, whole((1, part.shape[1])))
        else:
            call.out("o_" + name, part.shape, F32, whole(part.shape))

    def kernel(r):
        r.o_d_in[...] = r.d_in[...].T

        @pl.when(pl.program_id(0) == 0)
        def _():
            for name in parts:
                if name == "ln":
                    for k in range(r.ln.shape[0]):
                        getattr(r, f"o_ln{k}")[...] = r.ln[k:k + 1]
                else:
                    getattr(r, "o_" + name)[...] = getattr(r, name)[...]

    return call.run(kernel, "hand_over", (n // width,))

AXES = ("gx", "gy")


def make_body(gx, gy):
    def gathered(*shards):
        return [lax.all_gather(s, AXES, axis=0, tiled=True) for s in shards]

    def summed(part):
        return lax.psum_scatter(part.astype(F32), AXES, scatter_dimension=0, tiled=True)

    def body(tokens, timesteps, cotangent, char_table, time_weight, ln1_gain, ln1_bias, w_qkv, w_attn_out, ln2_gain, ln2_bias, w_up, w_down):
        devices = gx * gy
        feat = time_weight.shape[1]
        ff = w_up.shape[1]
        chars = char_table.shape[0]
        per = feat // devices
        nz = gx // 2 if gy == 4 and gx % 2 == 0 and per % 16 == 0 and per <= 128 else 0
        shards = [char_table, ln1_gain, ln1_bias, ln2_gain, ln2_bias, time_weight, w_qkv, w_attn_out, w_up, w_down]
        if nz:
            saved = attention_forward(nz, tokens, timesteps, shards)
            small = saved["first_o"].reshape(feat, 128 + feat)
            w_qkv, w_attn_out, w_up, w_down = (saved[k].reshape(-1, saved[k].shape[-1]) for k in ("qkv_o", "out_o", "up", "down"))
        else:
            shards = [lax.all_gather(char_table, AXES, axis=1, tiled=True)] + gathered(*shards[1:])
            _, _, _, _, _, _, w_qkv, w_attn_out, w_up, w_down = shards
            saved = attention_forward(0, tokens, timesteps, shards)
            small = saved["small"]
        saved.update(feed_forward(chars, saved["middle"], cotangent, saved["mixed"], small, w_up, w_down))
        got = attention_backward(nz, chars, tokens, saved["waves"], small, w_qkv, w_attn_out, saved, ff)
        if nz:
            parts = {k: got["o_" + k] for k in ("up", "out", "down", "qkv", "time", "char", "ln")}
        else:
            up_out, down, qkv, rest = (summed(p) for p in (saved["d_up"], saved["d_down"], got["d_qkv"], got["d_rest"]))
            parts = {"up": up_out[:, :ff], "out": up_out[:, ff:], "down": down, "qkv": qkv, "time": rest[:, 128:],
                     "char": rest[:, :chars].T, "ln": rest[:, chars:chars + 4].T}
        o = hand_over(got["d_in"], parts)
        ln = [o[f"o_ln{k}"].reshape(per) for k in range(4)]
        return (saved["result"], o["o_d_in"], o["o_char"], o["o_time"], ln[0], ln[1], o["o_qkv"], o["o_out"], ln[2], ln[3], o["o_up"], o["o_down"])
    return body


def solution(mesh):
    every = P(AXES)
    rows, cols = P(AXES, None), P(None, AXES)
    return jax.shard_map(
        make_body(mesh.shape["gx"], mesh.shape["gy"]),
        mesh=mesh,
        in_specs=(every, every, rows, cols, rows, every, every, rows, rows, every, every, rows, rows),
        out_specs=(rows, rows, cols, rows, every, every, rows, rows, every, every, rows, rows),
        check_vma=False,
    )
```

```python
import math
import types

import jax
import jax.numpy as jnp
from jax import lax
from jax.experimental import pallas as pl
from jax.experimental.pallas import tpu as pltpu
from jax.sharding import PartitionSpec as P

F32, BF16 = jnp.float32, jnp.bfloat16
MESH = pl.DeviceIdType.MESH
AXES = ("gx", "gy")
HEADS = 8
EPSILON = 1e-05
VMEM_LIMIT = 63 * 2**20
BLOCKS = (2, 2, 2)
X, Y, CORE = range(3)


def place():
    gx, gy = lax.axis_index(AXES[0]), lax.axis_index(AXES[1])
    return gx // 2, gx % 2, gy // 2, gy % 2


def device(z, x, y, c):
    return (z * 2 + x, y * 2 + c)


def across(axis):
    z, x, y, c = place()
    return ((z, 1 - x, y, c), (z, x, 1 - y, c), (z, x, y, 1 - c))[axis]


def greet(nz):
    z, x, y, c = place()
    barrier = pltpu.get_barrier_semaphore()
    for where in [across(axis) for axis in (X, Y, CORE)] + [((z + d) % nz, x, y, c) for d in range(1, nz)]:
        pl.semaphore_signal(barrier, inc=1, device_id=device(*where), device_id_type=MESH)


def greeted(nz):
    pl.semaphore_wait(pltpu.get_barrier_semaphore(), 3 + nz - 1)


def halves(width):
    middle = width // 256 * 128
    return pl.ds(0, middle), pl.ds(middle, width - middle)


def blocks_of(out, number):
    if number % 4:
        return out.at[pl.ds(0, number), 0, 0, 0]
    return out.at[pl.ds(0, number // 4), :, :, 0]


class Gather:
    LINES, SIDES, CORNERS, CORES = range(4)

    @staticmethod
    def scratch(nz):
        return pltpu.SemaphoreType.DMA((2, 4))

    def __init__(self, nz, shard, out, sems):
        self.nz, self.shard, self.out, self.sems = nz, shard, out, sems
        self.zs, self.count, self.base, self.waits = pl.ds(0, nz), nz, 0, True

    def send(self, src, dst, sent, came, where):
        return pltpu.make_async_remote_copy(
            src_ref=src, dst_ref=dst, send_sem=self.sems.at[0, sent + (self.base if sent else 0)],
            recv_sem=self.sems.at[1, came + (self.base if came else 0)], device_id=device(*where), device_id_type=MESH)

    def some(self, number, stage):
        ref = blocks_of(self.out, number)
        return self.send(ref, ref, stage, stage, across(CORE))

    def pass_on(self, axis, a, b, sent, came, cut=None):
        c = place()[3]
        ref = self.out.at[self.zs, a, b, c]
        if cut is not None:
            ref = ref.at[:, :, cut]
        self.send(ref, ref, sent, came, across(axis)).start()

    def lines(self):
        z, x, y, c = place()
        for d in range(1, self.nz):
            self.send(self.shard, self.out.at[z, x, y, c], self.LINES, self.LINES, ((z + d) % self.nz, x, y, c)).start()

    def arrived(self):
        self.some(self.nz - 1, self.LINES).wait_recv()

    def sides(self):
        _, x, y, _ = place()
        if self.waits:
            self.arrived()
        self.pass_on(X, x, y, self.SIDES, self.SIDES)
        self.pass_on(Y, x, y, self.SIDES, self.SIDES)
        self.pass_on(CORE, x, y, self.SIDES, self.CORES)

    def corners(self):
        _, x, y, _ = place()
        lo, hi = halves(self.out.shape[-1])
        self.some(2 * self.count, self.SIDES).wait_recv()
        self.pass_on(X, x, 1 - y, self.CORNERS, self.CORNERS, lo)
        self.pass_on(Y, 1 - x, y, self.CORNERS, self.CORNERS, hi)
        self.pass_on(CORE, 1 - x, y, self.CORNERS, self.CORES)
        self.pass_on(CORE, x, 1 - y, self.CORNERS, self.CORES)

    def cores(self):
        _, x, y, _ = place()
        self.some(self.count, self.CORNERS).wait_recv()
        self.pass_on(CORE, 1 - x, 1 - y, self.CORES, self.CORES)

    def whole(self):
        self.some(4 * self.count, self.CORES).wait_recv()

    def sent(self):
        self.some(3 * self.count, self.SIDES).wait_send()
        self.some(3 * self.count, self.CORNERS).wait_send()
        self.some(self.count, self.CORES).wait_send()

    def finish(self):
        self.some(self.nz - 1, self.LINES).wait_send()
        self.sent()


class GatherLayers(Gather):
    @staticmethod
    def scratch(nz):
        return pltpu.SemaphoreType.DMA((2, 1 + 3 * nz))

    def layer(self, j):
        one = Gather(self.nz, self.shard, self.out, self.sems)
        one.zs, one.count, one.base, one.waits = pl.ds(j, 1), 1, 3 * j, False
        return one

    def sent(self):
        for j in range(self.nz):
            self.layer(j).sent()


class Scatter:
    @staticmethod
    def scratch(nz, tail):
        return [pltpu.VMEM((nz, 2, 2) + tail, BF16), pltpu.VMEM((nz,) + tail, BF16), pltpu.VMEM((2, nz) + tail, BF16),
                pltpu.VMEM((nz - 1,) + tail, BF16), pltpu.SemaphoreType.DMA((2, 4))]

    def __init__(self, nz, mine, temps, kept=None):
        self.nz, self.mine, self.kept = nz, mine, kept
        self.own, self.far, self.near, self.line, self.sems = temps
        self.width = self.own.shape[-1]

    def send(self, src, dst, stage, where):
        return pltpu.make_async_remote_copy(
            src_ref=src, dst_ref=dst, send_sem=self.sems.at[0, stage], recv_sem=self.sems.at[1, stage],
            device_id=device(*where), device_id_type=MESH)

    def done(self, ref, stage):
        self.send(ref, ref, stage, across(CORE)).wait()

    def add(self, a, b, cols, *values):
        spot = (slice(None), a, b, slice(None), cols)
        total = self.own[spot]
        for value in values:
            total = total + value
        self.own[spot] = total

    def cores(self):
        c = place()[3]
        self.send(self.mine.at[pl.ds(0, self.nz), :, :, 1 - c], self.own, 0, across(CORE)).start()

    def corners(self):
        _, x, y, c = place()
        every, all_z = pl.ds(0, self.width), pl.ds(0, self.nz)
        lo, hi = halves(self.width)
        self.done(self.own, 0)
        for number, (a, b) in enumerate(((1 - x, 1 - y), (1 - x, y), (x, 1 - y), (x, y))):
            self.add(a, b, every, self.mine[:, a, b, c] if self.kept is None else self.kept[:, a, b])
            if number == 0:
                self.send(self.own.at[all_z, 1 - x, 1 - y, :, lo], self.far.at[:, :, lo], 1, across(X)).start()
                self.send(self.own.at[all_z, 1 - x, 1 - y, :, hi], self.far.at[:, :, hi], 1, across(Y)).start()

    def sides(self):
        _, x, y, _ = place()
        all_z = pl.ds(0, self.nz)
        lo, hi = halves(self.width)
        self.done(self.far, 1)
        self.add(x, 1 - y, lo, self.far[:, :, lo])
        self.send(self.own.at[all_z, x, 1 - y], self.near.at[1], 2, across(Y)).start()
        self.add(1 - x, y, hi, self.far[:, :, hi])
        self.send(self.own.at[all_z, 1 - x, y], self.near.at[0], 2, across(X)).start()

    def lines(self):
        z, x, y, c = place()
        self.done(self.near, 2)
        self.add(x, y, pl.ds(0, self.width), self.near[0], self.near[1])
        for d in range(1, self.nz):
            to = (z + d) % self.nz
            self.send(self.own.at[to, x, y], self.line.at[d - 1], 3, (to, x, y, c)).start()

    def total(self):
        z, x, y, _ = place()
        self.done(self.line, 3)
        total = self.own[z, x, y].astype(F32)
        for d in range(1, self.nz):
            total = total + self.line[d - 1].astype(F32)
        return total


class Call:
    def __init__(self):
        self.ins, self.outs, self.temps = {}, {}, {}

    def arg(self, **named):
        self.ins.update(named)

    def out(self, **named):
        self.outs.update(named)

    def temp(self, **named):
        self.temps.update(named)

    def run(self, kernel, name, steps, collective=None):
        kinds = [k for kind in self.temps.values() for k in (kind if isinstance(kind, list) else [kind])]

        def body(*refs):
            refs = iter(refs)
            r = types.SimpleNamespace(**{n: next(refs) for n in [*self.ins, *self.outs]})
            for n, kind in self.temps.items():
                setattr(r, n, [next(refs) for _ in kind] if isinstance(kind, list) else next(refs))
            kernel(r)
        extra = {} if collective is None else dict(collective_id=collective, has_side_effects=True)
        got = pl.pallas_call(
            body, grid=(steps,), in_specs=[spec for _, spec in self.ins.values()], out_specs=[spec for *_, spec in self.outs.values()],
            out_shape=[jax.ShapeDtypeStruct(shape, kind) for shape, kind, _ in self.outs.values()], scratch_shapes=kinds,
            compiler_params=pltpu.CompilerParams(vmem_limit_bytes=VMEM_LIMIT, **extra), name=name,
        )(*[array for array, _ in self.ins.values()])
        return types.SimpleNamespace(**dict(zip(self.outs, got)))


def whole(shape):
    return pl.BlockSpec(tuple(shape), lambda i: (0,) * len(shape))


def lanes(rows, width, at=lambda i: i):
    return pl.BlockSpec((rows, width), lambda i: (0, at(i)))


ANYWHERE = pl.BlockSpec(memory_space=pl.ANY)


def dispatch(i, table):
    steps = sorted(table)

    def among(some):
        if len(some) == 1:
            @pl.when(i == some[0])
            def _():
                for act in table[some[0]]:
                    act()
            return
        half = len(some) // 2
        pl.when(i < some[half])(lambda: among(some[:half]))
        pl.when(i >= some[half])(lambda: among(some[half:]))
    if steps:
        among(steps)


def dot(left, right):
    return jnp.dot(left, right, preferred_element_type=F32)


def dot_nt(left, right):
    return lax.dot_general(left, right, (((1,), (1,)), ((), ())), preferred_element_type=F32)


def norm_rows(values):
    count = values.shape[0]
    shifted = values - jnp.sum(values, axis=0, keepdims=True) * (1.0 / count)
    inverse = lax.rsqrt(jnp.sum(shifted * shifted, axis=0, keepdims=True) * (1.0 / count) + EPSILON)
    return shifted * inverse, inverse


def norm_rows_back(grad, gain, normed, inverse):
    count = grad.shape[0]
    scaled = grad * gain
    lean = jnp.sum(scaled, axis=0, keepdims=True) * (1.0 / count)
    turn = jnp.sum(scaled * normed, axis=0, keepdims=True) * (1.0 / count)
    return inverse * (scaled - lean - normed * turn)


def fold(values):
    total = values[:, :128]
    for k in range(1, values.shape[1] // 128):
        total = total + values[:, 128 * k:128 * (k + 1)]
    return total


def flat(ref, cols=slice(None)):
    value = ref[(slice(None),) * (len(ref.shape) - 1) + (cols,)]
    return value.reshape(-1, value.shape[-1])


def param(table, column):
    return table[:, column:column + 1].astype(F32)


def gelu_parts(hidden, grad_active):
    cdf = 0.5 + 0.5 * lax.erf(hidden * math.sqrt(0.5))
    bell = jnp.exp2(hidden * hidden * (-0.5 * math.log2(math.e))) * (1.0 / math.sqrt(2.0 * math.pi))
    return (hidden * cdf).astype(BF16), (grad_active.astype(BF16).astype(F32) * (cdf + hidden * bell)).astype(BF16)


def fill_waves(r, feat):
    half = feat // 2
    r.steps_row[...] = jnp.zeros_like(r.steps_row)
    r.steps_row[:, :r.steps.shape[1]] = r.steps[...].astype(F32)
    rate = jnp.exp(lax.broadcasted_iota(jnp.int32, (half, 128), 0).astype(F32) * (-math.log(10000.0) / half))
    angles = rate * r.steps_row[...]
    r.waves[:half, :] = jnp.sin(angles).astype(BF16)
    r.waves[half:, :] = jnp.cos(angles).astype(BF16)


def fill_small(r, chars):
    count = r.char.shape[0]
    r.square[...] = jnp.zeros_like(r.square)
    for k, ref in enumerate((r.g1, r.b1, r.g2, r.b2)):
        r.square[chars + k:chars + k + 1, :count] = ref[...].astype(F32)
    r.small_shard[...] = r.square[...].T[:count].astype(BF16)
    r.small_shard[:, :chars] = r.char[...]


def one_hot_of(tok):
    return (lax.broadcasted_iota(jnp.int32, (128, tok.shape[1]), 0) == tok).astype(BF16)


class Heads:
    def __init__(self, feat):
        self.size = feat // HEADS
        self.q, self.k, self.v = ([pl.ds(part * feat + h * self.size, self.size) for h in range(HEADS)] for part in range(3))

    def scores(self, project, scores):
        for h in range(HEADS):
            scores[h] = dot(project[self.k[h], :].T, project[self.q[h], :])

    def softmax(self, scores, powers, inverses):
        turn = math.log2(math.e) / math.sqrt(self.size)
        for h in range(HEADS):
            value = scores[h]
            power = jnp.exp2((value - jnp.max(value, axis=0, keepdims=True)) * turn)
            inverses[h:h + 1, :] = 1.0 / jnp.sum(power, axis=0, keepdims=True)
            powers[h] = power.astype(BF16)

    def mix(self, project, powers, inverses, mixed):
        for h in range(HEADS):
            mixed[self.q[h], :] = (dot(project[self.v[h], :], powers[h]) * inverses[h:h + 1, :]).astype(BF16)

    def scale_grad(self, grad_mixed, inverses, mixed, scaled, lean):
        for h in range(HEADS):
            value = grad_mixed[self.q[h], :] * inverses[h:h + 1, :]
            lean[h:h + 1, :] = jnp.sum(value * mixed[self.q[h], :].astype(F32), axis=0, keepdims=True)
            scaled[self.q[h], :] = value.astype(BF16)

    def grad_probs(self, project, scaled, scores):
        for h in range(HEADS):
            scores[h] = dot(project[self.v[h], :].T, scaled[self.q[h], :])

    def grad_scores(self, powers, scores, lean, grads):
        for h in range(HEADS):
            grads[h] = (powers[h].astype(F32) * (scores[h] - lean[h:h + 1, :])).astype(BF16)

    def grad_project(self, project, scaled, powers, grads, out, cols):
        scale = 1.0 / math.sqrt(self.size)
        for h in range(HEADS):
            out[self.v[h], cols] = dot_nt(scaled[self.q[h], :], powers[h]).astype(BF16)
            out[self.q[h], cols] = (dot(project[self.k[h], :], grads[h]) * scale).astype(BF16)
            out[self.k[h], cols] = (dot_nt(project[self.q[h], :], grads[h]) * scale).astype(BF16)


def forward(nz, tokens, timesteps, cotangent, char, g1, b1, g2, b2, time_w, w_qkv, w_out, w_up, w_down, chunk=512):
    seqs = timesteps.shape[0]
    n = tokens.shape[0]
    length = n // seqs
    feat, ff = time_w.shape[1], w_up.shape[1]
    count, chars = char.shape
    pair = 2 if seqs % 2 == 0 else 1
    items, width = seqs // pair, pair * length
    wide = ff // nz if nz else 512
    tiles, chunks = ff // wide, n // chunk
    item_of = lambda i: jnp.minimum(i, items - 1)
    tile_of = lambda i: jnp.clip(i - items, 0, tiles - 1)
    chunk_of = lambda i: jnp.maximum(i - items - tiles, 0)
    heads = Heads(feat)
    call = Call()
    at_once = lambda value: (value, whole(value.shape))
    call.arg(tok=at_once(tokens.reshape(seqs, 1, length)), steps=at_once(timesteps.reshape(1, seqs)), char=at_once(char),
             g1=at_once(g1.reshape(1, count)), b1=at_once(b1.reshape(1, count)), g2=at_once(g2.reshape(1, count)),
             b2=at_once(b2.reshape(1, count)), time_w=at_once(time_w), w_qkv=at_once(w_qkv), w_out=at_once(w_out), w_up=at_once(w_up),
             w_down=at_once(w_down), cot=(cotangent, pl.BlockSpec((width, feat), lambda i: (item_of(i), 0))))
    call.out(start_o=((feat, n), F32, ANYWHERE), mixed_o=((feat, n), BF16, ANYWHERE), project_o=((3 * feat, n), BF16, ANYWHERE),
             powers=((seqs, HEADS, length, length), BF16, pl.BlockSpec((pair, HEADS, length, length), lambda i: (item_of(i), 0, 0, 0))),
             inv=((seqs, HEADS, length), F32, whole((seqs, HEADS, length))), waves=((feat, 128), BF16, whole((feat, 128))),
             grad=((feat, n), F32, lanes(feat, chunk, chunk_of)), ln=((2, feat, 128), F32, whole((2, feat, 128))),
             d_down=((ff, feat), BF16, pl.BlockSpec((ff // chunks, feat), lambda i: (chunk_of(i), 0))),
             middle_o=((feat, n), F32, ANYWHERE), act_o=((ff, n), BF16, ANYWHERE), down_o=((feat, ff), BF16, ANYWHERE))
    parts = 3
    if nz:
        per = feat // (nz * 8)
        blocks = lambda tail: (nz,) + BLOCKS + tail
        landing = lambda *tail: pltpu.VMEM(blocks(tail), BF16)
        sems = Gather.scratch(nz)
        call.temp(first=landing(count, 128 + feat), first_sems=sems, out=landing(count, feat), out_sems=sems,
                  qkv=[landing(count, feat)] * parts, qkv_sems=[sems] * parts, ups=[landing(count, wide)] * tiles, up_sems=[sems] * tiles,
                  down=landing(*w_down.shape), down_sems=GatherLayers.scratch(nz), first_shard=pltpu.VMEM((count, 128 + feat), BF16),
                  save_sems=pltpu.SemaphoreType.DMA((2 + parts,)),
                  mine=pltpu.VMEM((tiles,) + blocks((per, wide)), BF16), sums=Scatter.scratch(nz, (per, wide)) * tiles)
        call.out(first_o=(blocks((count, 128 + feat)), BF16, ANYWHERE), out_o=(blocks((count, feat)), BF16, ANYWHERE),
                 qkv_o=(blocks(w_qkv.shape), BF16, ANYWHERE), o_up=((per, ff), F32, whole((per, ff))))
    else:
        call.out(small=((count, 128), BF16, whole((count, 128))), d_up=((feat, ff), BF16, lanes(feat, wide, tile_of)))
    vmem = lambda kind, *shape: pltpu.VMEM(shape, kind)
    call.temp(small_shard=vmem(BF16, count, 128), square=vmem(F32, 128, max(count, 128)), steps_row=vmem(F32, 1, 128),
              stamps=vmem(F32, feat, 128), out_t=vmem(BF16, feat, feat), starts=vmem(F32, feat, n), mixed=vmem(BF16, feat, n),
              scores=vmem(F32, pair * HEADS, length, length), middle=vmem(F32, feat, n), low2=vmem(BF16, feat, n), cot_f=vmem(BF16, feat, n),
              down_t=vmem(BF16, feat, ff), up=vmem(BF16, feat, ff), up_t=vmem(BF16, wide, feat), down_rows=vmem(BF16, wide, feat),
              act=vmem(BF16, ff, n), gh=vmem(BF16, ff, n), later_sems=pltpu.SemaphoreType.DMA((3,)), soon_sems=pltpu.SemaphoreType.DMA((3,)))

    def kernel(r):
        i = pl.program_id(0)
        proj, low = r.act.at[pl.ds(0, 3 * feat)], r.gh.at[pl.ds(0, feat)]
        later = [pltpu.make_async_copy(a, b, r.later_sems.at[k])
                 for k, (a, b) in enumerate(((r.middle, r.middle_o), (r.act, r.act_o), (r.down_t, r.down_o)))]
        soon = [pltpu.make_async_copy(a, b, r.soon_sems.at[k])
                for k, (a, b) in enumerate(((proj, r.project_o), (r.starts, r.start_o), (r.mixed, r.mixed_o)))]
        if nz:
            z, x, y, c = place()
            first = Gather(nz, r.first_shard, r.first, r.first_sems)
            qkv = [Gather(nz, r.w_qkv.at[:, pl.ds(p * feat, feat)], r.qkv[p], r.qkv_sems[p]) for p in range(parts)]
            out = Gather(nz, r.w_out, r.out, r.out_sems)
            ups = [Gather(nz, r.w_up.at[:, pl.ds(j * wide, wide)], r.ups[j], r.up_sems[j]) for j in range(tiles)]
            down = GatherLayers(nz, r.w_down, r.down, r.down_sems)
            needs = [(ups[j], down.layer(j)) for j in range(tiles)]
            every = (pl.ds(0, nz), slice(None), slice(None), slice(None), slice(None))
            save = [pltpu.make_async_copy(r.first, r.first_o, r.save_sems.at[0]), pltpu.make_async_copy(r.out, r.out_o, r.save_sems.at[1])]
            save += [pltpu.make_async_copy(g.out, r.qkv_o.at[every + (pl.ds(p * feat, feat),)], r.save_sems.at[2 + p]) for p, g in enumerate(qkv)]
            groups = [Scatter(nz, r.mine.at[j], r.sums[5 * j:5 * j + 5]) for j in range(tiles)]

        def small():
            return flat(r.first, slice(0, 128)) if nz else r.small[...]

        def begin(some):
            table = small()
            for k in some:
                cols = pl.ds(k * length, length)
                lane = lax.broadcasted_iota(jnp.int32, r.stamps.shape, 1)
                stamp = jnp.sum(jnp.where(lane == k, r.stamps[...], 0.0), axis=1, keepdims=True)
                start = dot(table, one_hot_of(r.tok[k])) + stamp
                r.starts[:, cols] = start
                normed, _ = norm_rows(start)
                low[:, cols] = (normed * param(table, chars) + param(table, chars + 1)).astype(BF16)

        def multiply(p, weights):
            proj[p * feat:(p + 1) * feat] = dot(weights.T, low[...]).astype(BF16)

        def prelude():
            r.ln[...] = jnp.zeros_like(r.ln)
            if not nz:
                fill_small(r, chars)
                r.small[...] = r.small_shard[...]
                fill_waves(r, feat)
                r.stamps[...] = dot(r.time_w[...].T, r.waves[...])
                r.out_t[...] = r.w_out[...].T
                begin(range(seqs))
                for p in range(parts):
                    multiply(p, r.w_qkv[:, p * feat:(p + 1) * feat])
                for copy in soon[:2]:
                    copy.start()
                return
            greet(nz)
            fill_small(r, chars)
            q, k, v = qkv
            r.first_shard[:, :128] = r.small_shard[...]
            r.first_shard[:, 128:] = r.time_w[...]
            for g in (first, out, q, k, v, *ups, down):
                g.out[z, x, y, c] = g.shard[...]
            greeted(nz)
            first.lines()
            q.lines()
            fill_waves(r, feat)
            first.sides()
            k.lines()
            q.sides()
            v.lines()
            first.corners()
            k.sides()
            out.lines()
            q.corners()
            first.cores()
            v.sides()
            ups[0].lines()
            k.corners()
            q.cores()
            first.whole()
            r.stamps[...] = dot(flat(r.first, slice(128, 128 + feat)).T, r.waves[...])
            begin(range(0, seqs // 2))
            out.sides()
            down.lines()
            v.corners()
            k.cores()
            begin(range(seqs // 2, seqs))
            soon[1].start()
            q.whole()
            multiply(0, flat(r.qkv[0]))
            out.corners()
            v.cores()
            ups[0].sides()
            ups[1].lines()
            k.whole()
            multiply(1, flat(r.qkv[1]))
            v.whole()
            multiply(2, flat(r.qkv[2]))
            soon[0].start()
            out.cores()
            for g in ups[2:]:
                g.lines()
            down.arrived()
            needs[0][1].sides()

        def all_out():
            if nz:
                out.whole()
                r.out_t[...] = flat(r.out).T
                for copy in save:
                    copy.start()

        def tile_weights(j):
            if nz:
                for part in needs[j]:
                    part.whole()
                tile = flat(r.ups[j])
                r.down_rows[...] = flat(r.down.at[pl.ds(j, 1)])
            else:
                tile = r.w_up[:, j * wide:(j + 1) * wide]
                r.down_rows[...] = r.w_down[j * wide:(j + 1) * wide]
            r.up[:, j * wide:(j + 1) * wide] = tile
            r.up_t[...] = tile.T

        before = {}

        def at(step, *acts):
            before.setdefault(step, []).extend(acts)

        at(0, prelude)
        if nz:
            for j, some in enumerate(needs):
                for part in some:
                    if j > 0:
                        at(j, part.sides)
                    at(j + 1, part.corners)
                    at(j + 2, part.cores)
            for j, g in enumerate(groups):
                at(items + j + 1, g.cores)
                at(items + j + 2, g.corners)
                at(items + j + 3, g.sides)
                at(items + j + 4, g.lines)
        at(items, *[copy.wait for copy in soon[:2]], soon[2].start)
        for j in range(tiles):
            at(items + j, lambda j=j: tile_weights(j))
        at(items + tiles, soon[2].wait, *[copy.start for copy in later])
        dispatch(i, before)

        @pl.when(i < items)
        def _():
            def views(k):
                cols = pl.ds(pl.multiple_of((i * pair + k) * length, length), length)
                return proj.at[:, cols], r.scores.at[pl.ds(k * HEADS, HEADS)], r.powers.at[k], r.inv.at[i * pair + k], r.mixed.at[:, cols]

            for k in range(pair):
                project, scores, powers, inverses, mixed = views(k)
                heads.scores(project, scores)
            for k in range(pair):
                project, scores, powers, inverses, mixed = views(k)
                heads.softmax(scores, powers, inverses)
                heads.mix(project, powers, inverses, mixed)
            pl.when(i == 0)(all_out)
            cols = pl.ds(pl.multiple_of(i * width, width), width)
            middle = r.starts[:, cols] + dot(r.out_t[...], r.mixed[:, cols])
            r.middle[:, cols] = middle
            normed, _ = norm_rows(middle)
            r.low2[:, cols] = (normed * param(small(), chars + 2) + param(small(), chars + 3)).astype(BF16)
            r.cot_f[:, cols] = r.cot[...].T

        @pl.when((i >= items) & (i < items + tiles))
        def _():
            first_row = pl.multiple_of((i - items) * wide, wide)
            rows = pl.ds(first_row, wide)
            r.down_t[:, rows] = r.down_rows[...].T
            for t in range(chunks):
                cols = pl.ds(t * chunk, chunk)
                for half in range(2):
                    some = pl.ds(half * wide // 2, wide // 2)
                    part = pl.ds(pl.multiple_of(first_row + half * (wide // 2), wide // 2), wide // 2)
                    r.act[part, cols], r.gh[part, cols] = gelu_parts(
                        dot(r.up_t[some, :], r.low2[:, cols]), dot(r.down_rows[some, :], r.cot_f[:, cols]))
            d_up = dot_nt(r.low2[...], r.gh[rows, :]).astype(BF16)
            if nz:
                r.mine[i - items] = d_up.reshape(blocks((per, wide)))
            else:
                r.d_up[...] = d_up

        @pl.when(i >= items + tiles)
        def _():
            cols = pl.ds(pl.multiple_of((i - items - tiles) * chunk, chunk), chunk)
            grad_normed = dot(r.up[...], r.gh[:, cols])
            share = ff // chunks
            r.d_down[...] = dot_nt(r.act[pl.ds(pl.multiple_of((i - items - tiles) * share, share), share), :], r.cot_f[...]).astype(BF16)
            normed, inverse = norm_rows(r.middle[:, cols])
            gain = param(small(), chars + 2)
            r.grad[...] = r.cot_f[:, cols].astype(F32) + norm_rows_back(grad_normed, gain, normed, inverse)
            r.ln[0] += fold(grad_normed * normed)
            r.ln[1] += fold(grad_normed)

        @pl.when(i == items + tiles + chunks - 1)
        def _():
            for copy in later:
                copy.wait()
            if nz:
                for g in (first, *qkv, out, *ups, down):
                    g.finish()
                for copy in save:
                    copy.wait()
                for j in range(tiles):
                    r.o_up[:, j * wide:(j + 1) * wide] = groups[j].total()

    return call.run(kernel, "forward_and_ffn", items + tiles + chunks, 0 if nz else None)


def backward(nz, chars, tokens, small, w_qkv, w_out, saved, chunk=512):
    feat, n = saved.start_o.shape
    seqs = saved.powers.shape[0]
    ff = saved.act_o.shape[0]
    length = n // seqs
    pair = 2 if seqs % 2 == 0 else 1
    items, width, chunks = seqs // pair, pair * length, n // chunk
    heads = Heads(feat)
    late = lambda i: jnp.clip(i - items, 0, items - 1)
    soon = lambda i: jnp.minimum(i, items - 1)
    twice = lambda i: jnp.where(i < 2 * items, i % items, items - 1)
    last = lambda i: jnp.maximum(i - 2 * items, 0)
    at_once = lambda value: (value, whole(value.shape))
    call = Call()
    call.arg(tok=(tokens.reshape(seqs, 1, length), pl.BlockSpec((pair, 1, length), lambda i: (late(i), 0, 0))), waves=at_once(saved.waves),
             small=(small, whole((feat, 128))), w_qkv=(w_qkv, ANYWHERE), w_out=at_once(w_out), start=(saved.start_o, lanes(feat, width, twice)),
             grad=(saved.grad, lanes(feat, width, twice)), project=(saved.project_o, lanes(3 * feat, width, soon)),
             powers=(saved.powers, pl.BlockSpec((pair, HEADS, length, length), lambda i: (soon(i), 0, 0, 0))), inv=at_once(saved.inv),
             mixed=at_once(saved.mixed_o), ln2=(saved.ln, ANYWHERE),
             middle_i=(saved.middle_o, ANYWHERE), act_i=(saved.act_o, ANYWHERE), down_i=(saved.down_o, ANYWHERE))
    call.out(d_in=((feat, n), F32, lanes(feat, width, late)), result=((feat, n), F32, lanes(feat, chunk, last)))
    vmem = lambda kind, *shape: pltpu.VMEM(shape, kind)
    call.temp(ln1=vmem(F32, 2, feat, 128), d_char=vmem(F32, feat, 128), low_f=vmem(BF16, feat, n), gp_f=vmem(BF16, 3 * feat, n),
              scores=vmem(F32, HEADS, length, length), grads=vmem(BF16, HEADS, length, length), grad_mixed=vmem(F32, feat, width),
              scaled=vmem(BF16, feat, width), lean=vmem(F32, seqs, HEADS, length), ga_f=vmem(BF16, feat, n), gs_f=vmem(F32, feat, 128),
              act=vmem(BF16, ff, n), middle=vmem(F32, feat, n), down_t=vmem(BF16, feat, ff), qkv=vmem(BF16, feat, 3 * feat),
              ln2_s=vmem(F32, 2, feat, 128), fetch_sems=pltpu.SemaphoreType.DMA((5,)))
    parts = 4
    if nz:
        devices = nz * 8
        per, down_per = feat // devices, ff // devices
        blocks = (nz,) + BLOCKS
        call.arg(d_down=(saved.d_down.reshape(blocks + (down_per, feat)), ANYWHERE))
        small_out = lambda *shape: (shape, F32, whole(shape))
        call.out(o_out=small_out(per, feat), o_down=small_out(down_per, feat), o_qkv=small_out(per, 3 * feat), o_time=small_out(per, feat),
                 o_char=small_out(per, chars), o_ln=small_out(4, per))
        call.temp(down_sums=Scatter.scratch(nz, (down_per, feat)), rest_sums=Scatter.scratch(nz, (per, 128 + feat)),
                  at_sums=Scatter.scratch(nz, (per, feat)) * parts, kept=vmem(BF16, nz, 2, 2, down_per, feat), kept_sem=pltpu.SemaphoreType.DMA,
                  d_at=[vmem(BF16, *blocks, per, feat)] * parts, d_rest=vmem(BF16, *blocks, per, 128 + feat))
    else:
        call.out(d_at=((feat, 4 * feat), BF16, whole((feat, 4 * feat))), d_rest=((feat, 128 + feat), BF16, whole((feat, 128 + feat))))

    def kernel(r):
        i = pl.program_id(0)
        fetch = [pltpu.make_async_copy(a, b, r.fetch_sems.at[k])
                 for k, (a, b) in enumerate(((r.w_qkv, r.qkv), (r.ln2, r.ln2_s), (r.middle_i, r.middle), (r.act_i, r.act), (r.down_i, r.down_t)))]
        if nz:
            c = place()[3]
            down = Scatter(nz, r.d_down, r.down_sums, r.kept)
            ats = [Scatter(nz, r.d_at[p], r.at_sums[5 * p:5 * p + 5]) for p in range(parts)]
            rest = Scatter(nz, r.d_rest, r.rest_sums)
            keep = pltpu.make_async_copy(r.d_down.at[pl.ds(0, nz), :, :, c], r.kept, r.kept_sem)

        def tall(value):
            value = value.astype(BF16)
            return value.reshape(blocks + (per, value.shape[-1])) if nz else value

        def prelude():
            if nz:
                greet(nz)
                keep.start()
            for copy in fetch:
                copy.start()
            r.ln1[...] = jnp.zeros_like(r.ln1)
            r.d_char[...] = jnp.zeros_like(r.d_char)
            r.gs_f[...] = jnp.zeros_like(r.gs_f)

        def products():
            pairs = [(r.mixed, r.ga_f)] + [(r.low_f, r.gp_f.at[pl.ds(p * feat, feat)]) for p in range(3)]
            for p, (left, right) in enumerate(pairs):
                product = tall(dot_nt(left[...], right[...]))
                if nz:
                    r.d_at[p][...] = product
                    ats[p].cores()
                    if p > 0:
                        ats[p - 1].corners()
                else:
                    r.d_at[:, p * feat:(p + 1) * feat] = product

        def rest_products():
            lane = lax.broadcasted_iota(jnp.int32, r.d_char.shape, 1)
            table = jnp.where(lane < chars, r.d_char[...], 0.0)
            for k, ref in enumerate((r.ln1.at[0], r.ln1.at[1], r.ln2_s.at[0], r.ln2_s.at[1])):
                table = jnp.where(lane == chars + k, jnp.sum(ref[...], axis=1, keepdims=True), table)
            r.d_rest[..., :128] = tall(table)
            r.d_rest[..., 128:] = tall(dot_nt(r.waves[...], r.gs_f[...].astype(BF16)))
            if nz:
                rest.cores()

        before = {}

        def at(step, *acts):
            before.setdefault(step, []).extend(acts)

        at(0, prelude)
        if nz:
            at(1, lambda: greeted(nz), down.cores, keep.wait)
            at(2, down.corners)
            at(items, down.sides)
        at(items, fetch[0].wait, fetch[1].wait, products)
        if nz:
            at(items + 1, ats[3].corners, ats[0].sides, ats[1].sides)
            at(items + 2, down.lines, ats[2].sides, ats[3].sides, ats[0].lines)
            at(items + 3, ats[1].lines)
        at(2 * items, rest_products, *[copy.wait for copy in fetch[2:]])
        if nz:
            at(2 * items, ats[2].lines, ats[3].lines)
            at(2 * items + 1, rest.corners)
            at(2 * items + 2, rest.sides)
        dispatch(i, before)

        @pl.when(i < items)
        def _():
            cols = pl.ds(pl.multiple_of(i * width, width), width)
            grad_low = r.grad[...].astype(BF16)
            r.ga_f[:, cols] = grad_low
            r.grad_mixed[...] = dot(r.w_out[...], grad_low).astype(BF16).astype(F32)
            for k in range(pair):
                here = pl.ds(k * length, length)
                item = i * pair + k
                there = pl.ds(pl.multiple_of(item * length, length), length)
                project, scaled, powers = r.project.at[:, here], r.scaled.at[:, here], r.powers.at[k]
                heads.scale_grad(r.grad_mixed.at[:, here], r.inv.at[item], r.mixed.at[:, there], scaled, r.lean.at[item])
                heads.grad_probs(project, scaled, r.scores)
                heads.grad_scores(powers, r.scores, r.lean.at[item], r.grads)
                heads.grad_project(project, scaled, powers, r.grads, r.gp_f, there)
            normed, _ = norm_rows(r.start[...])
            r.low_f[:, cols] = (normed * param(r.small, chars) + param(r.small, chars + 1)).astype(BF16)

        @pl.when((i >= items) & (i < 2 * items))
        def _():
            k = i - items
            cols = pl.ds(pl.multiple_of(k * width, width), width)
            grad_normed = dot(r.qkv[...], r.gp_f[:, cols])
            normed, inverse = norm_rows(r.start[...])
            d_in = r.grad[...] + norm_rows_back(grad_normed, param(r.small, chars), normed, inverse)
            r.d_in[...] = d_in
            r.ln1[0] += fold(grad_normed * normed)
            r.ln1[1] += fold(grad_normed)
            lane = lax.broadcasted_iota(jnp.int32, r.gs_f.shape, 1)
            sums = r.gs_f[...]
            for j in range(pair):
                part = d_in[:, j * length:(j + 1) * length]
                sums = jnp.where(lane == k * pair + j, jnp.sum(part, axis=1, keepdims=True), sums)
                one_hot = one_hot_of(r.tok[j])
                high = part.astype(BF16)
                rest_of = (part - high.astype(F32)).astype(BF16)
                r.d_char[...] += dot_nt(high, one_hot) + dot_nt(rest_of, one_hot)
            r.gs_f[...] = sums

        @pl.when(i >= 2 * items)
        def _():
            cols = pl.ds(pl.multiple_of((i - 2 * items) * chunk, chunk), chunk)
            r.result[...] = r.middle[:, cols] + dot(r.down_t[...], r.act[:, cols])

        if nz:
            @pl.when(i == 2 * items + chunks - 1)
            def _():
                rest.lines()
                r.o_down[...] = down.total()
                r.o_out[...] = ats[0].total()
                for p in range(3):
                    r.o_qkv[:, p * feat:(p + 1) * feat] = ats[1 + p].total()
                total = rest.total()
                r.o_time[...] = total[:, 128:]
                r.o_char[...] = total[:, :chars]
                r.o_ln[...] = total[:, :128].T[chars:chars + 4]

    return call.run(kernel, "backward", 2 * items + chunks, 1 if nz else None)


def hand_over(result, d_in, ln, *others, width=1024):
    feat, n = d_in.shape
    call = Call()
    turned = ((n, feat), F32, pl.BlockSpec((width, feat), lambda i: (i, 0)))
    call.arg(result=(result, lanes(feat, width)), d_in=(d_in, lanes(feat, width)), ln=(ln, whole(ln.shape)))
    call.arg(**{f"a{k}": (value, whole(value.shape)) for k, value in enumerate(others)})
    call.out(o_result=turned, o_d_in=turned, **{f"l{k}": ((1, ln.shape[1]), F32, whole((1, ln.shape[1]))) for k in range(4)})
    call.out(**{f"o{k}": (value.shape, F32, whole(value.shape)) for k, value in enumerate(others)})

    def kernel(r):
        r.o_result[...] = r.result[...].T
        r.o_d_in[...] = r.d_in[...].T

        @pl.when(pl.program_id(0) == 0)
        def _():
            for k, ref in enumerate((r.l0, r.l1, r.l2, r.l3)):
                ref[...] = r.ln[k:k + 1]
            for k in range(len(others)):
                getattr(r, f"o{k}")[...] = getattr(r, f"a{k}")[...]

    got = call.run(kernel, "hand_over", n // width)
    return got.o_result, got.o_d_in, [getattr(got, f"l{k}") for k in range(4)], [getattr(got, f"o{k}") for k in range(len(others))]


def make_body(gx, gy):
    def gathered(*shards):
        return [lax.all_gather(s, AXES, axis=0, tiled=True) for s in shards]

    def summed(part):
        return lax.psum_scatter(part.astype(F32), AXES, scatter_dimension=0, tiled=True)

    def body(tokens, timesteps, cotangent, char_table, time_weight, ln1_gain, ln1_bias, w_qkv, w_attn_out, ln2_gain, ln2_bias, w_up, w_down):
        feat = time_weight.shape[1]
        chars = char_table.shape[0]
        per = feat // (gx * gy)
        nz = gx // 2 if gy == 4 and gx % 8 == 0 and per % 16 == 0 else 0
        shards = [char_table.T, ln1_gain, ln1_bias, ln2_gain, ln2_bias, time_weight, w_qkv, w_attn_out, w_up, w_down]
        if not nz:
            shards = gathered(*shards)
        saved = forward(nz, tokens, timesteps, cotangent, *shards)
        if nz:
            small, w_qkv, w_out = (value.reshape(feat, value.shape[-1]) for value in (saved.first_o, saved.qkv_o, saved.out_o))
            got = backward(nz, chars, tokens, small, w_qkv, w_out, saved)
            ln, sums = got.o_ln, (got.o_char, got.o_time, got.o_qkv, got.o_out, saved.o_up, got.o_down)
        else:
            got = backward(nz, chars, tokens, saved.small, *shards[6:8], saved)
            up, down, at, rest = (summed(p) for p in (saved.d_up, saved.d_down, got.d_at, got.d_rest))
            ln, sums = rest[:, chars:chars + 4].T, (rest[:, :chars], rest[:, 128:], at[:, feat:], at[:, :feat], up, down)
        result, d_in, lns, (char, time, qkv, out, up, down) = hand_over(got.result, got.d_in, ln, *sums)
        g1, b1, g2, b2 = (value.reshape(per) for value in lns)
        return result, d_in, char.T, time, g1, b1, qkv, out, g2, b2, up, down
    return body


def solution(mesh):
    every = P(AXES)
    rows, cols = P(AXES, None), P(None, AXES)
    return jax.shard_map(
        make_body(mesh.shape[AXES[0]], mesh.shape[AXES[1]]),
        mesh=mesh,
        in_specs=(every, every, rows, cols, rows, every, every, rows, rows, every, every, rows, rows),
        out_specs=(rows, rows, cols, rows, every, every, rows, rows, every, every, rows, rows),
        check_vma=False,
    )
```

```python
import math
import types

import jax
import jax.numpy as jnp
from jax import lax
from jax.experimental import pallas as pl
from jax.experimental.pallas import tpu as pltpu
from jax.sharding import PartitionSpec as P

F32, BF16 = jnp.float32, jnp.bfloat16
MESH = pl.DeviceIdType.MESH
AXES = ("gx", "gy")
HEADS = 8
EPSILON = 1e-05
VMEM_LIMIT = 63 * 2**20
BLOCKS = (2, 2, 2)
X, Y, CORE = range(3)


def place():
    gx, gy = lax.axis_index(AXES[0]), lax.axis_index(AXES[1])
    return gx // 2, gx % 2, gy // 2, gy % 2


def device(z, x, y, c):
    return (z * 2 + x, y * 2 + c)


def across(axis):
    z, x, y, c = place()
    return ((z, 1 - x, y, c), (z, x, 1 - y, c), (z, x, y, 1 - c))[axis]


def greet(nz):
    z, x, y, c = place()
    barrier = pltpu.get_barrier_semaphore()
    for where in [across(axis) for axis in (X, Y, CORE)] + [((z + d) % nz, x, y, c) for d in range(1, nz)]:
        pl.semaphore_signal(barrier, inc=1, device_id=device(*where), device_id_type=MESH)


def greeted(nz):
    pl.semaphore_wait(pltpu.get_barrier_semaphore(), 3 + nz - 1)


def halves(width):
    middle = width // 256 * 128
    return pl.ds(0, middle), pl.ds(middle, width - middle)


def blocks_of(out, number):
    if number % 4:
        return out.at[pl.ds(0, number), 0, 0, 0]
    return out.at[pl.ds(0, number // 4), :, :, 0]


class Gather:
    LINES, SIDES, CORNERS, CORES = range(4)

    @staticmethod
    def scratch(nz):
        return pltpu.SemaphoreType.DMA((2, 4))

    def __init__(self, nz, shard, out, sems):
        self.nz, self.shard, self.out, self.sems = nz, shard, out, sems
        self.zs, self.count, self.base, self.waits = pl.ds(0, nz), nz, 0, True

    def send(self, src, dst, sent, came, where):
        return pltpu.make_async_remote_copy(
            src_ref=src, dst_ref=dst, send_sem=self.sems.at[0, sent + (self.base if sent else 0)],
            recv_sem=self.sems.at[1, came + (self.base if came else 0)], device_id=device(*where), device_id_type=MESH)

    def some(self, number, stage):
        ref = blocks_of(self.out, number)
        return self.send(ref, ref, stage, stage, across(CORE))

    def pass_on(self, axis, a, b, sent, came, cut=None):
        c = place()[3]
        ref = self.out.at[self.zs, a, b, c]
        if cut is not None:
            ref = ref.at[:, :, cut]
        self.send(ref, ref, sent, came, across(axis)).start()

    def lines(self):
        z, x, y, c = place()
        for d in range(1, self.nz):
            self.send(self.shard, self.out.at[z, x, y, c], self.LINES, self.LINES, ((z + d) % self.nz, x, y, c)).start()

    def arrived(self):
        self.some(self.nz - 1, self.LINES).wait_recv()

    def sides(self):
        _, x, y, _ = place()
        if self.waits:
            self.arrived()
        self.pass_on(X, x, y, self.SIDES, self.SIDES)
        self.pass_on(Y, x, y, self.SIDES, self.SIDES)
        self.pass_on(CORE, x, y, self.SIDES, self.CORES)

    def corners(self):
        _, x, y, _ = place()
        lo, hi = halves(self.out.shape[-1])
        self.some(2 * self.count, self.SIDES).wait_recv()
        self.pass_on(X, x, 1 - y, self.CORNERS, self.CORNERS, lo)
        self.pass_on(Y, 1 - x, y, self.CORNERS, self.CORNERS, hi)
        self.pass_on(CORE, 1 - x, y, self.CORNERS, self.CORES)
        self.pass_on(CORE, x, 1 - y, self.CORNERS, self.CORES)

    def cores(self):
        _, x, y, _ = place()
        self.some(self.count, self.CORNERS).wait_recv()
        self.pass_on(CORE, 1 - x, 1 - y, self.CORES, self.CORES)

    def whole(self):
        self.some(4 * self.count, self.CORES).wait_recv()

    def sent(self):
        self.some(3 * self.count, self.SIDES).wait_send()
        self.some(3 * self.count, self.CORNERS).wait_send()
        self.some(self.count, self.CORES).wait_send()

    def finish(self):
        self.some(self.nz - 1, self.LINES).wait_send()
        self.sent()


class GatherLayers(Gather):
    @staticmethod
    def scratch(nz):
        return pltpu.SemaphoreType.DMA((2, 1 + 3 * nz))

    def layer(self, j):
        one = Gather(self.nz, self.shard, self.out, self.sems)
        one.zs, one.count, one.base, one.waits = pl.ds(j, 1), 1, 3 * j, False
        return one

    def sent(self):
        for j in range(self.nz):
            self.layer(j).sent()


class Scatter:
    @staticmethod
    def scratch(nz, tail):
        return [pltpu.VMEM((nz, 2, 2) + tail, BF16), pltpu.VMEM((nz,) + tail, BF16), pltpu.VMEM((2, nz) + tail, BF16),
                pltpu.VMEM((nz - 1,) + tail, BF16), pltpu.SemaphoreType.DMA((2, 4))]

    def __init__(self, nz, mine, temps, kept=None):
        self.nz, self.mine, self.kept = nz, mine, kept
        self.own, self.far, self.near, self.line, self.sems = temps
        self.width = self.own.shape[-1]

    def send(self, src, dst, stage, where):
        return pltpu.make_async_remote_copy(
            src_ref=src, dst_ref=dst, send_sem=self.sems.at[0, stage], recv_sem=self.sems.at[1, stage],
            device_id=device(*where), device_id_type=MESH)

    def done(self, ref, stage):
        self.send(ref, ref, stage, across(CORE)).wait()

    def add(self, a, b, cols, *values):
        spot = (slice(None), a, b, slice(None), cols)
        total = self.own[spot]
        for value in values:
            total = total + value
        self.own[spot] = total

    def cores(self):
        c = place()[3]
        self.send(self.mine.at[pl.ds(0, self.nz), :, :, 1 - c], self.own, 0, across(CORE)).start()

    def corners(self):
        _, x, y, c = place()
        every, all_z = pl.ds(0, self.width), pl.ds(0, self.nz)
        lo, hi = halves(self.width)
        self.done(self.own, 0)
        for number, (a, b) in enumerate(((1 - x, 1 - y), (1 - x, y), (x, 1 - y), (x, y))):
            self.add(a, b, every, self.mine[:, a, b, c] if self.kept is None else self.kept[:, a, b])
            if number == 0:
                self.send(self.own.at[all_z, 1 - x, 1 - y, :, lo], self.far.at[:, :, lo], 1, across(X)).start()
                self.send(self.own.at[all_z, 1 - x, 1 - y, :, hi], self.far.at[:, :, hi], 1, across(Y)).start()

    def sides(self):
        _, x, y, _ = place()
        all_z = pl.ds(0, self.nz)
        lo, hi = halves(self.width)
        self.done(self.far, 1)
        self.add(x, 1 - y, lo, self.far[:, :, lo])
        self.send(self.own.at[all_z, x, 1 - y], self.near.at[1], 2, across(Y)).start()
        self.add(1 - x, y, hi, self.far[:, :, hi])
        self.send(self.own.at[all_z, 1 - x, y], self.near.at[0], 2, across(X)).start()

    def lines(self):
        z, x, y, c = place()
        self.done(self.near, 2)
        self.add(x, y, pl.ds(0, self.width), self.near[0], self.near[1])
        for d in range(1, self.nz):
            to = (z + d) % self.nz
            self.send(self.own.at[to, x, y], self.line.at[d - 1], 3, (to, x, y, c)).start()

    def total(self):
        z, x, y, _ = place()
        self.done(self.line, 3)
        total = self.own[z, x, y].astype(F32)
        for d in range(1, self.nz):
            total = total + self.line[d - 1].astype(F32)
        return total


class Call:
    def __init__(self):
        self.ins, self.outs, self.temps = {}, {}, {}

    def arg(self, **named):
        self.ins.update(named)

    def out(self, **named):
        self.outs.update(named)

    def temp(self, **named):
        self.temps.update(named)

    def run(self, kernel, name, steps=None, collective=None):
        kinds = [k for kind in self.temps.values() for k in (kind if isinstance(kind, list) else [kind])]

        def body(*refs):
            refs = iter(refs)
            r = types.SimpleNamespace(**{n: next(refs) for n in [*self.ins, *self.outs]})
            for n, kind in self.temps.items():
                setattr(r, n, [next(refs) for _ in kind] if isinstance(kind, list) else next(refs))
            kernel(r)
        extra = {} if collective is None else dict(collective_id=collective, has_side_effects=True)
        got = pl.pallas_call(
            body, grid=() if steps is None else (steps,), in_specs=[spec for _, spec in self.ins.values()], out_specs=[spec for *_, spec in self.outs.values()],
            out_shape=[jax.ShapeDtypeStruct(shape, kind) for shape, kind, _ in self.outs.values()], scratch_shapes=kinds,
            compiler_params=pltpu.CompilerParams(vmem_limit_bytes=VMEM_LIMIT, **extra), name=name,
        )(*[array for array, _ in self.ins.values()])
        return types.SimpleNamespace(**dict(zip(self.outs, got)))


def whole(shape):
    return pl.BlockSpec(tuple(shape), lambda i: (0,) * len(shape))


def lanes(rows, width, at=lambda i: i):
    return pl.BlockSpec((rows, width), lambda i: (0, at(i)))


ANYWHERE = pl.BlockSpec(memory_space=pl.ANY)
RESIDENT = pl.BlockSpec(memory_space=pltpu.VMEM)


def dot(left, right):
    return jnp.dot(left, right, preferred_element_type=F32)


def dot_nt(left, right):
    return lax.dot_general(left, right, (((1,), (1,)), ((), ())), preferred_element_type=F32)


def norm_rows(values):
    count = values.shape[0]
    shifted = values - jnp.sum(values, axis=0, keepdims=True) * (1.0 / count)
    inverse = lax.rsqrt(jnp.sum(shifted * shifted, axis=0, keepdims=True) * (1.0 / count) + EPSILON)
    return shifted * inverse, inverse


def norm_rows_back(grad, gain, normed, inverse):
    count = grad.shape[0]
    scaled = grad * gain
    lean = jnp.sum(scaled, axis=0, keepdims=True) * (1.0 / count)
    turn = jnp.sum(scaled * normed, axis=0, keepdims=True) * (1.0 / count)
    return inverse * (scaled - lean - normed * turn)


def fold(values):
    total = values[:, :128]
    for k in range(1, values.shape[1] // 128):
        total = total + values[:, 128 * k:128 * (k + 1)]
    return total


def flat(ref, cols=slice(None)):
    value = ref[(slice(None),) * (len(ref.shape) - 1) + (cols,)]
    return value.reshape(-1, value.shape[-1])


def param(table, column):
    return table[:, column:column + 1].astype(F32)


def gelu_parts(hidden, grad_active):
    cdf = 0.5 + 0.5 * lax.erf(hidden * math.sqrt(0.5))
    bell = jnp.exp2(hidden * hidden * (-0.5 * math.log2(math.e))) * (1.0 / math.sqrt(2.0 * math.pi))
    return (hidden * cdf).astype(BF16), (grad_active.astype(BF16).astype(F32) * (cdf + hidden * bell)).astype(BF16)


def fill_waves(r, feat):
    half = feat // 2
    r.steps_row[...] = jnp.zeros_like(r.steps_row)
    r.steps_row[:, :r.steps.shape[1]] = r.steps[...].astype(F32)
    rate = jnp.exp(lax.broadcasted_iota(jnp.int32, (half, 128), 0).astype(F32) * (-math.log(10000.0) / half))
    angles = rate * r.steps_row[...]
    r.waves[:half, :] = jnp.sin(angles).astype(BF16)
    r.waves[half:, :] = jnp.cos(angles).astype(BF16)


def fill_small(r, chars):
    count = r.char.shape[0]
    r.square[...] = jnp.zeros_like(r.square)
    for k, ref in enumerate((r.g1, r.b1, r.g2, r.b2)):
        r.square[chars + k:chars + k + 1, :count] = ref[...].astype(F32)
    r.small_shard[...] = r.square[...].T[:count].astype(BF16)
    r.small_shard[:, :chars] = r.char[...]


ITEM_HIGH, ITEM_LOW = 32, 64


def one_hot_of(tok, item):
    row = lax.broadcasted_iota(jnp.int32, (128, tok.shape[1]), 0)
    return ((row == tok) | (row == ITEM_HIGH + item) | (row == ITEM_LOW + item)).astype(BF16)


class Heads:
    def __init__(self, feat):
        self.size = feat // HEADS
        self.q, self.k, self.v = ([pl.ds(part * feat + h * self.size, self.size) for h in range(HEADS)] for part in range(3))

    def scores(self, project, scores):
        for h in range(HEADS):
            scores[h] = dot(project[self.k[h], :].T, project[self.q[h], :])

    def softmax(self, scores, powers, inverses):
        turn = math.log2(math.e) / math.sqrt(self.size)
        for h in range(HEADS):
            value = scores[h]
            power = jnp.exp2((value - jnp.max(value, axis=0, keepdims=True)) * turn)
            inverses[h:h + 1, :] = 1.0 / jnp.sum(power, axis=0, keepdims=True)
            powers[h] = power.astype(BF16)

    def mix(self, project, powers, inverses, mixed):
        for h in range(HEADS):
            mixed[self.q[h], :] = (dot(project[self.v[h], :], powers[h]) * inverses[h:h + 1, :]).astype(BF16)

    def scale_grad(self, grad_mixed, inverses, mixed, scaled, lean):
        for h in range(HEADS):
            value = grad_mixed[self.q[h], :] * inverses[h:h + 1, :]
            lean[h:h + 1, :] = jnp.sum(value * mixed[self.q[h], :].astype(F32), axis=0, keepdims=True)
            scaled[self.q[h], :] = value.astype(BF16)

    def grad_probs(self, project, scaled, scores):
        for h in range(HEADS):
            scores[h] = dot(project[self.v[h], :].T, scaled[self.q[h], :])

    def grad_scores(self, powers, scores, lean, grads):
        for h in range(HEADS):
            grads[h] = (powers[h].astype(F32) * (scores[h] - lean[h:h + 1, :])).astype(BF16)

    def grad_project(self, project, scaled, powers, grads, out, cols):
        scale = 1.0 / math.sqrt(self.size)
        for h in range(HEADS):
            out[self.v[h], cols] = dot_nt(scaled[self.q[h], :], powers[h]).astype(BF16)
            out[self.q[h], cols] = (dot(project[self.k[h], :], grads[h]) * scale).astype(BF16)
            out[self.k[h], cols] = (dot_nt(project[self.q[h], :], grads[h]) * scale).astype(BF16)


class Stream:
    def __init__(self, sems):
        self.sems, self.open = sems, {}

    def start(self, number, src, dst):
        copy = pltpu.make_async_copy(src, dst, self.sems.at[number])
        copy.start()
        self.open[number] = copy

    def wait(self, number):
        if number in self.open:
            self.open.pop(number).wait()

    def close(self):
        for number in list(self.open):
            self.wait(number)


def forward(nz, tokens, timesteps, cotangent, char, g1, b1, g2, b2, time_w, w_qkv, w_out, w_up, w_down, chunk=512):
    seqs = timesteps.shape[0]
    n = tokens.shape[0]
    length = n // seqs
    feat, ff = time_w.shape[1], w_up.shape[1]
    count, chars = char.shape
    pair = 2 if seqs % 2 == 0 else 1
    items, width = seqs // pair, pair * length
    wide = ff // nz if nz else 512
    tiles, chunks = ff // wide, n // chunk
    share = ff // chunks
    heads = Heads(feat)
    call = Call()
    at_once = lambda value: (value, RESIDENT)
    call.arg(tok=at_once(tokens.reshape(seqs, 1, length)), steps=at_once(timesteps.reshape(1, seqs)), char=at_once(char),
             g1=at_once(g1.reshape(1, count)), b1=at_once(b1.reshape(1, count)), g2=at_once(g2.reshape(1, count)),
             b2=at_once(b2.reshape(1, count)), time_w=at_once(time_w), w_qkv=at_once(w_qkv), w_out=at_once(w_out), w_up=at_once(w_up),
             w_down=at_once(w_down), cot=(cotangent, ANYWHERE))
    call.out(start_o=((feat, n), F32, ANYWHERE), mixed_o=((feat, n), BF16, ANYWHERE), project_o=((3 * feat, n), BF16, ANYWHERE),
             powers_o=((seqs, HEADS, length, length), BF16, ANYWHERE), inv=((seqs, HEADS, length), F32, RESIDENT),
             waves=((feat, 128), BF16, RESIDENT), grad_o=((feat, n), F32, ANYWHERE), ln=((2, feat, 128), F32, RESIDENT),
             d_down_o=((ff, feat), BF16, ANYWHERE), middle_o=((feat, n), F32, ANYWHERE), act_o=((ff, n), BF16, ANYWHERE),
             down_o=((feat, ff), BF16, ANYWHERE))
    parts = 3
    vmem = lambda kind, *shape: pltpu.VMEM(shape, kind)
    if nz:
        per = feat // (nz * 8)
        blocks = lambda *tail: (nz,) + BLOCKS + tail
        landing = lambda *tail: vmem(BF16, *blocks(*tail))
        sems = Gather.scratch(nz)
        call.temp(first=landing(count, 128 + feat), first_sems=sems, out=landing(count, feat), out_sems=sems,
                  qkv=[landing(count, feat)] * parts, qkv_sems=[sems] * parts, ups=[landing(count, wide)] * tiles, up_sems=[sems] * tiles,
                  down=landing(*w_down.shape), down_sems=GatherLayers.scratch(nz), first_shard=vmem(BF16, count, 128 + feat),
                  mine=[landing(per, wide)] * tiles, sums=Scatter.scratch(nz, (per, wide)) * tiles)
        call.out(first_o=(blocks(count, 128 + feat), BF16, ANYWHERE), out_o=(blocks(count, feat), BF16, ANYWHERE),
                 qkv_o=(blocks(*w_qkv.shape), BF16, ANYWHERE), o_up=((per, ff), F32, RESIDENT))
    else:
        call.out(small=((count, 128), BF16, RESIDENT), d_up=((feat, ff), BF16, RESIDENT))
    call.temp(small_shard=vmem(BF16, count, 128), square=vmem(F32, 128, max(count, 128)), steps_row=vmem(F32, 1, 128),
              table=vmem(BF16, feat, 128), out_t=vmem(BF16, feat, feat), starts=vmem(F32, feat, n), mixed=vmem(BF16, feat, n),
              powers=[vmem(BF16, pair, HEADS, length, length)] * 2, scores=vmem(F32, pair * HEADS, length, length),
              middle=vmem(F32, feat, n), low2=vmem(BF16, feat, n), cot_t=vmem(BF16, max(n, ff), feat), cot_f=vmem(BF16, feat, n),
              down_t=vmem(BF16, feat, ff), up=vmem(BF16, feat, ff), up_t=vmem(BF16, wide, feat),
              act=vmem(BF16, ff, n), gh=vmem(BF16, ff, n), gn=[vmem(F32, feat, chunk)] * 2,
              sems=pltpu.SemaphoreType.DMA((24,)))

    def kernel(r):
        proj, low = r.act.at[pl.ds(0, 3 * feat)], r.gh.at[pl.ds(0, feat)]
        stream = Stream(r.sems)
        if nz:
            z, x, y, c = place()
            first = Gather(nz, r.first_shard, r.first, r.first_sems)
            qkv = [Gather(nz, r.w_qkv.at[:, pl.ds(p * feat, feat)], r.qkv[p], r.qkv_sems[p]) for p in range(parts)]
            out = Gather(nz, r.w_out, r.out, r.out_sems)
            ups = [Gather(nz, r.w_up.at[:, pl.ds(j * wide, wide)], r.ups[j], r.up_sems[j]) for j in range(tiles)]
            down = GatherLayers(nz, r.w_down, r.down, r.down_sems)
            needs = [(ups[j], down.layer(j)) for j in range(tiles)]
            order = [ups[0], ups[1], needs[0][1], needs[1][1]] + [part for some in needs[2:] for part in some]
            groups = [Scatter(nz, r.mine[j], r.sums[5 * j:5 * j + 5]) for j in range(tiles)]

        def small():
            return flat(r.first, slice(0, 128)) if nz else r.small[...]

        def stamps(weights):
            stamp = dot(weights.T, r.waves[...])
            lane = lax.broadcasted_iota(jnp.int32, stamp.shape, 1)
            stamp = jnp.where(lane < seqs, stamp, 0.0)
            high = stamp.astype(BF16)
            rest = (stamp - high.astype(F32)).astype(BF16)
            shift = lambda value, by: jnp.concatenate([value[:, 128 - by:], value[:, :128 - by]], axis=1)
            chars_only = jnp.where(lane < chars, small(), jnp.zeros_like(high))
            r.table[...] = chars_only + shift(high, ITEM_HIGH) + shift(rest, ITEM_LOW)

        def begin(some):
            table = small()
            gain, bias = param(table, chars), param(table, chars + 1)
            for k in some:
                cols = pl.ds(k * length, length)
                start = dot(r.table[...], one_hot_of(r.tok[k], k))
                r.starts[:, cols] = start
                normed, _ = norm_rows(start)
                low[:, cols] = (normed * gain + bias).astype(BF16)

        def multiply(p, weights):
            proj[p * feat:(p + 1) * feat] = dot(weights.T, low[...]).astype(BF16)

        def keep():
            stream.start(0, proj, r.project_o)
            stream.start(1, r.starts, r.start_o)

        def prelude():
            stream.start(2, r.cot, r.cot_t.at[pl.ds(0, n)])
            r.ln[...] = jnp.zeros_like(r.ln)
            if not nz:
                fill_small(r, chars)
                r.small[...] = r.small_shard[...]
                fill_waves(r, feat)
                stamps(r.time_w[...])
                r.out_t[...] = r.w_out[...].T
                begin(range(seqs))
                for p in range(parts):
                    multiply(p, r.w_qkv[:, p * feat:(p + 1) * feat])
                keep()
                return
            greet(nz)
            fill_small(r, chars)
            q, k, v = qkv
            r.first_shard[:, :128] = r.small_shard[...]
            r.first_shard[:, 128:] = r.time_w[...]
            for g in (first, out, q, k, v, *ups, down):
                g.out[z, x, y, c] = g.shard[...]
            greeted(nz)
            first.lines()
            q.lines()
            k.lines()
            fill_waves(r, feat)
            first.sides()
            v.lines()
            q.sides()
            out.lines()
            k.sides()
            ups[0].lines()
            first.corners()
            v.sides()
            ups[1].lines()
            q.corners()
            down.lines()
            first.cores()
            k.corners()
            out.sides()
            first.whole()
            stamps(flat(r.first, slice(128, 128 + feat)))
            begin(range(0, seqs // 2))
            q.cores()
            v.corners()
            ups[0].sides()
            begin(range(seqs // 2, seqs))
            k.cores()
            out.corners()
            q.whole()
            multiply(0, flat(r.qkv[0]))
            v.cores()
            ups[1].sides()
            for g in ups[2:]:
                g.lines()
            k.whole()
            multiply(1, flat(r.qkv[1]))
            out.cores()
            down.arrived()
            needs[0][1].sides()
            v.whole()
            multiply(2, flat(r.qkv[2]))
            ups[0].corners()
            keep()

        def heads_of(i, k):
            cols = pl.ds((i * pair + k) * length, length)
            return proj.at[:, cols], r.scores.at[pl.ds(k * HEADS, HEADS)], r.powers[i % 2].at[k], r.inv.at[i * pair + k], r.mixed.at[:, cols]

        def after_heads(i):
            cols = pl.ds(i * width, width)
            table = small()
            middle = r.starts[:, cols] + dot(r.out_t[...], r.mixed[:, cols])
            r.middle[:, cols] = middle
            normed, _ = norm_rows(middle)
            r.low2[:, cols] = (normed * param(table, chars + 2) + param(table, chars + 3)).astype(BF16)
            r.cot_f[:, cols] = r.cot_t[cols, :].T

        def weights_step(step):
            if not nz:
                return
            for part in order[max(2 * step - 2, 0):2 * step]:
                part.cores()
            for part in order[max(2 * step, 1):2 * step + 2]:
                part.corners()
            for part in order[2 * step + 4 if step else 3:2 * step + 6]:
                part.sides()

        def sums_step(step):
            if not nz:
                return
            for j, g in enumerate(groups):
                stage = step - j - 1
                if 0 <= stage < 3:
                    (g.corners, g.sides, g.lines)[stage]()

        def layer_back(m):
            cols = pl.ds(m * chunk, chunk)
            normed, inverse = norm_rows(r.middle[:, cols])
            grad_normed = r.gn[m % 2][...]
            grad = r.cot_f[:, cols].astype(F32) + norm_rows_back(grad_normed, param(small(), chars + 2), normed, inverse)
            r.starts[:, cols] = grad
            r.ln[0] += fold(grad_normed * normed)
            r.ln[1] += fold(grad_normed)
            stream.start(10 + m, r.starts.at[:, cols], r.grad_o.at[:, cols])

        prelude()
        for i in range(items):
            stream.wait(3 + i % 2)
            views = [heads_of(i, k) for k in range(pair)]
            for project, scores, *_ in views:
                heads.scores(project, scores)
            if i == 1:
                if nz:
                    out.whole()
                    r.out_t[...] = flat(r.out).T
                    every = (pl.ds(0, nz), slice(None), slice(None), slice(None), slice(None))
                    for p, g in enumerate(qkv):
                        stream.start(5 + p, g.out, r.qkv_o.at[every + (pl.ds(p * feat, feat),)])
                    stream.start(8, r.first, r.first_o)
                    stream.start(9, r.out, r.out_o)
                stream.wait(2)
            if i > 0:
                after_heads(i - 1)
            for project, scores, powers, inverses, mixed in views:
                heads.softmax(scores, powers, inverses)
                heads.mix(project, powers, inverses, mixed)
            stream.start(3 + i % 2, r.powers[i % 2], r.powers_o.at[pl.ds(i * pair, pair)])
            weights_step(i)
        after_heads(items - 1)
        stream.wait(0)
        stream.wait(1)
        stream.start(0, r.mixed, r.mixed_o)
        stream.start(1, r.middle, r.middle_o)
        for j in range(tiles):
            rows = pl.ds(j * wide, wide)
            if nz:
                for part in needs[j]:
                    part.whole()
                r.up[:, rows] = flat(r.ups[j])
                tile_down = flat(r.down.at[pl.ds(j, 1)])
            else:
                r.up[:, rows] = r.w_up[:, rows]
                tile_down = r.w_down[rows, :]
            r.up_t[...] = r.up[:, rows].T
            r.down_t[:, rows] = tile_down.T
            for t in range(chunks):
                cols = pl.ds(t * chunk, chunk)
                for half in range(2):
                    some = slice(half * wide // 2, (half + 1) * wide // 2)
                    part = pl.ds(j * wide + half * (wide // 2), wide // 2)
                    r.act[part, cols], r.gh[part, cols] = gelu_parts(
                        dot(r.up_t[some, :], r.low2[:, cols]), dot(tile_down[some], r.cot_f[:, cols]))
            weights_step(items + j)
            sums_step(j)
            d_up = dot_nt(r.low2[...], r.gh[rows, :]).astype(BF16)
            if nz:
                r.mine[j][...] = d_up.reshape(blocks(per, wide))
                groups[j].cores()
            else:
                r.d_up[:, rows] = d_up
        stream.start(14, r.act, r.act_o)
        stream.start(15, r.down_t, r.down_o)
        for m in range(chunks):
            cols, rows = pl.ds(m * chunk, chunk), pl.ds(m * share, share)
            r.gn[m % 2][...] = dot(r.up[...], r.gh[:, cols])
            if m > 0:
                layer_back(m - 1)
            r.cot_t[rows, :] = dot_nt(r.act[rows, :], r.cot_f[...]).astype(BF16)
            sums_step(tiles + m)
            stream.start(16 + m, r.cot_t.at[rows], r.d_down_o.at[rows])
        layer_back(chunks - 1)
        if nz:
            for g in (first, *qkv, out, *ups, down):
                g.finish()
            for j in range(tiles):
                r.o_up[:, j * wide:(j + 1) * wide] = groups[j].total()
        stream.close()

    return call.run(kernel, "forward_and_ffn", None, 0 if nz else None)


def backward(nz, chars, tokens, small, w_qkv, w_out, saved, chunk=512):
    feat, n = saved.start_o.shape
    seqs = saved.powers_o.shape[0]
    ff = saved.act_o.shape[0]
    length = n // seqs
    pair = 2 if seqs % 2 == 0 else 1
    items, width, chunks = seqs // pair, pair * length, n // chunk
    heads = Heads(feat)
    vmem = lambda kind, *shape: pltpu.VMEM(shape, kind)
    there = lambda value: (value, ANYWHERE)
    call = Call()
    call.arg(tok=(tokens.reshape(seqs, 1, length), RESIDENT), waves=(saved.waves, RESIDENT), inv=(saved.inv, RESIDENT), small_i=there(small),
             qkv_i=there(w_qkv), out_i=there(w_out), start_i=there(saved.start_o), grad_i=there(saved.grad_o), project_i=there(saved.project_o),
             powers_i=there(saved.powers_o), mixed_i=there(saved.mixed_o), ln2_i=there(saved.ln),
             middle_i=there(saved.middle_o), act_i=there(saved.act_o), down_i=there(saved.down_o))
    call.out(d_in=((feat, n), F32, ANYWHERE), result=((feat, n), F32, ANYWHERE))
    call.temp(small=vmem(BF16, feat, 128), qkv=vmem(BF16, feat, 3 * feat), w_out=vmem(BF16, feat, feat), start=vmem(F32, feat, n),
              grad=vmem(F32, feat, n), project=[vmem(BF16, 3 * feat, width)] * 2, powers=[vmem(BF16, pair, HEADS, length, length)] * 2,
              mixed=vmem(BF16, feat, n), ln2=vmem(F32, 2, feat, 128), middle=vmem(F32, feat, n), act=[vmem(BF16, ff, chunk)] * 2,
              down_t=vmem(BF16, feat, ff), ln1=vmem(F32, 2, feat, 128), d_char=vmem(F32, feat, 128), low_f=vmem(BF16, feat, n),
              gp_f=vmem(BF16, 3 * feat, n), ga_f=vmem(BF16, feat, n), scores=vmem(F32, pair * HEADS, length, length),
              grads=vmem(BF16, pair * HEADS, length, length), grad_mixed=vmem(F32, feat, width), scaled=vmem(BF16, feat, width),
              lean=vmem(F32, seqs, HEADS, length), gn=[vmem(F32, feat, width)] * 2, sems=pltpu.SemaphoreType.DMA((40,)))
    parts = 4
    if nz:
        devices = nz * 8
        per, down_per = feat // devices, ff // devices
        blocks = (nz,) + BLOCKS
        call.arg(d_down=there(saved.d_down_o.reshape(blocks + (down_per, feat))))
        small_out = lambda *shape: (shape, F32, RESIDENT)
        call.out(o_out=small_out(per, feat), o_down=small_out(down_per, feat), o_qkv=small_out(per, 3 * feat), o_time=small_out(per, feat),
                 o_char=small_out(per, chars), o_ln=small_out(4, per))
        call.temp(down_sums=Scatter.scratch(nz, (down_per, feat)), rest_sums=Scatter.scratch(nz, (per, 128 + feat)),
                  at_sums=Scatter.scratch(nz, (per, feat)) * parts, kept=vmem(BF16, nz, 2, 2, down_per, feat),
                  d_at=[vmem(BF16, *blocks, per, feat)] * parts, d_rest=vmem(BF16, *blocks, per, 128 + feat))
    else:
        call.out(d_at=((feat, 4 * feat), BF16, RESIDENT), d_rest=((feat, 128 + feat), BF16, RESIDENT))

    def kernel(r):
        stream = Stream(r.sems)
        if nz:
            c = place()[3]
            down = Scatter(nz, r.d_down, r.down_sums, r.kept)
            ats = [Scatter(nz, r.d_at[p], r.at_sums[5 * p:5 * p + 5]) for p in range(parts)]
            rest = Scatter(nz, r.d_rest, r.rest_sums)

        def tall(value):
            value = value.astype(BF16)
            return value.reshape(blocks + (per, value.shape[-1])) if nz else value

        def columns(i):
            return pl.ds(i * width, width)

        def fetch_item(i):
            stream.start(9 + i, r.grad_i.at[:, columns(i)], r.grad.at[:, columns(i)])
            if i == 0:
                stream.start(2, r.small_i.at[:, pl.ds(0, 128)], r.small)
            stream.start(13 + i, r.start_i.at[:, columns(i)], r.start.at[:, columns(i)])
            stream.start(29 + i, r.mixed_i.at[:, columns(i)], r.mixed.at[:, columns(i)])
            stream.start(17 + i % 2, r.project_i.at[:, columns(i)], r.project[i % 2])
            stream.start(19 + i % 2, r.powers_i.at[pl.ds(i * pair, pair)], r.powers[i % 2])

        def fetch_chunk(m):
            stream.start(6 + 2 * (m % 2), r.act_i.at[:, pl.ds(m * chunk, chunk)], r.act[m % 2])

        def norm_again(i):
            normed, _ = norm_rows(r.start[:, columns(i)])
            r.low_f[:, columns(i)] = (normed * param(r.small[...], chars) + param(r.small[...], chars + 1)).astype(BF16)

        def products():
            pairs = [(r.mixed, r.ga_f)] + [(r.low_f, r.gp_f.at[pl.ds(p * feat, feat)]) for p in range(3)]
            for p, (left, right) in enumerate(pairs):
                product = tall(dot_nt(left[...], right[...]))
                if nz:
                    r.d_at[p][...] = product
                    ats[p].cores()
                    if p > 0:
                        ats[p - 1].corners()
                else:
                    r.d_at[:, p * feat:(p + 1) * feat] = product

        def layer_back(i):
            grad_normed = r.gn[i % 2][...]
            normed, inverse = norm_rows(r.start[:, columns(i)])
            d_in = r.grad[:, columns(i)] + norm_rows_back(grad_normed, param(r.small[...], chars), normed, inverse)
            r.start[:, columns(i)] = d_in
            stream.start(21 + i, r.start.at[:, columns(i)], r.d_in.at[:, columns(i)])
            r.ln1[0] += fold(grad_normed * normed)
            r.ln1[1] += fold(grad_normed)
            one_hot = jnp.concatenate([one_hot_of(r.tok[i * pair + k], i * pair + k) for k in range(pair)], axis=1)
            high = d_in.astype(BF16)
            low = (d_in - high.astype(F32)).astype(BF16)
            r.d_char[...] += dot_nt(high, one_hot) + dot_nt(low, one_hot)

        def rest_products():
            lane = lax.broadcasted_iota(jnp.int32, r.d_char.shape, 1)
            sums = r.d_char[...]
            table = jnp.where(lane < chars, sums, 0.0)
            for k, ref in enumerate((r.ln1.at[0], r.ln1.at[1], r.ln2.at[0], r.ln2.at[1])):
                table = jnp.where(lane == chars + k, jnp.sum(ref[...], axis=1, keepdims=True), table)
            stamps = jnp.concatenate([sums[:, ITEM_HIGH:], sums[:, :ITEM_HIGH]], axis=1)
            stamps = jnp.where(lane < seqs, stamps, 0.0).astype(BF16)
            r.d_rest[..., :128] = tall(table)
            r.d_rest[..., 128:] = tall(dot_nt(r.waves[...], stamps))

        def result(m):
            cols = pl.ds(m * chunk, chunk)
            stream.wait(6 + 2 * (m % 2))
            r.middle[:, cols] = r.middle[:, cols] + dot(r.down_t[...], r.act[m % 2][...])
            stream.start(25 + m, r.middle.at[:, cols], r.result.at[:, cols])
            if m + 2 < chunks:
                fetch_chunk(m + 2)

        if nz:
            greet(nz)
        stream.start(0, r.out_i, r.w_out)
        fetch_item(0)
        r.ln1[...] = jnp.zeros_like(r.ln1)
        r.d_char[...] = jnp.zeros_like(r.d_char)
        for i in range(items):
            stream.wait(0)
            stream.wait(9 + i)
            if nz and i == 1:
                greeted(nz)
                down.cores()
            if nz and i == 2:
                stream.wait(5)
                down.corners()
            grad_low = r.grad[:, columns(i)].astype(BF16)
            r.ga_f[:, columns(i)] = grad_low
            r.grad_mixed[...] = dot(r.w_out[...], grad_low).astype(BF16).astype(F32)
            stream.wait(2)
            stream.wait(13 + i)
            norm_again(i)
            for number in (29 + i, 17 + i % 2, 19 + i % 2):
                stream.wait(number)
            if i + 1 < items:
                fetch_item(i + 1)
            if i == 0:
                stream.start(3, r.qkv_i, r.qkv)
                stream.start(4, r.ln2_i, r.ln2)
                if nz:
                    stream.start(5, r.d_down.at[pl.ds(0, nz), :, :, c], r.kept)
            views = []
            for k in range(pair):
                here, item = pl.ds(k * length, length), i * pair + k
                cols, group = pl.ds(item * length, length), pl.ds(k * HEADS, HEADS)
                views.append((r.project[i % 2].at[:, here], r.scaled.at[:, here], r.powers[i % 2].at[k], r.scores.at[group], r.grads.at[group], cols))
                heads.scale_grad(r.grad_mixed.at[:, here], r.inv.at[item], r.mixed.at[:, cols], r.scaled.at[:, here], r.lean.at[item])
            for k, (project, scaled, powers, scores, grads, cols) in enumerate(views):
                heads.grad_probs(project, scaled, scores)
            for k, (project, scaled, powers, scores, grads, cols) in enumerate(views):
                heads.grad_scores(powers, scores, r.lean.at[i * pair + k], grads)
                heads.grad_project(project, scaled, powers, grads, r.gp_f, cols)
        stream.start(7, r.middle_i, r.middle)
        stream.start(5, r.down_i, r.down_t)
        for m in range(2):
            fetch_chunk(m)
        if nz:
            down.sides()
        stream.wait(3)
        products()
        for i in range(items):
            r.gn[i % 2][...] = dot(r.qkv[...], r.gp_f[:, columns(i)])
            if i > 0:
                layer_back(i - 1)
            if nz:
                if i == 0:
                    ats[3].corners()
                if i == 1:
                    ats[0].sides()
                    ats[1].sides()
                    down.lines()
                if i == 2:
                    ats[2].sides()
                    ats[3].sides()
                if i == 3:
                    ats[0].lines()
                    ats[1].lines()
        layer_back(items - 1)
        stream.wait(4)
        rest_products()
        stream.wait(7)
        stream.wait(5)
        if not nz:
            for m in range(chunks):
                result(m)
        else:
            rest.cores()
            ats[2].lines()
            ats[3].lines()
            result(0)
            rest.corners()
            for m in range(1, chunks - 1):
                result(m)
            rest.sides()
            result(chunks - 1)
            r.o_down[...] = down.total()
            r.o_out[...] = ats[0].total()
            for p in range(3):
                r.o_qkv[:, p * feat:(p + 1) * feat] = ats[1 + p].total()
            rest.lines()
            total = rest.total()
            r.o_time[...] = total[:, 128:]
            r.o_char[...] = total[:, :chars]
            r.o_ln[...] = total[:, :128].T[chars:chars + 4]
        stream.close()

    return call.run(kernel, "backward", None, 1 if nz else None)


def hand_over(result, d_in, ln, *others, width=1024):
    feat, n = d_in.shape
    call = Call()
    turned = ((n, feat), F32, pl.BlockSpec((width, feat), lambda i: (i, 0)))
    call.arg(result=(result, lanes(feat, width)), d_in=(d_in, lanes(feat, width)), ln=(ln, whole(ln.shape)))
    call.arg(**{f"a{k}": (value, whole(value.shape)) for k, value in enumerate(others)})
    call.out(o_result=turned, o_d_in=turned, **{f"l{k}": ((1, ln.shape[1]), F32, whole((1, ln.shape[1]))) for k in range(4)})
    call.out(**{f"o{k}": (value.shape, F32, whole(value.shape)) for k, value in enumerate(others)})

    def kernel(r):
        r.o_result[...] = r.result[...].T
        r.o_d_in[...] = r.d_in[...].T

        @pl.when(pl.program_id(0) == 0)
        def _():
            for k, ref in enumerate((r.l0, r.l1, r.l2, r.l3)):
                ref[...] = r.ln[k:k + 1]
            for k in range(len(others)):
                getattr(r, f"o{k}")[...] = getattr(r, f"a{k}")[...]

    got = call.run(kernel, "hand_over", n // width)
    return got.o_result, got.o_d_in, [getattr(got, f"l{k}") for k in range(4)], [getattr(got, f"o{k}") for k in range(len(others))]


def make_body(gx, gy):
    def gathered(*shards):
        return [lax.all_gather(s, AXES, axis=0, tiled=True) for s in shards]

    def summed(part):
        return lax.psum_scatter(part.astype(F32), AXES, scatter_dimension=0, tiled=True)

    def body(tokens, timesteps, cotangent, char_table, time_weight, ln1_gain, ln1_bias, w_qkv, w_attn_out, ln2_gain, ln2_bias, w_up, w_down):
        feat = time_weight.shape[1]
        chars = char_table.shape[0]
        per = feat // (gx * gy)
        nz = gx // 2 if gy == 4 and gx % 8 == 0 and per % 16 == 0 else 0
        shards = [char_table.T, ln1_gain, ln1_bias, ln2_gain, ln2_bias, time_weight, w_qkv, w_attn_out, w_up, w_down]
        if not nz:
            shards = gathered(*shards)
        saved = forward(nz, tokens, timesteps, cotangent, *shards)
        if nz:
            small, w_qkv, w_out = (value.reshape(feat, value.shape[-1]) for value in (saved.first_o, saved.qkv_o, saved.out_o))
            got = backward(nz, chars, tokens, small, w_qkv, w_out, saved)
            ln, sums = got.o_ln, (got.o_char, got.o_time, got.o_qkv, got.o_out, saved.o_up, got.o_down)
        else:
            got = backward(nz, chars, tokens, saved.small, *shards[6:8], saved)
            up, down, at, rest = (summed(p) for p in (saved.d_up, saved.d_down_o, got.d_at, got.d_rest))
            ln, sums = rest[:, chars:chars + 4].T, (rest[:, :chars], rest[:, 128:], at[:, feat:], at[:, :feat], up, down)
        result, d_in, lns, (char, time, qkv, out, up, down) = hand_over(got.result, got.d_in, ln, *sums)
        g1, b1, g2, b2 = (value.reshape(per) for value in lns)
        return result, d_in, char.T, time, g1, b1, qkv, out, g2, b2, up, down
    return body


def solution(mesh):
    every = P(AXES)
    rows, cols = P(AXES, None), P(None, AXES)
    return jax.shard_map(
        make_body(mesh.shape[AXES[0]], mesh.shape[AXES[1]]),
        mesh=mesh,
        in_specs=(every, every, rows, cols, rows, every, every, rows, rows, every, every, rows, rows),
        out_specs=(rows, rows, cols, rows, every, every, rows, rows, every, every, rows, rows),
        check_vma=False,
    )
```

```python
import math
import types

import jax
import jax.numpy as jnp
from jax import lax
from jax.experimental import pallas as pl
from jax.experimental.pallas import tpu as pltpu
from jax.sharding import PartitionSpec as P

F32, BF16 = jnp.float32, jnp.bfloat16
MESH = pl.DeviceIdType.MESH
AXES = ("gx", "gy")
HEADS = 8
EPSILON = 1e-05
VMEM_LIMIT = 63 * 2**20
BLOCKS = (2, 2, 2)
X, Y, CORE = range(3)


def place():
    gx, gy = lax.axis_index(AXES[0]), lax.axis_index(AXES[1])
    return gx // 2, gx % 2, gy // 2, gy % 2


def device(z, x, y, c):
    return (z * 2 + x, y * 2 + c)


def across(axis):
    z, x, y, c = place()
    return ((z, 1 - x, y, c), (z, x, 1 - y, c), (z, x, y, 1 - c))[axis]


def greet(nz):
    z, x, y, c = place()
    barrier = pltpu.get_barrier_semaphore()
    for where in [across(axis) for axis in (X, Y, CORE)] + [((z + d) % nz, x, y, c) for d in range(1, nz)]:
        pl.semaphore_signal(barrier, inc=1, device_id=device(*where), device_id_type=MESH)


def greeted(nz):
    pl.semaphore_wait(pltpu.get_barrier_semaphore(), 3 + nz - 1)


def halves(width):
    middle = width // 256 * 128
    return pl.ds(0, middle), pl.ds(middle, width - middle)


def blocks_of(out, number):
    if number % 4:
        return out.at[pl.ds(0, number), 0, 0, 0]
    return out.at[pl.ds(0, number // 4), :, :, 0]


class Gather:
    LINES, SIDES, CORNERS, CORES = range(4)

    @staticmethod
    def scratch(nz):
        return pltpu.SemaphoreType.DMA((2, 4))

    def __init__(self, nz, shard, out, sems):
        self.nz, self.shard, self.out, self.sems = nz, shard, out, sems
        self.zs, self.count, self.base, self.waits = pl.ds(0, nz), nz, 0, True

    def send(self, src, dst, sent, came, where):
        return pltpu.make_async_remote_copy(
            src_ref=src, dst_ref=dst, send_sem=self.sems.at[0, sent + (self.base if sent else 0)],
            recv_sem=self.sems.at[1, came + (self.base if came else 0)], device_id=device(*where), device_id_type=MESH)

    def some(self, number, stage):
        ref = blocks_of(self.out, number)
        return self.send(ref, ref, stage, stage, across(CORE))

    def pass_on(self, axis, a, b, sent, came, cut=None):
        c = place()[3]
        ref = self.out.at[self.zs, a, b, c]
        if cut is not None:
            ref = ref.at[:, :, cut]
        self.send(ref, ref, sent, came, across(axis)).start()

    def lines(self):
        z, x, y, c = place()
        for d in range(1, self.nz):
            self.send(self.shard, self.out.at[z, x, y, c], self.LINES, self.LINES, ((z + d) % self.nz, x, y, c)).start()

    def arrived(self):
        self.some(self.nz - 1, self.LINES).wait_recv()

    def sides(self):
        _, x, y, _ = place()
        if self.waits:
            self.arrived()
        self.pass_on(X, x, y, self.SIDES, self.SIDES)
        self.pass_on(Y, x, y, self.SIDES, self.SIDES)
        self.pass_on(CORE, x, y, self.SIDES, self.CORES)

    def corners(self):
        _, x, y, _ = place()
        lo, hi = halves(self.out.shape[-1])
        self.some(2 * self.count, self.SIDES).wait_recv()
        self.pass_on(X, x, 1 - y, self.CORNERS, self.CORNERS, lo)
        self.pass_on(Y, 1 - x, y, self.CORNERS, self.CORNERS, hi)
        self.pass_on(CORE, 1 - x, y, self.CORNERS, self.CORES)
        self.pass_on(CORE, x, 1 - y, self.CORNERS, self.CORES)

    def cores(self):
        _, x, y, _ = place()
        self.some(self.count, self.CORNERS).wait_recv()
        self.pass_on(CORE, 1 - x, 1 - y, self.CORES, self.CORES)

    def whole(self):
        self.some(4 * self.count, self.CORES).wait_recv()

    def sent(self):
        self.some(3 * self.count, self.SIDES).wait_send()
        self.some(3 * self.count, self.CORNERS).wait_send()
        self.some(self.count, self.CORES).wait_send()

    def finish(self):
        self.some(self.nz - 1, self.LINES).wait_send()
        self.sent()


class GatherLayers(Gather):
    @staticmethod
    def scratch(nz):
        return pltpu.SemaphoreType.DMA((2, 1 + 3 * nz))

    def layer(self, j):
        one = Gather(self.nz, self.shard, self.out, self.sems)
        one.zs, one.count, one.base, one.waits = pl.ds(j, 1), 1, 3 * j, False
        return one

    def sent(self):
        for j in range(self.nz):
            self.layer(j).sent()


class Scatter:
    @staticmethod
    def scratch(nz, tail):
        return [pltpu.VMEM((nz, 2, 2) + tail, BF16), pltpu.VMEM((nz,) + tail, BF16), pltpu.VMEM((2, nz) + tail, BF16),
                pltpu.VMEM((nz - 1,) + tail, BF16), pltpu.SemaphoreType.DMA((2, 4))]

    def __init__(self, nz, mine, temps, kept=None):
        self.nz, self.mine, self.kept = nz, mine, kept
        self.own, self.far, self.near, self.line, self.sems = temps
        self.width = self.own.shape[-1]

    def send(self, src, dst, stage, where):
        return pltpu.make_async_remote_copy(
            src_ref=src, dst_ref=dst, send_sem=self.sems.at[0, stage], recv_sem=self.sems.at[1, stage],
            device_id=device(*where), device_id_type=MESH)

    def done(self, ref, stage):
        self.send(ref, ref, stage, across(CORE)).wait()

    def add(self, a, b, cols, *values):
        spot = (slice(None), a, b, slice(None), cols)
        total = self.own[spot]
        for value in values:
            total = total + value
        self.own[spot] = total

    def cores(self):
        c = place()[3]
        self.send(self.mine.at[pl.ds(0, self.nz), :, :, 1 - c], self.own, 0, across(CORE)).start()

    def corners(self):
        _, x, y, c = place()
        every, all_z = pl.ds(0, self.width), pl.ds(0, self.nz)
        lo, hi = halves(self.width)
        self.done(self.own, 0)
        for number, (a, b) in enumerate(((1 - x, 1 - y), (1 - x, y), (x, 1 - y), (x, y))):
            self.add(a, b, every, self.mine[:, a, b, c] if self.kept is None else self.kept[:, a, b])
            if number == 0:
                self.send(self.own.at[all_z, 1 - x, 1 - y, :, lo], self.far.at[:, :, lo], 1, across(X)).start()
                self.send(self.own.at[all_z, 1 - x, 1 - y, :, hi], self.far.at[:, :, hi], 1, across(Y)).start()

    def sides(self):
        _, x, y, _ = place()
        all_z = pl.ds(0, self.nz)
        lo, hi = halves(self.width)
        self.done(self.far, 1)
        self.add(x, 1 - y, lo, self.far[:, :, lo])
        self.send(self.own.at[all_z, x, 1 - y], self.near.at[1], 2, across(Y)).start()
        self.add(1 - x, y, hi, self.far[:, :, hi])
        self.send(self.own.at[all_z, 1 - x, y], self.near.at[0], 2, across(X)).start()

    def lines(self):
        z, x, y, c = place()
        self.done(self.near, 2)
        self.add(x, y, pl.ds(0, self.width), self.near[0], self.near[1])
        for d in range(1, self.nz):
            to = (z + d) % self.nz
            self.send(self.own.at[to, x, y], self.line.at[d - 1], 3, (to, x, y, c)).start()

    def total(self):
        z, x, y, _ = place()
        self.done(self.line, 3)
        total = self.own[z, x, y].astype(F32)
        for d in range(1, self.nz):
            total = total + self.line[d - 1].astype(F32)
        return total


class Call:
    def __init__(self):
        self.ins, self.outs, self.temps = {}, {}, {}

    def arg(self, **named):
        self.ins.update(named)

    def out(self, **named):
        self.outs.update(named)

    def temp(self, **named):
        self.temps.update(named)

    def run(self, kernel, name, steps=None, collective=None):
        kinds = [k for kind in self.temps.values() for k in (kind if isinstance(kind, list) else [kind])]

        def body(*refs):
            refs = iter(refs)
            r = types.SimpleNamespace(**{n: next(refs) for n in [*self.ins, *self.outs]})
            for n, kind in self.temps.items():
                setattr(r, n, [next(refs) for _ in kind] if isinstance(kind, list) else next(refs))
            kernel(r)
        extra = {} if collective is None else dict(collective_id=collective, has_side_effects=True)
        got = pl.pallas_call(
            body, grid=() if steps is None else (steps,), in_specs=[spec for _, spec in self.ins.values()], out_specs=[spec for *_, spec in self.outs.values()],
            out_shape=[jax.ShapeDtypeStruct(shape, kind) for shape, kind, _ in self.outs.values()], scratch_shapes=kinds,
            compiler_params=pltpu.CompilerParams(vmem_limit_bytes=VMEM_LIMIT, **extra), name=name,
        )(*[array for array, _ in self.ins.values()])
        return types.SimpleNamespace(**dict(zip(self.outs, got)))


def whole(shape):
    return pl.BlockSpec(tuple(shape), lambda i: (0,) * len(shape))


def lanes(rows, width, at=lambda i: i):
    return pl.BlockSpec((rows, width), lambda i: (0, at(i)))


ANYWHERE = pl.BlockSpec(memory_space=pl.ANY)
RESIDENT = pl.BlockSpec(memory_space=pltpu.VMEM)


def at_step(i, table):
    for step, acts in enumerate(table):
        if acts:
            @pl.when(i == step)
            def _():
                for act in acts:
                    act()


def block_at(i, width):
    return pl.ds(pl.multiple_of(i * width, width), width)


def dot(left, right):
    return jnp.dot(left, right, preferred_element_type=F32)


def dot_nt(left, right):
    return lax.dot_general(left, right, (((1,), (1,)), ((), ())), preferred_element_type=F32)


def norm_rows(values):
    count = values.shape[0]
    shifted = values - jnp.sum(values, axis=0, keepdims=True) * (1.0 / count)
    inverse = lax.rsqrt(jnp.sum(shifted * shifted, axis=0, keepdims=True) * (1.0 / count) + EPSILON)
    return shifted * inverse, inverse


def norm_rows_back(grad, gain, normed, inverse):
    count = grad.shape[0]
    scaled = grad * gain
    lean = jnp.sum(scaled, axis=0, keepdims=True) * (1.0 / count)
    turn = jnp.sum(scaled * normed, axis=0, keepdims=True) * (1.0 / count)
    return inverse * (scaled - lean - normed * turn)


def fold(values):
    total = values[:, :128]
    for k in range(1, values.shape[1] // 128):
        total = total + values[:, 128 * k:128 * (k + 1)]
    return total


def flat(ref, cols=slice(None)):
    value = ref[(slice(None),) * (len(ref.shape) - 1) + (cols,)]
    return value.reshape(-1, value.shape[-1])


def param(table, column):
    return table[:, column:column + 1].astype(F32)


def gelu_parts(hidden, grad_active):
    cdf = 0.5 + 0.5 * lax.erf(hidden * math.sqrt(0.5))
    bell = jnp.exp2(hidden * hidden * (-0.5 * math.log2(math.e))) * (1.0 / math.sqrt(2.0 * math.pi))
    return (hidden * cdf).astype(BF16), (grad_active.astype(BF16).astype(F32) * (cdf + hidden * bell)).astype(BF16)


def fill_waves(r, feat):
    half = feat // 2
    r.steps_row[...] = jnp.zeros_like(r.steps_row)
    r.steps_row[:, :r.steps.shape[1]] = r.steps[...].astype(F32)
    rate = jnp.exp(lax.broadcasted_iota(jnp.int32, (half, 128), 0).astype(F32) * (-math.log(10000.0) / half))
    angles = rate * r.steps_row[...]
    r.waves[:half, :] = jnp.sin(angles).astype(BF16)
    r.waves[half:, :] = jnp.cos(angles).astype(BF16)


def fill_small(r, chars):
    count = r.char.shape[0]
    r.square[...] = jnp.zeros_like(r.square)
    for k, ref in enumerate((r.g1, r.b1, r.g2, r.b2)):
        r.square[chars + k:chars + k + 1, :count] = ref[...].astype(F32)
    r.small_shard[...] = r.square[...].T[:count].astype(BF16)
    r.small_shard[:, :chars] = r.char[...]


ITEM_HIGH, ITEM_LOW = 32, 64


def one_hot_of(tok, item):
    row = lax.broadcasted_iota(jnp.int32, (128, tok.shape[1]), 0)
    return ((row == tok) | (row == ITEM_HIGH + item) | (row == ITEM_LOW + item)).astype(BF16)


class Heads:
    def __init__(self, feat):
        self.size = feat // HEADS
        self.q, self.k, self.v = ([pl.ds(part * feat + h * self.size, self.size) for h in range(HEADS)] for part in range(3))

    def scores(self, project, scores):
        for h in range(HEADS):
            scores[h] = dot(project[self.k[h], :].T, project[self.q[h], :])

    def softmax(self, scores, powers, inverses):
        turn = math.log2(math.e) / math.sqrt(self.size)
        for h in range(HEADS):
            value = scores[h]
            power = jnp.exp2((value - jnp.max(value, axis=0, keepdims=True)) * turn)
            inverses[h:h + 1, :] = 1.0 / jnp.sum(power, axis=0, keepdims=True)
            powers[h] = power.astype(BF16)

    def mix(self, project, powers, inverses, mixed):
        for h in range(HEADS):
            mixed[self.q[h], :] = (dot(project[self.v[h], :], powers[h]) * inverses[h:h + 1, :]).astype(BF16)

    def scale_grad(self, grad_mixed, inverses, mixed, scaled, lean):
        for h in range(HEADS):
            value = grad_mixed[self.q[h], :] * inverses[h:h + 1, :]
            lean[h:h + 1, :] = jnp.sum(value * mixed[self.q[h], :].astype(F32), axis=0, keepdims=True)
            scaled[self.q[h], :] = value.astype(BF16)

    def grad_probs(self, project, scaled, scores):
        for h in range(HEADS):
            scores[h] = dot(project[self.v[h], :].T, scaled[self.q[h], :])

    def grad_scores(self, powers, scores, lean, grads):
        for h in range(HEADS):
            grads[h] = (powers[h].astype(F32) * (scores[h] - lean[h:h + 1, :])).astype(BF16)

    def grad_project(self, project, scaled, powers, grads, out, cols):
        scale = 1.0 / math.sqrt(self.size)
        for h in range(HEADS):
            out[self.v[h], cols] = dot_nt(scaled[self.q[h], :], powers[h]).astype(BF16)
            out[self.q[h], cols] = (dot(project[self.k[h], :], grads[h]) * scale).astype(BF16)
            out[self.k[h], cols] = (dot_nt(project[self.q[h], :], grads[h]) * scale).astype(BF16)


class Stream:
    def __init__(self, sems):
        self.sems = sems

    def start(self, number, src, dst):
        pltpu.make_async_copy(src, dst, self.sems.at[number]).start()

    def wait(self, number, src, dst):
        pltpu.make_async_copy(src, dst, self.sems.at[number]).wait()


def forward(nz, tokens, timesteps, cotangent, char, g1, b1, g2, b2, time_w, w_qkv, w_out, w_up, w_down, chunk=512):
    seqs = timesteps.shape[0]
    n = tokens.shape[0]
    length = n // seqs
    feat, ff = time_w.shape[1], w_up.shape[1]
    count, chars = char.shape
    pair = 2 if seqs % 2 == 0 else 1
    items, width = seqs // pair, pair * length
    wide = ff // nz if nz else 512
    tiles, chunks = ff // wide, n // chunk
    share = ff // chunks
    heads = Heads(feat)
    call = Call()
    at_once = lambda value: (value, RESIDENT)
    call.arg(tok=at_once(tokens.reshape(seqs, 1, length)), steps=at_once(timesteps.reshape(1, seqs)), char=at_once(char),
             g1=at_once(g1.reshape(1, count)), b1=at_once(b1.reshape(1, count)), g2=at_once(g2.reshape(1, count)),
             b2=at_once(b2.reshape(1, count)), time_w=at_once(time_w), w_qkv=at_once(w_qkv), w_out=at_once(w_out), w_up=at_once(w_up),
             w_down=at_once(w_down), cot=(cotangent, ANYWHERE))
    call.out(start_o=((feat, n), F32, ANYWHERE), mixed_o=((feat, n), BF16, ANYWHERE), project_o=((3 * feat, n), BF16, ANYWHERE),
             powers_o=((seqs, HEADS, length, length), BF16, ANYWHERE), inv=((seqs, HEADS, length), F32, RESIDENT),
             waves=((feat, 128), BF16, RESIDENT), grad_o=((feat, n), F32, ANYWHERE), ln=((2, feat, 128), F32, RESIDENT),
             d_down_o=((ff, feat), BF16, ANYWHERE), middle_o=((feat, n), F32, ANYWHERE), act_o=((ff, n), BF16, ANYWHERE),
             down_o=((feat, ff), BF16, ANYWHERE))
    parts = 3
    vmem = lambda kind, *shape: pltpu.VMEM(shape, kind)
    if nz:
        per = feat // (nz * 8)
        blocks = lambda *tail: (nz,) + BLOCKS + tail
        landing = lambda *tail: vmem(BF16, *blocks(*tail))
        sems = Gather.scratch(nz)
        call.temp(first=landing(count, 128 + feat), first_sems=sems, out=landing(count, feat), out_sems=sems,
                  qkv=[landing(count, feat)] * parts, qkv_sems=[sems] * parts, ups=vmem(BF16, tiles, *blocks(count, wide)), up_sems=[sems] * tiles,
                  down=landing(*w_down.shape), down_sems=GatherLayers.scratch(nz), first_shard=vmem(BF16, count, 128 + feat),
                  mine=vmem(BF16, tiles, *blocks(per, wide)), sums=Scatter.scratch(nz, (per, wide)) * tiles)
        call.out(first_o=(blocks(count, 128 + feat), BF16, ANYWHERE), out_o=(blocks(count, feat), BF16, ANYWHERE),
                 qkv_o=(blocks(*w_qkv.shape), BF16, ANYWHERE), o_up=((per, ff), F32, RESIDENT))
    else:
        call.out(small=((count, 128), BF16, RESIDENT), d_up=((feat, ff), BF16, RESIDENT))
    call.temp(small_shard=vmem(BF16, count, 128), square=vmem(F32, 128, max(count, 128)), steps_row=vmem(F32, 1, 128),
              table=vmem(BF16, feat, 128), out_t=vmem(BF16, feat, feat), starts=vmem(F32, feat, n), mixed=vmem(BF16, feat, n),
              powers=vmem(BF16, 2, pair, HEADS, length, length), scores=vmem(F32, pair * HEADS, length, length),
              middle=vmem(F32, feat, n), low2=vmem(BF16, feat, n), cot_t=vmem(BF16, max(n, ff), feat), cot_f=vmem(BF16, feat, n),
              down_t=vmem(BF16, feat, ff), up=vmem(BF16, feat, ff), up_t=vmem(BF16, wide, feat),
              act=vmem(BF16, ff, n), gh=vmem(BF16, ff, n), gn=vmem(F32, feat, chunk), tile_down=vmem(BF16, wide, feat),
              sems=pltpu.SemaphoreType.DMA((14 + 2 * chunks,)))

    def kernel(r):
        proj, low = r.act.at[pl.ds(0, 3 * feat)], r.gh.at[pl.ds(0, feat)]
        stream = Stream(r.sems)
        if nz:
            z, x, y, c = place()
            first = Gather(nz, r.first_shard, r.first, r.first_sems)
            qkv = [Gather(nz, r.w_qkv.at[:, pl.ds(p * feat, feat)], r.qkv[p], r.qkv_sems[p]) for p in range(parts)]
            out = Gather(nz, r.w_out, r.out, r.out_sems)
            ups = [Gather(nz, r.w_up.at[:, pl.ds(j * wide, wide)], r.ups.at[j], r.up_sems[j]) for j in range(tiles)]
            down = GatherLayers(nz, r.w_down, r.down, r.down_sems)
            needs = [(ups[j], down.layer(j)) for j in range(tiles)]
            order = [ups[0], ups[1], needs[0][1], needs[1][1]] + [part for some in needs[2:] for part in some]
            groups = [Scatter(nz, r.mine.at[j], r.sums[5 * j:5 * j + 5]) for j in range(tiles)]

        def small():
            return flat(r.first, slice(0, 128)) if nz else r.small[...]

        def stamps(weights):
            stamp = dot(weights.T, r.waves[...])
            lane = lax.broadcasted_iota(jnp.int32, stamp.shape, 1)
            stamp = jnp.where(lane < seqs, stamp, 0.0)
            high = stamp.astype(BF16)
            rest = (stamp - high.astype(F32)).astype(BF16)
            shift = lambda value, by: jnp.concatenate([value[:, 128 - by:], value[:, :128 - by]], axis=1)
            chars_only = jnp.where(lane < chars, small(), jnp.zeros_like(high))
            r.table[...] = chars_only + shift(high, ITEM_HIGH) + shift(rest, ITEM_LOW)

        def begin(some):
            table = small()
            gain, bias = param(table, chars), param(table, chars + 1)
            for k in some:
                cols = pl.ds(k * length, length)
                start = dot(r.table[...], one_hot_of(r.tok[k], k))
                r.starts[:, cols] = start
                normed, _ = norm_rows(start)
                low[:, cols] = (normed * gain + bias).astype(BF16)

        def multiply(p, weights):
            proj[p * feat:(p + 1) * feat] = dot(weights.T, low[...]).astype(BF16)

        to_hbm = [(proj, r.project_o), (r.starts, r.start_o), (r.mixed, r.mixed_o), (r.middle, r.middle_o), (r.act, r.act_o), (r.down_t, r.down_o)]
        if nz:
            every = (pl.ds(0, nz), slice(None), slice(None), slice(None), slice(None))
            to_hbm += [(r.first, r.first_o), (r.out, r.out_o)] + [(g.out, r.qkv_o.at[every + (pl.ds(p * feat, feat),)]) for p, g in enumerate(qkv)]
        cot_in = (11, r.cot, r.cot_t.at[pl.ds(0, n)])

        def leave(*numbers):
            for k in numbers:
                stream.start(k, *to_hbm[k])

        def left(*numbers):
            for k in numbers:
                stream.wait(k, *to_hbm[k])

        def powers_copy(i):
            return 12 + i % 2, r.powers.at[i % 2], r.powers_o.at[pl.ds(i * pair, pair)]

        def grad_copy(m):
            cols = block_at(m, chunk)
            return 14 + m, r.starts.at[:, cols], r.grad_o.at[:, cols]

        def d_down_copy(m):
            rows = block_at(m, share)
            return 14 + chunks + m, r.cot_t.at[rows], r.d_down_o.at[rows]

        def prelude():
            stream.start(*cot_in)
            r.ln[...] = jnp.zeros_like(r.ln)
            if not nz:
                fill_small(r, chars)
                r.small[...] = r.small_shard[...]
                fill_waves(r, feat)
                stamps(r.time_w[...])
                r.out_t[...] = r.w_out[...].T
                begin(range(seqs))
                for p in range(parts):
                    multiply(p, r.w_qkv[:, p * feat:(p + 1) * feat])
                leave(0, 1)
                return
            greet(nz)
            fill_small(r, chars)
            q, k, v = qkv
            r.first_shard[:, :128] = r.small_shard[...]
            r.first_shard[:, 128:] = r.time_w[...]
            for g in (first, out, q, k, v, *ups, down):
                g.out[z, x, y, c] = g.shard[...]
            greeted(nz)
            first.lines()
            q.lines()
            k.lines()
            fill_waves(r, feat)
            first.sides()
            v.lines()
            q.sides()
            out.lines()
            k.sides()
            ups[0].lines()
            first.corners()
            v.sides()
            ups[1].lines()
            q.corners()
            down.lines()
            first.cores()
            k.corners()
            out.sides()
            first.whole()
            stamps(flat(r.first, slice(128, 128 + feat)))
            begin(range(0, seqs // 2))
            q.cores()
            v.corners()
            ups[0].sides()
            begin(range(seqs // 2, seqs))
            k.cores()
            out.corners()
            q.whole()
            multiply(0, flat(r.qkv[0]))
            v.cores()
            ups[1].sides()
            for g in ups[2:]:
                g.lines()
            k.whole()
            multiply(1, flat(r.qkv[1]))
            out.cores()
            down.arrived()
            needs[0][1].sides()
            v.whole()
            multiply(2, flat(r.qkv[2]))
            ups[0].corners()
            out.whole()
            r.out_t[...] = flat(r.out).T
            leave(0, 1, *range(6, 8 + parts))

        def item(i):
            views = []
            for k in range(pair):
                cols = block_at(i * pair + k, length)
                views.append((proj.at[:, cols], r.scores.at[pl.ds(k * HEADS, HEADS)], r.powers.at[i % 2, k], r.inv.at[i * pair + k], r.mixed.at[:, cols]))
            for project, scores, *_ in views:
                heads.scores(project, scores)
            for project, scores, powers, inverses, mixed in views:
                heads.softmax(scores, powers, inverses)
                heads.mix(project, powers, inverses, mixed)
            stream.start(*powers_copy(i))
            cols = block_at(i, width)
            table = small()
            middle = r.starts[:, cols] + dot(r.out_t[...], r.mixed[:, cols])
            r.middle[:, cols] = middle
            normed, _ = norm_rows(middle)
            r.low2[:, cols] = (normed * param(table, chars + 2) + param(table, chars + 3)).astype(BF16)
            r.cot_f[:, cols] = r.cot_t[cols, :].T

        def weights_step(step):
            if not nz:
                return []
            acts = [part.cores for part in order[max(2 * step - 2, 0):2 * step]]
            acts += [part.corners for part in order[max(2 * step, 1):2 * step + 2]]
            return acts + [part.sides for part in order[2 * step + 4 if step else 3:2 * step + 6]]

        def sums_step(step):
            if not nz:
                return []
            return [(g.corners, g.sides, g.lines)[step - j - 1] for j, g in enumerate(groups) if 0 <= step - j - 1 < 3]

        def tile(j):
            rows = block_at(j, wide)
            if nz:
                at_step(j, [[part.whole for part in some] for some in needs])
                r.up[:, rows] = flat(r.ups.at[j])
                r.tile_down[...] = flat(r.down.at[pl.ds(j, 1)])
            else:
                r.up[:, rows] = r.w_up[:, rows]
                r.tile_down[...] = r.w_down[rows, :]
            r.up_t[...] = r.up[:, rows].T
            r.down_t[:, rows] = r.tile_down[...].T
            for t in range(chunks):
                cols = pl.ds(t * chunk, chunk)
                for half in range(2):
                    some = pl.ds(half * wide // 2, wide // 2)
                    part = block_at(2 * j + half, wide // 2)
                    r.act[part, cols], r.gh[part, cols] = gelu_parts(
                        dot(r.up_t[some, :], r.low2[:, cols]), dot(r.tile_down[some, :], r.cot_f[:, cols]))
            at_step(j, [weights_step(items + k) + sums_step(k) for k in range(tiles)])
            d_up = dot_nt(r.low2[...], r.gh[rows, :]).astype(BF16)
            if nz:
                r.mine[j] = d_up.reshape(blocks(per, wide))
                at_step(j, [[g.cores] for g in groups])
            else:
                r.d_up[:, rows] = d_up

        def layer_back(m):
            cols, rows = block_at(m, chunk), block_at(m, share)
            r.gn[...] = dot(r.up[...], r.gh[:, cols])
            r.cot_t[rows, :] = dot_nt(r.act[rows, :], r.cot_f[...]).astype(BF16)
            stream.start(*d_down_copy(m))
            normed, inverse = norm_rows(r.middle[:, cols])
            grad_normed = r.gn[...]
            r.starts[:, cols] = r.cot_f[:, cols].astype(F32) + norm_rows_back(grad_normed, param(small(), chars + 2), normed, inverse)
            r.ln[0] += fold(grad_normed * normed)
            r.ln[1] += fold(grad_normed)
            stream.start(*grad_copy(m))

        prelude()
        stream.wait(*cot_in)

        def items_loop(i, _):
            @pl.when(i >= 2)
            def _():
                stream.wait(*powers_copy(i - 2))
            item(i)
            at_step(i, [weights_step(k) for k in range(items)])
            return 0
        lax.fori_loop(0, items, items_loop, 0)
        left(0, 1)
        leave(2, 3)

        def tiles_loop(j, _):
            tile(j)
            return 0
        lax.fori_loop(0, tiles, tiles_loop, 0)
        leave(4, 5)

        def chunks_loop(m, _):
            layer_back(m)
            at_step(m, [sums_step(tiles + k) for k in range(chunks)])
            return 0
        lax.fori_loop(0, chunks, chunks_loop, 0)
        if nz:
            for g in (first, *qkv, out, *ups, down):
                g.finish()
            for j in range(tiles):
                r.o_up[:, j * wide:(j + 1) * wide] = groups[j].total()
        left(*range(2, len(to_hbm)))
        for i in range(max(items - 2, 0), items):
            stream.wait(*powers_copy(i))
        for m in range(chunks):
            stream.wait(*d_down_copy(m))
            stream.wait(*grad_copy(m))

    return call.run(kernel, "forward_and_ffn", None, 0 if nz else None)


def backward(nz, chars, tokens, small, w_qkv, w_out, saved, chunk=512):
    feat, n = saved.start_o.shape
    seqs = saved.powers_o.shape[0]
    ff = saved.act_o.shape[0]
    length = n // seqs
    pair = 2 if seqs % 2 == 0 else 1
    items, width, chunks = seqs // pair, pair * length, n // chunk
    heads = Heads(feat)
    vmem = lambda kind, *shape: pltpu.VMEM(shape, kind)
    there = lambda value: (value, ANYWHERE)
    call = Call()
    call.arg(tok=(tokens.reshape(seqs, 1, length), RESIDENT), waves=(saved.waves, RESIDENT), inv=(saved.inv, RESIDENT), small_i=there(small),
             qkv_i=there(w_qkv), out_i=there(w_out), start_i=there(saved.start_o), grad_i=there(saved.grad_o), project_i=there(saved.project_o),
             powers_i=there(saved.powers_o), mixed_i=there(saved.mixed_o), ln2_i=there(saved.ln),
             middle_i=there(saved.middle_o), act_i=there(saved.act_o), down_i=there(saved.down_o))
    call.out(d_in=((feat, n), F32, ANYWHERE), result=((feat, n), F32, ANYWHERE))
    call.temp(small=vmem(BF16, feat, 128), qkv=vmem(BF16, feat, 3 * feat), w_out=vmem(BF16, feat, feat), start=vmem(F32, feat, n),
              grad=vmem(F32, feat, n), project=vmem(BF16, 2, 3 * feat, width), powers=vmem(BF16, 2, pair, HEADS, length, length),
              mixed=vmem(BF16, feat, n), ln2=vmem(F32, 2, feat, 128), middle=vmem(F32, feat, n), act=vmem(BF16, 2, ff, chunk),
              down_t=vmem(BF16, feat, ff), ln1=vmem(F32, 2, feat, 128), d_char=vmem(F32, feat, 128), low_f=vmem(BF16, feat, n),
              gp_f=vmem(BF16, 3 * feat, n), ga_f=vmem(BF16, feat, n), scores=vmem(F32, pair * HEADS, length, length),
              grads=vmem(BF16, pair * HEADS, length, length), grad_mixed=vmem(F32, feat, width), scaled=vmem(BF16, feat, width),
              lean=vmem(F32, seqs, HEADS, length), gn=vmem(F32, feat, width), sems=pltpu.SemaphoreType.DMA((12 + 4 * items + chunks,)))
    parts = 4
    if nz:
        devices = nz * 8
        per, down_per = feat // devices, ff // devices
        blocks = (nz,) + BLOCKS
        call.arg(d_down=there(saved.d_down_o.reshape(blocks + (down_per, feat))))
        small_out = lambda *shape: (shape, F32, RESIDENT)
        call.out(o_out=small_out(per, feat), o_down=small_out(down_per, feat), o_qkv=small_out(per, 3 * feat), o_time=small_out(per, feat),
                 o_char=small_out(per, chars), o_ln=small_out(4, per))
        call.temp(down_sums=Scatter.scratch(nz, (down_per, feat)), rest_sums=Scatter.scratch(nz, (per, 128 + feat)),
                  at_sums=Scatter.scratch(nz, (per, feat)) * parts, kept=vmem(BF16, nz, 2, 2, down_per, feat),
                  d_at=[vmem(BF16, *blocks, per, feat)] * parts, d_rest=vmem(BF16, *blocks, per, 128 + feat))
    else:
        call.out(d_at=((feat, 4 * feat), BF16, RESIDENT), d_rest=((feat, 128 + feat), BF16, RESIDENT))

    def kernel(r):
        stream = Stream(r.sems)
        if nz:
            c = place()[3]
            down = Scatter(nz, r.d_down, r.down_sums, r.kept)
            ats = [Scatter(nz, r.d_at[p], r.at_sums[5 * p:5 * p + 5]) for p in range(parts)]
            rest = Scatter(nz, r.d_rest, r.rest_sums)

        def tall(value):
            value = value.astype(BF16)
            return value.reshape(blocks + (per, value.shape[-1])) if nz else value

        def columns(i):
            return block_at(i, width)

        fixed = [(r.out_i, r.w_out), (r.small_i.at[:, pl.ds(0, 128)], r.small), (r.qkv_i, r.qkv), (r.ln2_i, r.ln2), (r.middle_i, r.middle),
                 (r.down_i, r.down_t)]
        if nz:
            fixed.append((r.d_down.at[pl.ds(0, nz), :, :, c], r.kept))

        def fetch(*numbers):
            for k in numbers:
                stream.start(k, *fixed[k])

        def fetched(*numbers):
            for k in numbers:
                stream.wait(k, *fixed[k])

        def item_copies(i):
            cols = columns(i)
            return [(12 + i, r.grad_i.at[:, cols], r.grad.at[:, cols]), (12 + items + i, r.start_i.at[:, cols], r.start.at[:, cols]),
                    (12 + 2 * items + i, r.mixed_i.at[:, cols], r.mixed.at[:, cols]), (8 + i % 2, r.project_i.at[:, cols], r.project.at[i % 2]),
                    (10 + i % 2, r.powers_i.at[pl.ds(i * pair, pair)], r.powers.at[i % 2])]

        def d_in_copy(i):
            return 12 + 3 * items + i, r.start.at[:, columns(i)], r.d_in.at[:, columns(i)]

        def act_copy(m):
            return 8 + m % 2, r.act_i.at[:, block_at(m, chunk)], r.act.at[m % 2]

        def result_copy(m):
            cols = block_at(m, chunk)
            return 12 + 4 * items + m, r.middle.at[:, cols], r.result.at[:, cols]

        def norm_again(i):
            normed, _ = norm_rows(r.start[:, columns(i)])
            r.low_f[:, columns(i)] = (normed * param(r.small[...], chars) + param(r.small[...], chars + 1)).astype(BF16)

        def products():
            pairs = [(r.mixed, r.ga_f)] + [(r.low_f, r.gp_f.at[pl.ds(p * feat, feat)]) for p in range(3)]
            for p, (left, right) in enumerate(pairs):
                product = tall(dot_nt(left[...], right[...]))
                if nz:
                    r.d_at[p][...] = product
                    ats[p].cores()
                    if p > 0:
                        ats[p - 1].corners()
                else:
                    r.d_at[:, p * feat:(p + 1) * feat] = product

        def layer_back(i):
            r.gn[...] = dot(r.qkv[...], r.gp_f[:, columns(i)])
            grad_normed = r.gn[...]
            normed, inverse = norm_rows(r.start[:, columns(i)])
            d_in = r.grad[:, columns(i)] + norm_rows_back(grad_normed, param(r.small[...], chars), normed, inverse)
            r.start[:, columns(i)] = d_in
            stream.start(*d_in_copy(i))
            r.ln1[0] += fold(grad_normed * normed)
            r.ln1[1] += fold(grad_normed)
            one_hot = jnp.concatenate([one_hot_of(r.tok[i * pair + k], i * pair + k) for k in range(pair)], axis=1)
            high = d_in.astype(BF16)
            low = (d_in - high.astype(F32)).astype(BF16)
            r.d_char[...] += dot_nt(high, one_hot) + dot_nt(low, one_hot)

        def rest_products():
            lane = lax.broadcasted_iota(jnp.int32, r.d_char.shape, 1)
            sums = r.d_char[...]
            table = jnp.where(lane < chars, sums, 0.0)
            for k, ref in enumerate((r.ln1.at[0], r.ln1.at[1], r.ln2.at[0], r.ln2.at[1])):
                table = jnp.where(lane == chars + k, jnp.sum(ref[...], axis=1, keepdims=True), table)
            stamps = jnp.concatenate([sums[:, ITEM_HIGH:], sums[:, :ITEM_HIGH]], axis=1)
            stamps = jnp.where(lane < seqs, stamps, 0.0).astype(BF16)
            r.d_rest[..., :128] = tall(table)
            r.d_rest[..., 128:] = tall(dot_nt(r.waves[...], stamps))

        def result(m):
            cols = block_at(m, chunk)
            stream.wait(*act_copy(m))
            r.middle[:, cols] = r.middle[:, cols] + dot(r.down_t[...], r.act[m % 2])
            stream.start(*result_copy(m))

            @pl.when(m + 2 < chunks)
            def _():
                stream.start(*act_copy(m + 2))

        def item(i):
            copies = item_copies(i)
            stream.wait(*copies[0])
            grad_low = r.grad[:, columns(i)].astype(BF16)
            r.ga_f[:, columns(i)] = grad_low
            r.grad_mixed[...] = dot(r.w_out[...], grad_low).astype(BF16).astype(F32)
            stream.wait(*copies[1])
            norm_again(i)
            for copy in copies[2:]:
                stream.wait(*copy)

            @pl.when(i + 1 < items)
            def _():
                for copy in item_copies(i + 1):
                    stream.start(*copy)
            views = []
            for k in range(pair):
                here, number = pl.ds(k * length, length), i * pair + k
                cols, group = block_at(number, length), pl.ds(k * HEADS, HEADS)
                views.append((r.project.at[i % 2, :, here], r.scaled.at[:, here], r.powers.at[i % 2, k], r.scores.at[group], r.grads.at[group], cols))
                heads.scale_grad(r.grad_mixed.at[:, here], r.inv.at[number], r.mixed.at[:, cols], r.scaled.at[:, here], r.lean.at[number])
            for project, scaled, powers, scores, grads, cols in views:
                heads.grad_probs(project, scaled, scores)
            for k, (project, scaled, powers, scores, grads, cols) in enumerate(views):
                heads.grad_scores(powers, scores, r.lean.at[i * pair + k], grads)
                heads.grad_project(project, scaled, powers, grads, r.gp_f, cols)

        if nz:
            greet(nz)
        fetch(0)
        first_copies = item_copies(0)
        stream.start(*first_copies[0])
        fetch(1)
        for copy in first_copies[1:]:
            stream.start(*copy)
        r.ln1[...] = jnp.zeros_like(r.ln1)
        r.d_char[...] = jnp.zeros_like(r.d_char)
        fetched(0, 1)

        def items_loop(i, _):
            item(i)
            if nz:
                at_step(i, [[lambda: fetch(6), lambda: greeted(nz), down.cores], [lambda: fetched(6), down.corners]])
            return 0
        lax.fori_loop(0, items, items_loop, 0)
        fetch(2, 3, 4, 5)
        for m in range(2):
            stream.start(*act_copy(m))
        if nz:
            down.sides()
        products()
        fetched(2)

        def back_loop(i, _):
            layer_back(i)
            if nz:
                at_step(i, [[ats[3].corners], [ats[0].sides, ats[1].sides, down.lines], [ats[2].sides, ats[3].sides], [ats[0].lines, ats[1].lines]])
            return 0
        lax.fori_loop(0, items, back_loop, 0)
        fetched(3)
        rest_products()
        fetched(4, 5)
        if nz:
            rest.cores()
            ats[2].lines()
            ats[3].lines()

        def result_loop(m, _):
            result(m)
            if nz:
                at_step(m, [[rest.corners]] + [[]] * (chunks - 3) + [[rest.sides]])
            return 0
        lax.fori_loop(0, chunks, result_loop, 0)
        if nz:
            r.o_down[...] = down.total()
            r.o_out[...] = ats[0].total()
            for p in range(3):
                r.o_qkv[:, p * feat:(p + 1) * feat] = ats[1 + p].total()
            rest.lines()
            total = rest.total()
            r.o_time[...] = total[:, 128:]
            r.o_char[...] = total[:, :chars]
            r.o_ln[...] = total[:, :128].T[chars:chars + 4]
        for i in range(items):
            stream.wait(*d_in_copy(i))
        for m in range(chunks):
            stream.wait(*result_copy(m))

    return call.run(kernel, "backward", None, 1 if nz else None)


def hand_over(result, d_in, ln, *others, width=1024):
    feat, n = d_in.shape
    call = Call()
    turned = ((n, feat), F32, pl.BlockSpec((width, feat), lambda i: (i, 0)))
    call.arg(result=(result, lanes(feat, width)), d_in=(d_in, lanes(feat, width)), ln=(ln, whole(ln.shape)))
    call.arg(**{f"a{k}": (value, whole(value.shape)) for k, value in enumerate(others)})
    call.out(o_result=turned, o_d_in=turned, **{f"l{k}": ((1, ln.shape[1]), F32, whole((1, ln.shape[1]))) for k in range(4)})
    call.out(**{f"o{k}": (value.shape, F32, whole(value.shape)) for k, value in enumerate(others)})

    def kernel(r):
        r.o_result[...] = r.result[...].T
        r.o_d_in[...] = r.d_in[...].T

        @pl.when(pl.program_id(0) == 0)
        def _():
            for k, ref in enumerate((r.l0, r.l1, r.l2, r.l3)):
                ref[...] = r.ln[k:k + 1]
            for k in range(len(others)):
                getattr(r, f"o{k}")[...] = getattr(r, f"a{k}")[...]

    got = call.run(kernel, "hand_over", n // width)
    return got.o_result, got.o_d_in, [getattr(got, f"l{k}") for k in range(4)], [getattr(got, f"o{k}") for k in range(len(others))]


def make_body(gx, gy):
    def gathered(*shards):
        return [lax.all_gather(s, AXES, axis=0, tiled=True) for s in shards]

    def summed(part):
        return lax.psum_scatter(part.astype(F32), AXES, scatter_dimension=0, tiled=True)

    def body(tokens, timesteps, cotangent, char_table, time_weight, ln1_gain, ln1_bias, w_qkv, w_attn_out, ln2_gain, ln2_bias, w_up, w_down):
        feat = time_weight.shape[1]
        chars = char_table.shape[0]
        per = feat // (gx * gy)
        nz = gx // 2 if gy == 4 and gx % 8 == 0 and per % 16 == 0 else 0
        shards = [char_table.T, ln1_gain, ln1_bias, ln2_gain, ln2_bias, time_weight, w_qkv, w_attn_out, w_up, w_down]
        if not nz:
            shards = gathered(*shards)
        saved = forward(nz, tokens, timesteps, cotangent, *shards)
        if nz:
            small, w_qkv, w_out = (value.reshape(feat, value.shape[-1]) for value in (saved.first_o, saved.qkv_o, saved.out_o))
            got = backward(nz, chars, tokens, small, w_qkv, w_out, saved)
            ln, sums = got.o_ln, (got.o_char, got.o_time, got.o_qkv, got.o_out, saved.o_up, got.o_down)
        else:
            got = backward(nz, chars, tokens, saved.small, *shards[6:8], saved)
            up, down, at, rest = (summed(p) for p in (saved.d_up, saved.d_down_o, got.d_at, got.d_rest))
            ln, sums = rest[:, chars:chars + 4].T, (rest[:, :chars], rest[:, 128:], at[:, feat:], at[:, :feat], up, down)
        result, d_in, lns, (char, time, qkv, out, up, down) = hand_over(got.result, got.d_in, ln, *sums)
        g1, b1, g2, b2 = (value.reshape(per) for value in lns)
        return result, d_in, char.T, time, g1, b1, qkv, out, g2, b2, up, down
    return body


def solution(mesh):
    every = P(AXES)
    rows, cols = P(AXES, None), P(None, AXES)
    return jax.shard_map(
        make_body(mesh.shape[AXES[0]], mesh.shape[AXES[1]]),
        mesh=mesh,
        in_specs=(every, every, rows, cols, rows, every, every, rows, rows, every, every, rows, rows),
        out_specs=(rows, rows, cols, rows, every, every, rows, rows, every, every, rows, rows),
        check_vma=False,
    )
```

```python
import math
import types

import jax
import jax.numpy as jnp
from jax import lax
from jax.experimental import pallas as pl
from jax.experimental.pallas import tpu as pltpu
from jax.sharding import PartitionSpec as P

F32, BF16 = jnp.float32, jnp.bfloat16
MESH = pl.DeviceIdType.MESH
AXES = ("gx", "gy")
HEADS = 8
EPSILON = 1e-05
VMEM_LIMIT = 63 * 2**20
BLOCKS = (2, 2, 2)
X, Y, CORE = range(3)


def place():
    gx, gy = lax.axis_index(AXES[0]), lax.axis_index(AXES[1])
    return gx // 2, gx % 2, gy // 2, gy % 2


def device(z, x, y, c):
    return (z * 2 + x, y * 2 + c)


def across(axis):
    z, x, y, c = place()
    return ((z, 1 - x, y, c), (z, x, 1 - y, c), (z, x, y, 1 - c))[axis]


def greet(nz):
    z, x, y, c = place()
    barrier = pltpu.get_barrier_semaphore()
    for where in [across(axis) for axis in (X, Y, CORE)] + [((z + d) % nz, x, y, c) for d in range(1, nz)]:
        pl.semaphore_signal(barrier, inc=1, device_id=device(*where), device_id_type=MESH)


def greeted(nz):
    pl.semaphore_wait(pltpu.get_barrier_semaphore(), 3 + nz - 1)


def halves(width):
    middle = width // 256 * 128
    return pl.ds(0, middle), pl.ds(middle, width - middle)


def blocks_of(out, number):
    if number % 4:
        return out.at[pl.ds(0, number), 0, 0, 0]
    return out.at[pl.ds(0, number // 4), :, :, 0]


class Gather:
    LINES, SIDES, CORNERS, CORES = range(4)

    @staticmethod
    def scratch(nz):
        return pltpu.SemaphoreType.DMA((2, 4))

    def __init__(self, nz, shard, out, sems):
        self.nz, self.shard, self.out, self.sems = nz, shard, out, sems
        self.zs, self.count, self.base, self.waits = pl.ds(0, nz), nz, 0, True

    def send(self, src, dst, sent, came, where):
        return pltpu.make_async_remote_copy(
            src_ref=src, dst_ref=dst, send_sem=self.sems.at[0, sent + (self.base if sent else 0)],
            recv_sem=self.sems.at[1, came + (self.base if came else 0)], device_id=device(*where), device_id_type=MESH)

    def some(self, number, stage):
        ref = blocks_of(self.out, number)
        return self.send(ref, ref, stage, stage, across(CORE))

    def pass_on(self, axis, a, b, sent, came, cut=None):
        c = place()[3]
        ref = self.out.at[self.zs, a, b, c]
        if cut is not None:
            ref = ref.at[:, :, cut]
        self.send(ref, ref, sent, came, across(axis)).start()

    def lines(self):
        z, x, y, c = place()
        for d in range(1, self.nz):
            self.send(self.shard, self.out.at[z, x, y, c], self.LINES, self.LINES, ((z + d) % self.nz, x, y, c)).start()

    def arrived(self):
        self.some(self.nz - 1, self.LINES).wait_recv()

    def sides(self):
        _, x, y, _ = place()
        if self.waits:
            self.arrived()
        self.pass_on(X, x, y, self.SIDES, self.SIDES)
        self.pass_on(Y, x, y, self.SIDES, self.SIDES)
        self.pass_on(CORE, x, y, self.SIDES, self.CORES)

    def corners(self):
        _, x, y, _ = place()
        lo, hi = halves(self.out.shape[-1])
        self.some(2 * self.count, self.SIDES).wait_recv()
        self.pass_on(X, x, 1 - y, self.CORNERS, self.CORNERS, lo)
        self.pass_on(Y, 1 - x, y, self.CORNERS, self.CORNERS, hi)
        self.pass_on(CORE, 1 - x, y, self.CORNERS, self.CORES)
        self.pass_on(CORE, x, 1 - y, self.CORNERS, self.CORES)

    def cores(self):
        _, x, y, _ = place()
        self.some(self.count, self.CORNERS).wait_recv()
        self.pass_on(CORE, 1 - x, 1 - y, self.CORES, self.CORES)

    def whole(self):
        self.some(4 * self.count, self.CORES).wait_recv()

    def sent(self):
        self.some(3 * self.count, self.SIDES).wait_send()
        self.some(3 * self.count, self.CORNERS).wait_send()
        self.some(self.count, self.CORES).wait_send()

    def finish(self):
        self.some(self.nz - 1, self.LINES).wait_send()
        self.sent()


class GatherLayers(Gather):
    @staticmethod
    def scratch(nz):
        return pltpu.SemaphoreType.DMA((2, 1 + 3 * nz))

    def layer(self, j):
        one = Gather(self.nz, self.shard, self.out, self.sems)
        one.zs, one.count, one.base, one.waits = pl.ds(j, 1), 1, 3 * j, False
        return one

    def sent(self):
        for j in range(self.nz):
            self.layer(j).sent()


class Scatter:
    @staticmethod
    def scratch(nz, tail):
        return [pltpu.VMEM((nz, 2, 2) + tail, BF16), pltpu.VMEM((nz,) + tail, BF16), pltpu.VMEM((2, nz) + tail, BF16),
                pltpu.VMEM((nz - 1,) + tail, BF16), pltpu.SemaphoreType.DMA((2, 4))]

    def __init__(self, nz, mine, temps, kept=None):
        self.nz, self.mine, self.kept = nz, mine, kept
        self.own, self.far, self.near, self.line, self.sems = temps
        self.width = self.own.shape[-1]

    def send(self, src, dst, stage, where):
        return pltpu.make_async_remote_copy(
            src_ref=src, dst_ref=dst, send_sem=self.sems.at[0, stage], recv_sem=self.sems.at[1, stage],
            device_id=device(*where), device_id_type=MESH)

    def done(self, ref, stage):
        self.send(ref, ref, stage, across(CORE)).wait()

    def add(self, a, b, cols, *values):
        spot = (slice(None), a, b, slice(None), cols)
        total = self.own[spot]
        for value in values:
            total = total + value
        self.own[spot] = total

    def cores(self):
        c = place()[3]
        self.send(self.mine.at[pl.ds(0, self.nz), :, :, 1 - c], self.own, 0, across(CORE)).start()

    def corners(self):
        _, x, y, c = place()
        every, all_z = pl.ds(0, self.width), pl.ds(0, self.nz)
        lo, hi = halves(self.width)
        self.done(self.own, 0)
        for number, (a, b) in enumerate(((1 - x, 1 - y), (1 - x, y), (x, 1 - y), (x, y))):
            self.add(a, b, every, self.mine[:, a, b, c] if self.kept is None else self.kept[:, a, b])
            if number == 0:
                self.send(self.own.at[all_z, 1 - x, 1 - y, :, lo], self.far.at[:, :, lo], 1, across(X)).start()
                self.send(self.own.at[all_z, 1 - x, 1 - y, :, hi], self.far.at[:, :, hi], 1, across(Y)).start()

    def sides(self):
        _, x, y, _ = place()
        all_z = pl.ds(0, self.nz)
        lo, hi = halves(self.width)
        self.done(self.far, 1)
        self.add(x, 1 - y, lo, self.far[:, :, lo])
        self.send(self.own.at[all_z, x, 1 - y], self.near.at[1], 2, across(Y)).start()
        self.add(1 - x, y, hi, self.far[:, :, hi])
        self.send(self.own.at[all_z, 1 - x, y], self.near.at[0], 2, across(X)).start()

    def lines(self):
        z, x, y, c = place()
        self.done(self.near, 2)
        self.add(x, y, pl.ds(0, self.width), self.near[0], self.near[1])
        for d in range(1, self.nz):
            to = (z + d) % self.nz
            self.send(self.own.at[to, x, y], self.line.at[d - 1], 3, (to, x, y, c)).start()

    def total(self):
        z, x, y, _ = place()
        self.done(self.line, 3)
        total = self.own[z, x, y].astype(F32)
        for d in range(1, self.nz):
            total = total + self.line[d - 1].astype(F32)
        return total


class Call:
    def __init__(self):
        self.ins, self.outs, self.temps = {}, {}, {}

    def arg(self, **named):
        self.ins.update(named)

    def out(self, **named):
        self.outs.update(named)

    def temp(self, **named):
        self.temps.update(named)

    def run(self, kernel, name, steps=None, collective=None):
        kinds = [k for kind in self.temps.values() for k in (kind if isinstance(kind, list) else [kind])]

        def body(*refs):
            refs = iter(refs)
            r = types.SimpleNamespace(**{n: next(refs) for n in [*self.ins, *self.outs]})
            for n, kind in self.temps.items():
                setattr(r, n, [next(refs) for _ in kind] if isinstance(kind, list) else next(refs))
            kernel(r)
        extra = {} if collective is None else dict(collective_id=collective, has_side_effects=True)
        got = pl.pallas_call(
            body, grid=() if steps is None else (steps,), in_specs=[spec for _, spec in self.ins.values()], out_specs=[spec for *_, spec in self.outs.values()],
            out_shape=[jax.ShapeDtypeStruct(shape, kind) for shape, kind, _ in self.outs.values()], scratch_shapes=kinds,
            compiler_params=pltpu.CompilerParams(vmem_limit_bytes=VMEM_LIMIT, **extra), name=name,
        )(*[array for array, _ in self.ins.values()])
        return types.SimpleNamespace(**dict(zip(self.outs, got)))


def whole(shape):
    return pl.BlockSpec(tuple(shape), lambda i: (0,) * len(shape))


def lanes(rows, width, at=lambda i: i):
    return pl.BlockSpec((rows, width), lambda i: (0, at(i)))


ANYWHERE = pl.BlockSpec(memory_space=pl.ANY)
RESIDENT = pl.BlockSpec(memory_space=pltpu.VMEM)


def at_step(i, table):
    for step, acts in enumerate(table):
        if acts:
            @pl.when(i == step)
            def _():
                for act in acts:
                    act()


def block_at(i, width):
    return pl.ds(pl.multiple_of(i * width, width), width)


def dot(left, right):
    return jnp.dot(left, right, preferred_element_type=F32)


def dot_nt(left, right):
    return lax.dot_general(left, right, (((1,), (1,)), ((), ())), preferred_element_type=F32)


def norm_rows(values):
    count = values.shape[0]
    shifted = values - jnp.sum(values, axis=0, keepdims=True) * (1.0 / count)
    inverse = lax.rsqrt(jnp.sum(shifted * shifted, axis=0, keepdims=True) * (1.0 / count) + EPSILON)
    return shifted * inverse, inverse


def norm_rows_back(grad, gain, normed, inverse):
    count = grad.shape[0]
    scaled = grad * gain
    lean = jnp.sum(scaled, axis=0, keepdims=True) * (1.0 / count)
    turn = jnp.sum(scaled * normed, axis=0, keepdims=True) * (1.0 / count)
    return inverse * (scaled - lean - normed * turn)


def fold(values):
    total = values[:, :128]
    for k in range(1, values.shape[1] // 128):
        total = total + values[:, 128 * k:128 * (k + 1)]
    return total


def flat(ref, cols=slice(None)):
    value = ref[(slice(None),) * (len(ref.shape) - 1) + (cols,)]
    return value.reshape(-1, value.shape[-1])


def param(table, column):
    return table[:, column:column + 1].astype(F32)


def gelu_parts(hidden, grad_active):
    cdf = 0.5 + 0.5 * lax.erf(hidden * math.sqrt(0.5))
    bell = jnp.exp2(hidden * hidden * (-0.5 * math.log2(math.e))) * (1.0 / math.sqrt(2.0 * math.pi))
    return (hidden * cdf).astype(BF16), (grad_active.astype(BF16).astype(F32) * (cdf + hidden * bell)).astype(BF16)


def fill_waves(r, feat):
    half = feat // 2
    r.steps_row[...] = jnp.zeros_like(r.steps_row)
    r.steps_row[:, :r.steps.shape[1]] = r.steps[...].astype(F32)
    rate = jnp.exp(lax.broadcasted_iota(jnp.int32, (half, 128), 0).astype(F32) * (-math.log(10000.0) / half))
    angles = rate * r.steps_row[...]
    r.waves[:half, :] = jnp.sin(angles).astype(BF16)
    r.waves[half:, :] = jnp.cos(angles).astype(BF16)


def fill_small(r, chars):
    count = r.char.shape[0]
    r.square[...] = jnp.zeros_like(r.square)
    for k, ref in enumerate((r.g1, r.b1, r.g2, r.b2)):
        r.square[chars + k:chars + k + 1, :count] = ref[...].astype(F32)
    r.small_shard[...] = r.square[...].T[:count].astype(BF16)
    r.small_shard[:, :chars] = r.char[...]


ITEM_HIGH, ITEM_LOW = 32, 64


def one_hot_of(tok, item):
    row = lax.broadcasted_iota(jnp.int32, (128, tok.shape[1]), 0)
    return ((row == tok) | (row == ITEM_HIGH + item) | (row == ITEM_LOW + item)).astype(BF16)


class Heads:
    def __init__(self, feat):
        self.size = feat // HEADS
        self.q, self.k, self.v = ([pl.ds(part * feat + h * self.size, self.size) for h in range(HEADS)] for part in range(3))

    def scores(self, project, scores):
        for h in range(HEADS):
            scores[h] = dot(project[self.k[h], :].T, project[self.q[h], :])

    def softmax(self, scores, powers, inverses):
        turn = math.log2(math.e) / math.sqrt(self.size)
        for h in range(HEADS):
            value = scores[h]
            power = jnp.exp2((value - jnp.max(value, axis=0, keepdims=True)) * turn)
            inverses[h:h + 1, :] = 1.0 / jnp.sum(power, axis=0, keepdims=True)
            powers[h] = power.astype(BF16)

    def mix(self, project, powers, inverses, mixed):
        for h in range(HEADS):
            mixed[self.q[h], :] = (dot(project[self.v[h], :], powers[h]) * inverses[h:h + 1, :]).astype(BF16)

    def scale_grad(self, grad_mixed, inverses, mixed, scaled, lean):
        for h in range(HEADS):
            value = grad_mixed[self.q[h], :] * inverses[h:h + 1, :]
            lean[h:h + 1, :] = jnp.sum(value * mixed[self.q[h], :].astype(F32), axis=0, keepdims=True)
            scaled[self.q[h], :] = value.astype(BF16)

    def grad_probs(self, project, scaled, scores):
        for h in range(HEADS):
            scores[h] = dot(project[self.v[h], :].T, scaled[self.q[h], :])

    def grad_scores(self, powers, scores, lean, grads):
        for h in range(HEADS):
            grads[h] = (powers[h].astype(F32) * (scores[h] - lean[h:h + 1, :])).astype(BF16)

    def grad_project(self, project, scaled, powers, grads, out, cols):
        scale = 1.0 / math.sqrt(self.size)
        for h in range(HEADS):
            out[self.v[h], cols] = dot_nt(scaled[self.q[h], :], powers[h]).astype(BF16)
            out[self.q[h], cols] = (dot(project[self.k[h], :], grads[h]) * scale).astype(BF16)
            out[self.k[h], cols] = (dot_nt(project[self.q[h], :], grads[h]) * scale).astype(BF16)


class Stream:
    def __init__(self, sems):
        self.sems = sems

    def start(self, number, src, dst):
        pltpu.make_async_copy(src, dst, self.sems.at[number]).start()

    def wait(self, number, src, dst):
        pltpu.make_async_copy(src, dst, self.sems.at[number]).wait()


def forward(nz, tokens, timesteps, cotangent, char, g1, b1, g2, b2, time_w, w_qkv, w_out, w_up, w_down, chunk=512):
    seqs = timesteps.shape[0]
    n = tokens.shape[0]
    length = n // seqs
    feat, ff = time_w.shape[1], w_up.shape[1]
    count, chars = char.shape
    pair = 2 if seqs % 2 == 0 else 1
    items, width = seqs // pair, pair * length
    wide = ff // nz if nz else 512
    tiles, chunks = ff // wide, n // chunk
    share = ff // chunks
    heads = Heads(feat)
    call = Call()
    at_once = lambda value: (value, RESIDENT)
    call.arg(tok=at_once(tokens.reshape(seqs, 1, length)), steps=at_once(timesteps.reshape(1, seqs)), char=at_once(char),
             g1=at_once(g1.reshape(1, count)), b1=at_once(b1.reshape(1, count)), g2=at_once(g2.reshape(1, count)),
             b2=at_once(b2.reshape(1, count)), time_w=at_once(time_w), w_qkv=at_once(w_qkv), w_out=at_once(w_out), w_up=at_once(w_up),
             w_down=at_once(w_down), cot=(cotangent, ANYWHERE))
    call.out(start_o=((feat, n), F32, ANYWHERE), mixed_o=((feat, n), BF16, ANYWHERE), project_o=((3 * feat, n), BF16, ANYWHERE),
             powers_o=((seqs, HEADS, length, length), BF16, ANYWHERE), inv=((seqs, HEADS, length), F32, RESIDENT),
             waves=((feat, 128), BF16, RESIDENT), grad_o=((feat, n), F32, ANYWHERE), ln=((2, feat, 128), F32, RESIDENT),
             d_down_o=((ff, feat), BF16, ANYWHERE), middle_o=((feat, n), F32, ANYWHERE), act_o=((ff, n), BF16, ANYWHERE),
             down_o=((feat, ff), BF16, ANYWHERE), d_out_o=((feat, feat), BF16, ANYWHERE))
    parts = 3
    vmem = lambda kind, *shape: pltpu.VMEM(shape, kind)
    if nz:
        per = feat // (nz * 8)
        blocks = lambda *tail: (nz,) + BLOCKS + tail
        landing = lambda *tail: vmem(BF16, *blocks(*tail))
        sems = Gather.scratch(nz)
        call.temp(first=landing(count, 128 + feat), first_sems=sems, out=landing(count, feat), out_sems=sems,
                  qkv=[landing(count, feat)] * parts, qkv_sems=[sems] * parts, ups=vmem(BF16, tiles, *blocks(count, wide)), up_sems=[sems] * tiles,
                  down=landing(*w_down.shape), down_sems=GatherLayers.scratch(nz), first_shard=vmem(BF16, count, 128 + feat),
                  mine=vmem(BF16, tiles, *blocks(per, wide)), sums=Scatter.scratch(nz, (per, wide)) * tiles)
        call.out(first_o=(blocks(count, 128 + feat), BF16, ANYWHERE), out_o=(blocks(count, feat), BF16, ANYWHERE),
                 qkv_o=(blocks(*w_qkv.shape), BF16, ANYWHERE), o_up=((per, ff), F32, RESIDENT))
    else:
        call.out(small=((count, 128), BF16, RESIDENT), d_up=((feat, ff), BF16, RESIDENT))
    call.temp(small_shard=vmem(BF16, count, 128), square=vmem(F32, 128, max(count, 128)), steps_row=vmem(F32, 1, 128),
              table=vmem(BF16, feat, 128), out_t=vmem(BF16, feat, feat), starts=vmem(F32, feat, n), mixed=vmem(BF16, feat, n),
              powers=vmem(BF16, 2, pair, HEADS, length, length), scores=vmem(F32, pair * HEADS, length, length),
              middle=vmem(F32, feat, n), low2=vmem(BF16, feat, n), cot_t=vmem(BF16, max(n, ff), feat), cot_f=vmem(BF16, feat, n),
              d_out=vmem(BF16, feat, feat), down_t=vmem(BF16, feat, ff), up=vmem(BF16, feat, ff), up_t=vmem(BF16, wide, feat),
              act=vmem(BF16, ff, n), gh=vmem(BF16, ff, n), gn=vmem(F32, feat, chunk), tile_down=vmem(BF16, wide, feat),
              sems=pltpu.SemaphoreType.DMA((15 + 2 * chunks,)))

    def kernel(r):
        proj, low = r.act.at[pl.ds(0, 3 * feat)], r.gh.at[pl.ds(0, feat)]
        stream = Stream(r.sems)
        if nz:
            z, x, y, c = place()
            first = Gather(nz, r.first_shard, r.first, r.first_sems)
            qkv = [Gather(nz, r.w_qkv.at[:, pl.ds(p * feat, feat)], r.qkv[p], r.qkv_sems[p]) for p in range(parts)]
            out = Gather(nz, r.w_out, r.out, r.out_sems)
            ups = [Gather(nz, r.w_up.at[:, pl.ds(j * wide, wide)], r.ups.at[j], r.up_sems[j]) for j in range(tiles)]
            down = GatherLayers(nz, r.w_down, r.down, r.down_sems)
            needs = [(ups[j], down.layer(j)) for j in range(tiles)]
            order = [ups[0], ups[1], needs[0][1], needs[1][1]] + [part for some in needs[2:] for part in some]
            groups = [Scatter(nz, r.mine.at[j], r.sums[5 * j:5 * j + 5]) for j in range(tiles)]

        def small():
            return flat(r.first, slice(0, 128)) if nz else r.small[...]

        def stamps(weights):
            stamp = dot(weights.T, r.waves[...])
            lane = lax.broadcasted_iota(jnp.int32, stamp.shape, 1)
            stamp = jnp.where(lane < seqs, stamp, 0.0)
            high = stamp.astype(BF16)
            rest = (stamp - high.astype(F32)).astype(BF16)
            shift = lambda value, by: jnp.concatenate([value[:, 128 - by:], value[:, :128 - by]], axis=1)
            chars_only = jnp.where(lane < chars, small(), jnp.zeros_like(high))
            r.table[...] = chars_only + shift(high, ITEM_HIGH) + shift(rest, ITEM_LOW)

        def begin(some):
            table = small()
            gain, bias = param(table, chars), param(table, chars + 1)
            for k in some:
                cols = pl.ds(k * length, length)
                start = dot(r.table[...], one_hot_of(r.tok[k], k))
                r.starts[:, cols] = start
                normed, _ = norm_rows(start)
                low[:, cols] = (normed * gain + bias).astype(BF16)

        def multiply(p, weights):
            proj[p * feat:(p + 1) * feat] = dot(weights.T, low[...]).astype(BF16)

        to_hbm = [(proj, r.project_o), (r.starts, r.start_o), (r.mixed, r.mixed_o), (r.middle, r.middle_o), (r.act, r.act_o), (r.down_t, r.down_o)]
        d_out_copy = (14 + 2 * chunks, r.d_out, r.d_out_o)
        if nz:
            every = (pl.ds(0, nz), slice(None), slice(None), slice(None), slice(None))
            to_hbm += [(r.first, r.first_o), (r.out, r.out_o)] + [(g.out, r.qkv_o.at[every + (pl.ds(p * feat, feat),)]) for p, g in enumerate(qkv)]
        cot_in = (11, r.cot, r.cot_t.at[pl.ds(0, n)])

        def leave(*numbers):
            for k in numbers:
                stream.start(k, *to_hbm[k])

        def left(*numbers):
            for k in numbers:
                stream.wait(k, *to_hbm[k])

        def powers_copy(i):
            return 12 + i % 2, r.powers.at[i % 2], r.powers_o.at[pl.ds(i * pair, pair)]

        def grad_copy(m):
            cols = block_at(m, chunk)
            return 14 + m, r.starts.at[:, cols], r.grad_o.at[:, cols]

        def d_down_copy(m):
            rows = block_at(m, share)
            return 14 + chunks + m, r.cot_t.at[rows], r.d_down_o.at[rows]

        def prelude():
            stream.start(*cot_in)
            r.ln[...] = jnp.zeros_like(r.ln)
            if not nz:
                fill_small(r, chars)
                r.small[...] = r.small_shard[...]
                fill_waves(r, feat)
                stamps(r.time_w[...])
                r.out_t[...] = r.w_out[...].T
                begin(range(seqs))
                for p in range(parts):
                    multiply(p, r.w_qkv[:, p * feat:(p + 1) * feat])
                leave(0, 1)
                return
            greet(nz)
            fill_small(r, chars)
            q, k, v = qkv
            r.first_shard[:, :128] = r.small_shard[...]
            r.first_shard[:, 128:] = r.time_w[...]
            for g in (first, out, q, k, v, *ups, down):
                g.out[z, x, y, c] = g.shard[...]
            greeted(nz)
            first.lines()
            q.lines()
            k.lines()
            fill_waves(r, feat)
            first.sides()
            v.lines()
            q.sides()
            out.lines()
            k.sides()
            ups[0].lines()
            first.corners()
            v.sides()
            ups[1].lines()
            q.corners()
            down.lines()
            first.cores()
            k.corners()
            v.corners()
            out.sides()
            first.whole()
            stamps(flat(r.first, slice(128, 128 + feat)))
            begin(range(0, seqs // 2))
            q.cores()
            ups[0].sides()
            begin(range(seqs // 2, seqs))
            k.cores()
            q.whole()
            multiply(0, flat(r.qkv[0]))
            v.cores()
            out.corners()
            ups[1].sides()
            for g in ups[2:]:
                g.lines()
            k.whole()
            multiply(1, flat(r.qkv[1]))
            down.arrived()
            needs[0][1].sides()
            v.whole()
            multiply(2, flat(r.qkv[2]))
            ups[0].corners()
            leave(0, 1)

        def out_weights():
            out.cores()
            out.whole()
            r.out_t[...] = flat(r.out).T
            leave(*range(6, 8 + parts))

        def item(i):
            views = []
            for k in range(pair):
                cols = block_at(i * pair + k, length)
                views.append((proj.at[:, cols], r.scores.at[pl.ds(k * HEADS, HEADS)], r.powers.at[i % 2, k], r.inv.at[i * pair + k], r.mixed.at[:, cols]))
            for project, scores, *_ in views:
                heads.scores(project, scores)
            for project, scores, powers, inverses, mixed in views:
                heads.softmax(scores, powers, inverses)
                heads.mix(project, powers, inverses, mixed)
            stream.start(*powers_copy(i))
            if nz:
                at_step(i, [[out_weights]])
            cols = block_at(i, width)
            table = small()
            middle = r.starts[:, cols] + dot(r.out_t[...], r.mixed[:, cols])
            r.middle[:, cols] = middle
            normed, _ = norm_rows(middle)
            r.low2[:, cols] = (normed * param(table, chars + 2) + param(table, chars + 3)).astype(BF16)
            r.cot_f[:, cols] = r.cot_t[cols, :].T

        def weights_step(step):
            if not nz:
                return []
            cores = lambda p: p + 1 if p < 4 else p // 2 + 3
            corners = lambda p: p - 1 if p < 3 else (p + 1) // 2
            acts = [part.cores for p, part in enumerate(order) if cores(p) == step]
            acts += [part.corners for p, part in enumerate(order) if p > 0 and corners(p) == step]
            return acts + [part.sides for part in order[2 * step + 3:2 * step + 5]]

        def sums_step(step):
            if not nz:
                return []
            late = tiles - 3
            acts = []
            for j in reversed(range(tiles)):
                stage = step - j - 1
                if j == late and step in (tiles, tiles + 1):
                    stage = 2 if step == tiles + 1 else -1
                if 0 <= stage < 3:
                    acts.append((groups[j].corners, groups[j].sides, groups[j].lines)[stage])
            return acts

        def tile(j):
            rows = block_at(j, wide)
            if nz:
                at_step(j, [[part.whole for part in some] for some in needs])
                r.up[:, rows] = flat(r.ups.at[j])
                r.tile_down[...] = flat(r.down.at[pl.ds(j, 1)])
            else:
                r.up[:, rows] = r.w_up[:, rows]
                r.tile_down[...] = r.w_down[rows, :]
            r.up_t[...] = r.up[:, rows].T
            r.down_t[:, rows] = r.tile_down[...].T
            for t in range(chunks):
                cols = pl.ds(t * chunk, chunk)
                for half in range(2):
                    some = pl.ds(half * wide // 2, wide // 2)
                    part = block_at(2 * j + half, wide // 2)
                    r.act[part, cols], r.gh[part, cols] = gelu_parts(
                        dot(r.up_t[some, :], r.low2[:, cols]), dot(r.tile_down[some, :], r.cot_f[:, cols]))
            at_step(j, [weights_step(items + k) + sums_step(k) for k in range(tiles)])
            d_up = dot_nt(r.low2[...], r.gh[rows, :]).astype(BF16)
            if nz:
                r.mine[j] = d_up.reshape(blocks(per, wide))
                at_step(j, [[g.cores] for g in groups])
            else:
                r.d_up[:, rows] = d_up

        def layer_back(m):
            cols, rows = block_at(m, chunk), block_at(m, share)
            r.gn[...] = dot(r.up[...], r.gh[:, cols])
            at_step(m, [sums_step(tiles + k) for k in range(chunks)])
            r.cot_t[rows, :] = dot_nt(r.act[rows, :], r.cot_f[...]).astype(BF16)
            stream.start(*d_down_copy(m))
            normed, inverse = norm_rows(r.middle[:, cols])
            grad_normed = r.gn[...]
            grad = r.cot_f[:, cols].astype(F32) + norm_rows_back(grad_normed, param(small(), chars + 2), normed, inverse)
            r.starts[:, cols] = grad
            r.low2[:, cols] = grad.astype(BF16)
            r.ln[0] += fold(grad_normed * normed)
            r.ln[1] += fold(grad_normed)
            stream.start(*grad_copy(m))

        prelude()
        stream.wait(*cot_in)

        def items_loop(i, _):
            @pl.when(i >= 2)
            def _():
                stream.wait(*powers_copy(i - 2))
            item(i)
            at_step(i, [weights_step(k) for k in range(items)])
            return 0
        lax.fori_loop(0, items, items_loop, 0)
        left(0, 1)
        leave(2, 3)

        def tiles_loop(j, _):
            tile(j)
            return 0
        lax.fori_loop(0, tiles, tiles_loop, 0)
        leave(4, 5)

        def chunks_loop(m, _):
            layer_back(m)
            return 0
        lax.fori_loop(0, chunks, chunks_loop, 0)
        r.d_out[...] = dot_nt(r.mixed[...], r.low2[...]).astype(BF16)
        stream.start(*d_out_copy)
        if nz:
            for g in (first, *qkv, out, *ups, down):
                g.finish()
            for j in range(tiles):
                r.o_up[:, j * wide:(j + 1) * wide] = groups[j].total()
        left(*range(2, len(to_hbm)))
        stream.wait(*d_out_copy)
        for i in range(max(items - 2, 0), items):
            stream.wait(*powers_copy(i))
        for m in range(chunks):
            stream.wait(*d_down_copy(m))
            stream.wait(*grad_copy(m))

    return call.run(kernel, "forward_and_ffn", None, 0 if nz else None)


def backward(nz, chars, tokens, small, w_qkv, w_out, saved, chunk=512):
    feat, n = saved.start_o.shape
    seqs = saved.powers_o.shape[0]
    ff = saved.act_o.shape[0]
    length = n // seqs
    pair = 2 if seqs % 2 == 0 else 1
    items, width, chunks = seqs // pair, pair * length, n // chunk
    heads = Heads(feat)
    vmem = lambda kind, *shape: pltpu.VMEM(shape, kind)
    there = lambda value: (value, ANYWHERE)
    call = Call()
    call.arg(tok=(tokens.reshape(seqs, 1, length), RESIDENT), waves=(saved.waves, RESIDENT), inv=(saved.inv, RESIDENT), small_i=there(small),
             qkv_i=there(w_qkv), out_i=there(w_out), start_i=there(saved.start_o), grad_i=there(saved.grad_o), project_i=there(saved.project_o),
             powers_i=there(saved.powers_o), mixed_i=there(saved.mixed_o), ln2_i=there(saved.ln),
             middle_i=there(saved.middle_o), act_i=there(saved.act_o), down_i=there(saved.down_o))
    call.out(d_in=((feat, n), F32, ANYWHERE), result=((feat, n), F32, ANYWHERE))
    call.temp(small=vmem(BF16, feat, 128), qkv=vmem(BF16, feat, 3 * feat), w_out=vmem(BF16, feat, feat), start=vmem(F32, feat, n),
              grad=vmem(F32, feat, n), project=vmem(BF16, 2, 3 * feat, width), powers=vmem(BF16, 2, pair, HEADS, length, length),
              mixed=vmem(BF16, feat, n), ln2=vmem(F32, 2, feat, 128), middle=vmem(F32, feat, n), act=vmem(BF16, 2, ff, chunk),
              down_t=vmem(BF16, feat, ff), ln1=vmem(F32, 2, feat, 128), d_char=vmem(F32, feat, 128), low_f=vmem(BF16, feat, n),
              gp_f=vmem(BF16, 3 * feat, n), scores=vmem(F32, pair * HEADS, length, length),
              grads=vmem(BF16, pair * HEADS, length, length), grad_mixed=vmem(F32, feat, width), scaled=vmem(BF16, feat, width),
              lean=vmem(F32, seqs, HEADS, length), gn=vmem(F32, feat, width), sems=pltpu.SemaphoreType.DMA((12 + 4 * items + chunks,)))
    parts = 4
    if nz:
        devices = nz * 8
        per, down_per = feat // devices, ff // devices
        blocks = (nz,) + BLOCKS
        call.arg(d_down=there(saved.d_down_o.reshape(blocks + (down_per, feat))), d_out_i=there(saved.d_out_o.reshape(blocks + (per, feat))))
        small_out = lambda *shape: (shape, F32, RESIDENT)
        call.out(o_out=small_out(per, feat), o_down=small_out(down_per, feat), o_qkv=small_out(per, 3 * feat), o_time=small_out(per, feat),
                 o_char=small_out(per, chars), o_ln=small_out(4, per))
        call.temp(down_sums=Scatter.scratch(nz, (down_per, feat)), rest_sums=Scatter.scratch(nz, (per, 128 + feat)),
                  at_sums=Scatter.scratch(nz, (per, feat)) * parts, kept=vmem(BF16, nz, 2, 2, down_per, feat),
                  d_at=[vmem(BF16, *blocks, per, feat)] * parts, d_rest=vmem(BF16, *blocks, per, 128 + feat))
    else:
        call.out(d_at=((feat, 3 * feat), BF16, RESIDENT), d_rest=((feat, 128 + feat), BF16, RESIDENT))

    def kernel(r):
        stream = Stream(r.sems)
        if nz:
            c = place()[3]
            down = Scatter(nz, r.d_down, r.down_sums, r.kept)
            *ats, out = [Scatter(nz, r.d_at[p], r.at_sums[5 * p:5 * p + 5]) for p in range(parts)]
            rest = Scatter(nz, r.d_rest, r.rest_sums)

        def tall(value):
            value = value.astype(BF16)
            return value.reshape(blocks + (per, value.shape[-1])) if nz else value

        def columns(i):
            return block_at(i, width)

        fixed = [(r.out_i, r.w_out), (r.small_i.at[:, pl.ds(0, 128)], r.small), (r.qkv_i, r.qkv), (r.ln2_i, r.ln2), (r.middle_i, r.middle),
                 (r.down_i, r.down_t)]
        if nz:
            fixed += [(r.d_down.at[pl.ds(0, nz), :, :, c], r.kept), (r.d_out_i, r.d_at[3])]

        def fetch(*numbers):
            for k in numbers:
                stream.start(k, *fixed[k])

        def fetched(*numbers):
            for k in numbers:
                stream.wait(k, *fixed[k])

        def item_copies(i):
            cols = columns(i)
            return [(12 + i, r.grad_i.at[:, cols], r.grad.at[:, cols]), (12 + items + i, r.start_i.at[:, cols], r.start.at[:, cols]),
                    (12 + 2 * items + i, r.mixed_i.at[:, cols], r.mixed.at[:, cols]), (8 + i % 2, r.project_i.at[:, cols], r.project.at[i % 2]),
                    (10 + i % 2, r.powers_i.at[pl.ds(i * pair, pair)], r.powers.at[i % 2])]

        def d_in_copy(i):
            return 12 + 3 * items + i, r.start.at[:, columns(i)], r.d_in.at[:, columns(i)]

        def act_copy(m):
            return 8 + m % 2, r.act_i.at[:, block_at(m, chunk)], r.act.at[m % 2]

        def result_copy(m):
            cols = block_at(m, chunk)
            return 12 + 4 * items + m, r.middle.at[:, cols], r.result.at[:, cols]

        def norm_again(i):
            normed, _ = norm_rows(r.start[:, columns(i)])
            r.low_f[:, columns(i)] = (normed * param(r.small[...], chars) + param(r.small[...], chars + 1)).astype(BF16)

        def product(p):
            value = tall(dot_nt(r.low_f[...], r.gp_f[p * feat:(p + 1) * feat, :]))
            if nz:
                r.d_at[p][...] = value
                ats[p].cores()
            else:
                r.d_at[:, p * feat:(p + 1) * feat] = value

        def layer_back(i):
            r.gn[...] = dot(r.qkv[...], r.gp_f[:, columns(i)])
            grad_normed = r.gn[...]
            normed, inverse = norm_rows(r.start[:, columns(i)])
            d_in = r.grad[:, columns(i)] + norm_rows_back(grad_normed, param(r.small[...], chars), normed, inverse)
            r.start[:, columns(i)] = d_in
            stream.start(*d_in_copy(i))
            r.ln1[0] += fold(grad_normed * normed)
            r.ln1[1] += fold(grad_normed)
            one_hot = jnp.concatenate([one_hot_of(r.tok[i * pair + k], i * pair + k) for k in range(pair)], axis=1)
            high = d_in.astype(BF16)
            low = (d_in - high.astype(F32)).astype(BF16)
            r.d_char[...] += dot_nt(high, one_hot) + dot_nt(low, one_hot)

        def rest_products():
            lane = lax.broadcasted_iota(jnp.int32, r.d_char.shape, 1)
            sums = r.d_char[...]
            table = jnp.where(lane < chars, sums, 0.0)
            for k, ref in enumerate((r.ln1.at[0], r.ln1.at[1], r.ln2.at[0], r.ln2.at[1])):
                table = jnp.where(lane == chars + k, jnp.sum(ref[...], axis=1, keepdims=True), table)
            stamps = jnp.concatenate([sums[:, ITEM_HIGH:], sums[:, :ITEM_HIGH]], axis=1)
            stamps = jnp.where(lane < seqs, stamps, 0.0).astype(BF16)
            r.d_rest[..., :128] = tall(table)
            r.d_rest[..., 128:] = tall(dot_nt(r.waves[...], stamps))

        def result(m):
            cols = block_at(m, chunk)
            stream.wait(*act_copy(m))
            r.middle[:, cols] = r.middle[:, cols] + dot(r.down_t[...], r.act[m % 2])
            stream.start(*result_copy(m))

            @pl.when(m + 2 < chunks)
            def _():
                stream.start(*act_copy(m + 2))

        def item(i):
            copies = item_copies(i)
            stream.wait(*copies[0])
            grad_low = r.grad[:, columns(i)].astype(BF16)
            r.grad_mixed[...] = dot(r.w_out[...], grad_low).astype(BF16).astype(F32)
            stream.wait(*copies[1])
            norm_again(i)
            for copy in copies[2:]:
                stream.wait(*copy)
            if nz:
                at_step(i, [[lambda: fetch(6, 7), lambda: greeted(nz), down.cores]])

            @pl.when(i + 1 < items)
            def _():
                for copy in item_copies(i + 1):
                    stream.start(*copy)
            views = []
            for k in range(pair):
                here, number = pl.ds(k * length, length), i * pair + k
                cols, group = block_at(number, length), pl.ds(k * HEADS, HEADS)
                views.append((r.project.at[i % 2, :, here], r.scaled.at[:, here], r.powers.at[i % 2, k], r.scores.at[group], r.grads.at[group], cols))
                heads.scale_grad(r.grad_mixed.at[:, here], r.inv.at[number], r.mixed.at[:, cols], r.scaled.at[:, here], r.lean.at[number])
            for project, scaled, powers, scores, grads, cols in views:
                heads.grad_probs(project, scaled, scores)
            for k, (project, scaled, powers, scores, grads, cols) in enumerate(views):
                heads.grad_scores(powers, scores, r.lean.at[i * pair + k], grads)
                heads.grad_project(project, scaled, powers, grads, r.gp_f, cols)

        if nz:
            greet(nz)
        fetch(0)
        first_copies = item_copies(0)
        stream.start(*first_copies[0])
        fetch(1)
        for copy in first_copies[1:]:
            stream.start(*copy)
        r.ln1[...] = jnp.zeros_like(r.ln1)
        r.d_char[...] = jnp.zeros_like(r.d_char)
        fetched(0, 1)

        def items_loop(i, _):
            item(i)
            if nz:
                at_step(i, [[lambda: fetched(6, 7), down.corners, out.cores], [out.corners], [down.sides, out.sides]])
            return 0
        lax.fori_loop(0, items, items_loop, 0)
        fetch(2, 3, 4, 5)
        for m in range(2):
            stream.start(*act_copy(m))
        product(0)
        product(1)
        if nz:
            ats[0].corners()
        fetched(2)

        def back_loop(i, _):
            layer_back(i)
            if nz:
                at_step(i, [[ats[1].corners, down.lines], [ats[0].sides, out.lines], [ats[1].sides], [ats[0].lines]])
            return 0
        lax.fori_loop(0, items, back_loop, 0)
        fetched(3)
        rest_products()
        fetched(4, 5)
        if nz:
            rest.cores()
        product(2)
        if nz:
            rest.corners()
            ats[1].lines()

        def result_loop(m, _):
            result(m)
            if nz:
                at_step(m, [[ats[2].corners]] + [[]] * (chunks - 4) + [[rest.sides], [ats[2].sides], [rest.lines]])
            return 0
        lax.fori_loop(0, chunks, result_loop, 0)
        if nz:
            r.o_down[...] = down.total()
            r.o_out[...] = out.total()
            for p in range(2):
                r.o_qkv[:, p * feat:(p + 1) * feat] = ats[p].total()
            ats[2].lines()
            total = rest.total()
            r.o_time[...] = total[:, 128:]
            r.o_char[...] = total[:, :chars]
            r.o_ln[...] = total[:, :128].T[chars:chars + 4]
            r.o_qkv[:, 2 * feat:] = ats[2].total()
        for i in range(items):
            stream.wait(*d_in_copy(i))
        for m in range(chunks):
            stream.wait(*result_copy(m))

    return call.run(kernel, "backward", None, 1 if nz else None)


def hand_over(result, d_in, ln, *others, width=1024):
    feat, n = d_in.shape
    call = Call()
    turned = ((n, feat), F32, pl.BlockSpec((width, feat), lambda i: (i, 0)))
    call.arg(result=(result, lanes(feat, width)), d_in=(d_in, lanes(feat, width)), ln=(ln, whole(ln.shape)))
    call.arg(**{f"a{k}": (value, whole(value.shape)) for k, value in enumerate(others)})
    call.out(o_result=turned, o_d_in=turned, **{f"l{k}": ((1, ln.shape[1]), F32, whole((1, ln.shape[1]))) for k in range(4)})
    call.out(**{f"o{k}": (value.shape, F32, whole(value.shape)) for k, value in enumerate(others)})

    def kernel(r):
        r.o_result[...] = r.result[...].T
        r.o_d_in[...] = r.d_in[...].T

        @pl.when(pl.program_id(0) == 0)
        def _():
            for k, ref in enumerate((r.l0, r.l1, r.l2, r.l3)):
                ref[...] = r.ln[k:k + 1]
            for k in range(len(others)):
                getattr(r, f"o{k}")[...] = getattr(r, f"a{k}")[...]

    got = call.run(kernel, "hand_over", n // width)
    return got.o_result, got.o_d_in, [getattr(got, f"l{k}") for k in range(4)], [getattr(got, f"o{k}") for k in range(len(others))]


def make_body(gx, gy):
    def gathered(*shards):
        return [lax.all_gather(s, AXES, axis=0, tiled=True) for s in shards]

    def summed(part):
        return lax.psum_scatter(part.astype(F32), AXES, scatter_dimension=0, tiled=True)

    def body(tokens, timesteps, cotangent, char_table, time_weight, ln1_gain, ln1_bias, w_qkv, w_attn_out, ln2_gain, ln2_bias, w_up, w_down):
        feat = time_weight.shape[1]
        chars = char_table.shape[0]
        per = feat // (gx * gy)
        nz = gx // 2 if gy == 4 and gx % 8 == 0 and per % 16 == 0 else 0
        shards = [char_table.T, ln1_gain, ln1_bias, ln2_gain, ln2_bias, time_weight, w_qkv, w_attn_out, w_up, w_down]
        if not nz:
            shards = gathered(*shards)
        saved = forward(nz, tokens, timesteps, cotangent, *shards)
        if nz:
            small, w_qkv, w_out = (value.reshape(feat, value.shape[-1]) for value in (saved.first_o, saved.qkv_o, saved.out_o))
            got = backward(nz, chars, tokens, small, w_qkv, w_out, saved)
            ln, sums = got.o_ln, (got.o_char, got.o_time, got.o_qkv, got.o_out, saved.o_up, got.o_down)
        else:
            got = backward(nz, chars, tokens, saved.small, *shards[6:8], saved)
            up, down, at, rest = (summed(p) for p in (saved.d_up, saved.d_down_o, got.d_at, got.d_rest))
            ln, sums = rest[:, chars:chars + 4].T, (rest[:, :chars], rest[:, 128:], at, summed(saved.d_out_o), up, down)
        result, d_in, lns, (char, time, qkv, out, up, down) = hand_over(got.result, got.d_in, ln, *sums)
        g1, b1, g2, b2 = (value.reshape(per) for value in lns)
        return result, d_in, char.T, time, g1, b1, qkv, out, g2, b2, up, down
    return body


def solution(mesh):
    every = P(AXES)
    rows, cols = P(AXES, None), P(None, AXES)
    return jax.shard_map(
        make_body(mesh.shape[AXES[0]], mesh.shape[AXES[1]]),
        mesh=mesh,
        in_specs=(every, every, rows, cols, rows, every, every, rows, rows, every, every, rows, rows),
        out_specs=(rows, rows, cols, rows, every, every, rows, rows, every, every, rows, rows),
        check_vma=False,
    )
```

```python
import math
import types

import jax
import jax.numpy as jnp
from jax import lax
from jax.experimental import pallas as pl
from jax.experimental.pallas import tpu as pltpu
from jax.sharding import PartitionSpec as P

F32, BF16 = jnp.float32, jnp.bfloat16
MESH = pl.DeviceIdType.MESH
AXES = ("gx", "gy")
HEADS = 8
EPSILON = 1e-05
VMEM_LIMIT = 63 * 2**20
BLOCKS = (2, 2, 2)
X, Y, CORE = range(3)


def place():
    gx, gy = lax.axis_index(AXES[0]), lax.axis_index(AXES[1])
    return gx // 2, gx % 2, gy // 2, gy % 2


def device(z, x, y, c):
    return (z * 2 + x, y * 2 + c)


def across(axis):
    z, x, y, c = place()
    return ((z, 1 - x, y, c), (z, x, 1 - y, c), (z, x, y, 1 - c))[axis]


def greet(nz):
    z, x, y, c = place()
    barrier = pltpu.get_barrier_semaphore()
    for where in [across(axis) for axis in (X, Y, CORE)] + [((z + d) % nz, x, y, c) for d in range(1, nz)]:
        pl.semaphore_signal(barrier, inc=1, device_id=device(*where), device_id_type=MESH)


def greeted(nz):
    pl.semaphore_wait(pltpu.get_barrier_semaphore(), 3 + nz - 1)


def halves(width):
    middle = width // 256 * 128
    return pl.ds(0, middle), pl.ds(middle, width - middle)


def blocks_of(out, number):
    if number % 4:
        return out.at[pl.ds(0, number), 0, 0, 0]
    return out.at[pl.ds(0, number // 4), :, :, 0]


class Gather:
    LINES, SIDES, CORNERS, CORES = range(4)

    @staticmethod
    def scratch(nz):
        return pltpu.SemaphoreType.DMA((2, 4))

    def __init__(self, nz, shard, out, sems):
        self.nz, self.shard, self.out, self.sems = nz, shard, out, sems
        self.zs, self.count, self.base, self.waits = pl.ds(0, nz), nz, 0, True

    def send(self, src, dst, sent, came, where):
        return pltpu.make_async_remote_copy(
            src_ref=src, dst_ref=dst, send_sem=self.sems.at[0, sent + (self.base if sent else 0)],
            recv_sem=self.sems.at[1, came + (self.base if came else 0)], device_id=device(*where), device_id_type=MESH)

    def some(self, number, stage):
        ref = blocks_of(self.out, number)
        return self.send(ref, ref, stage, stage, across(CORE))

    def pass_on(self, axis, a, b, sent, came, cut=None):
        c = place()[3]
        ref = self.out.at[self.zs, a, b, c]
        if cut is not None:
            ref = ref.at[:, :, cut]
        self.send(ref, ref, sent, came, across(axis)).start()

    def lines(self):
        z, x, y, c = place()
        for d in range(1, self.nz):
            self.send(self.shard, self.out.at[z, x, y, c], self.LINES, self.LINES, ((z + d) % self.nz, x, y, c)).start()

    def arrived(self):
        self.some(self.nz - 1, self.LINES).wait_recv()

    def sides(self):
        _, x, y, _ = place()
        if self.waits:
            self.arrived()
        self.pass_on(X, x, y, self.SIDES, self.SIDES)
        self.pass_on(Y, x, y, self.SIDES, self.SIDES)
        self.pass_on(CORE, x, y, self.SIDES, self.CORES)

    def corners(self):
        _, x, y, _ = place()
        lo, hi = halves(self.out.shape[-1])
        self.some(2 * self.count, self.SIDES).wait_recv()
        self.pass_on(X, x, 1 - y, self.CORNERS, self.CORNERS, lo)
        self.pass_on(Y, 1 - x, y, self.CORNERS, self.CORNERS, hi)
        self.pass_on(CORE, 1 - x, y, self.CORNERS, self.CORES)
        self.pass_on(CORE, x, 1 - y, self.CORNERS, self.CORES)

    def cores(self):
        _, x, y, _ = place()
        self.some(self.count, self.CORNERS).wait_recv()
        self.pass_on(CORE, 1 - x, 1 - y, self.CORES, self.CORES)

    def whole(self):
        self.some(4 * self.count, self.CORES).wait_recv()

    def sent(self):
        self.some(3 * self.count, self.SIDES).wait_send()
        self.some(3 * self.count, self.CORNERS).wait_send()
        self.some(self.count, self.CORES).wait_send()

    def finish(self):
        self.some(self.nz - 1, self.LINES).wait_send()
        self.sent()


class GatherLayers(Gather):
    @staticmethod
    def scratch(nz):
        return pltpu.SemaphoreType.DMA((2, 1 + 3 * nz))

    def layer(self, j):
        one = Gather(self.nz, self.shard, self.out, self.sems)
        one.zs, one.count, one.base, one.waits = pl.ds(j, 1), 1, 3 * j, False
        return one

    def sent(self):
        for j in range(self.nz):
            self.layer(j).sent()


class Scatter:
    @staticmethod
    def scratch(nz, tail):
        return [pltpu.VMEM((nz, 2, 2) + tail, BF16), pltpu.VMEM((nz,) + tail, BF16), pltpu.VMEM((2, nz) + tail, BF16),
                pltpu.VMEM((nz - 1,) + tail, BF16), pltpu.SemaphoreType.DMA((2, 4))]

    def __init__(self, nz, mine, temps, kept=None):
        self.nz, self.mine, self.kept = nz, mine, kept
        self.own, self.far, self.near, self.line, self.sems = temps
        self.width = self.own.shape[-1]

    def send(self, src, dst, stage, where):
        return pltpu.make_async_remote_copy(
            src_ref=src, dst_ref=dst, send_sem=self.sems.at[0, stage], recv_sem=self.sems.at[1, stage],
            device_id=device(*where), device_id_type=MESH)

    def done(self, ref, stage):
        self.send(ref, ref, stage, across(CORE)).wait()

    def add(self, a, b, cols, *values):
        spot = (slice(None), a, b, slice(None), cols)
        total = self.own[spot]
        for value in values:
            total = total + value
        self.own[spot] = total

    def cores(self):
        c = place()[3]
        self.send(self.mine.at[pl.ds(0, self.nz), :, :, 1 - c], self.own, 0, across(CORE)).start()

    def corners(self):
        _, x, y, c = place()
        every, all_z = pl.ds(0, self.width), pl.ds(0, self.nz)
        lo, hi = halves(self.width)
        self.done(self.own, 0)
        for number, (a, b) in enumerate(((1 - x, 1 - y), (1 - x, y), (x, 1 - y), (x, y))):
            self.add(a, b, every, self.mine[:, a, b, c] if self.kept is None else self.kept[:, a, b])
            if number == 0:
                self.send(self.own.at[all_z, 1 - x, 1 - y, :, lo], self.far.at[:, :, lo], 1, across(X)).start()
                self.send(self.own.at[all_z, 1 - x, 1 - y, :, hi], self.far.at[:, :, hi], 1, across(Y)).start()

    def sides(self):
        _, x, y, _ = place()
        all_z = pl.ds(0, self.nz)
        lo, hi = halves(self.width)
        self.done(self.far, 1)
        self.add(x, 1 - y, lo, self.far[:, :, lo])
        self.send(self.own.at[all_z, x, 1 - y], self.near.at[1], 2, across(Y)).start()
        self.add(1 - x, y, hi, self.far[:, :, hi])
        self.send(self.own.at[all_z, 1 - x, y], self.near.at[0], 2, across(X)).start()

    def lines(self):
        z, x, y, c = place()
        self.done(self.near, 2)
        self.add(x, y, pl.ds(0, self.width), self.near[0], self.near[1])
        for d in range(1, self.nz):
            to = (z + d) % self.nz
            self.send(self.own.at[to, x, y], self.line.at[d - 1], 3, (to, x, y, c)).start()

    def total(self):
        z, x, y, _ = place()
        self.done(self.line, 3)
        total = self.own[z, x, y].astype(F32)
        for d in range(1, self.nz):
            total = total + self.line[d - 1].astype(F32)
        return total


class Call:
    def __init__(self):
        self.ins, self.outs, self.temps = {}, {}, {}

    def arg(self, **named):
        self.ins.update(named)

    def out(self, **named):
        self.outs.update(named)

    def temp(self, **named):
        self.temps.update(named)

    def run(self, kernel, name, steps=None, collective=None):
        kinds = [k for kind in self.temps.values() for k in (kind if isinstance(kind, list) else [kind])]

        def body(*refs):
            refs = iter(refs)
            r = types.SimpleNamespace(**{n: next(refs) for n in [*self.ins, *self.outs]})
            for n, kind in self.temps.items():
                setattr(r, n, [next(refs) for _ in kind] if isinstance(kind, list) else next(refs))
            kernel(r)
        extra = {} if collective is None else dict(collective_id=collective, has_side_effects=True)
        got = pl.pallas_call(
            body, grid=() if steps is None else (steps,), in_specs=[spec for _, spec in self.ins.values()], out_specs=[spec for *_, spec in self.outs.values()],
            out_shape=[jax.ShapeDtypeStruct(shape, kind) for shape, kind, _ in self.outs.values()], scratch_shapes=kinds,
            compiler_params=pltpu.CompilerParams(vmem_limit_bytes=VMEM_LIMIT, **extra), name=name,
        )(*[array for array, _ in self.ins.values()])
        return types.SimpleNamespace(**dict(zip(self.outs, got)))


def whole(shape):
    return pl.BlockSpec(tuple(shape), lambda i: (0,) * len(shape))


def lanes(rows, width, at=lambda i: i):
    return pl.BlockSpec((rows, width), lambda i: (0, at(i)))


ANYWHERE = pl.BlockSpec(memory_space=pl.ANY)
RESIDENT = pl.BlockSpec(memory_space=pltpu.VMEM)


def at_step(i, table):
    for step, acts in enumerate(table):
        if acts:
            @pl.when(i == step)
            def _():
                for act in acts:
                    act()


def block_at(i, width):
    return pl.ds(i * width if isinstance(i, int) else pl.multiple_of(i * width, width), width)


def dot(left, right):
    return jnp.dot(left, right, preferred_element_type=F32)


def dot_nt(left, right):
    return lax.dot_general(left, right, (((1,), (1,)), ((), ())), preferred_element_type=F32)


def norm_rows(values):
    count = values.shape[0]
    shifted = values - jnp.sum(values, axis=0, keepdims=True) * (1.0 / count)
    inverse = lax.rsqrt(jnp.sum(shifted * shifted, axis=0, keepdims=True) * (1.0 / count) + EPSILON)
    return shifted * inverse, inverse


def norm_rows_back(grad, gain, normed, inverse):
    count = grad.shape[0]
    scaled = grad * gain
    lean = jnp.sum(scaled, axis=0, keepdims=True) * (1.0 / count)
    turn = jnp.sum(scaled * normed, axis=0, keepdims=True) * (1.0 / count)
    return inverse * (scaled - lean - normed * turn)


def fold(values):
    total = values[:, :128]
    for k in range(1, values.shape[1] // 128):
        total = total + values[:, 128 * k:128 * (k + 1)]
    return total


def flat(ref, cols=slice(None)):
    value = ref[(slice(None),) * (len(ref.shape) - 1) + (cols,)]
    return value.reshape(-1, value.shape[-1])


def param(table, column):
    return table[:, column:column + 1].astype(F32)


def gelu_parts(hidden, grad_active):
    cdf = 0.5 + 0.5 * lax.erf(hidden * math.sqrt(0.5))
    bell = jnp.exp2(hidden * hidden * (-0.5 * math.log2(math.e))) * (1.0 / math.sqrt(2.0 * math.pi))
    return (hidden * cdf).astype(BF16), (grad_active.astype(BF16).astype(F32) * (cdf + hidden * bell)).astype(BF16)


def fill_waves(r, feat):
    half = feat // 2
    r.steps_row[...] = jnp.zeros_like(r.steps_row)
    r.steps_row[:, :r.steps.shape[1]] = r.steps[...].astype(F32)
    rate = jnp.exp(lax.broadcasted_iota(jnp.int32, (half, 128), 0).astype(F32) * (-math.log(10000.0) / half))
    angles = rate * r.steps_row[...]
    r.waves[:half, :] = jnp.sin(angles).astype(BF16)
    r.waves[half:, :] = jnp.cos(angles).astype(BF16)


def fill_small(r, chars):
    count = r.char.shape[0]
    r.square[...] = jnp.zeros_like(r.square)
    for k, ref in enumerate((r.g1, r.b1, r.g2, r.b2)):
        r.square[chars + k:chars + k + 1, :count] = ref[...].astype(F32)
    r.small_shard[...] = r.square[...].T[:count].astype(BF16)
    r.small_shard[:, :chars] = r.char[...]


ITEM_HIGH, ITEM_LOW = 32, 64


def one_hot_of(tok, item):
    row = lax.broadcasted_iota(jnp.int32, (128, tok.shape[1]), 0)
    return ((row == tok) | (row == ITEM_HIGH + item) | (row == ITEM_LOW + item)).astype(BF16)


class Heads:
    def __init__(self, feat):
        self.size = feat // HEADS
        self.q, self.k, self.v = ([pl.ds(part * feat + h * self.size, self.size) for h in range(HEADS)] for part in range(3))

    def scores(self, project, scores):
        for h in range(HEADS):
            scores[h] = dot(project[self.k[h], :].T, project[self.q[h], :])

    def softmax(self, scores, powers, inverses):
        turn = math.log2(math.e) / math.sqrt(self.size)
        for h in range(HEADS):
            value = scores[h]
            power = jnp.exp2((value - jnp.max(value, axis=0, keepdims=True)) * turn)
            inverses[h:h + 1, :] = 1.0 / jnp.sum(power, axis=0, keepdims=True)
            powers[h] = power.astype(BF16)

    def mix(self, project, powers, inverses, mixed):
        for h in range(HEADS):
            mixed[self.q[h], :] = (dot(project[self.v[h], :], powers[h]) * inverses[h:h + 1, :]).astype(BF16)

    def scale_grad(self, grad_mixed, inverses, mixed, scaled, lean):
        for h in range(HEADS):
            value = grad_mixed[self.q[h], :] * inverses[h:h + 1, :]
            lean[h:h + 1, :] = jnp.sum(value * mixed[self.q[h], :].astype(F32), axis=0, keepdims=True)
            scaled[self.q[h], :] = value.astype(BF16)

    def grad_probs(self, project, scaled, scores):
        for h in range(HEADS):
            scores[h] = dot(project[self.v[h], :].T, scaled[self.q[h], :])

    def grad_scores(self, powers, scores, lean, grads):
        for h in range(HEADS):
            grads[h] = (powers[h].astype(F32) * (scores[h] - lean[h:h + 1, :])).astype(BF16)

    def grad_project(self, project, scaled, powers, grads, out, cols):
        scale = 1.0 / math.sqrt(self.size)
        for h in range(HEADS):
            out[self.v[h], cols] = dot_nt(scaled[self.q[h], :], powers[h]).astype(BF16)
            out[self.q[h], cols] = (dot(project[self.k[h], :], grads[h]) * scale).astype(BF16)
            out[self.k[h], cols] = (dot_nt(project[self.q[h], :], grads[h]) * scale).astype(BF16)


class Stream:
    def __init__(self, sems):
        self.sems = sems

    def start(self, number, src, dst):
        pltpu.make_async_copy(src, dst, self.sems.at[number]).start()

    def wait(self, number, src, dst):
        pltpu.make_async_copy(src, dst, self.sems.at[number]).wait()


def forward(nz, tokens, timesteps, cotangent, char, g1, b1, g2, b2, time_w, w_qkv, w_out, w_up, w_down, chunk=512):
    seqs = timesteps.shape[0]
    n = tokens.shape[0]
    length = n // seqs
    feat, ff = time_w.shape[1], w_up.shape[1]
    count, chars = char.shape
    pair = 2 if seqs % 2 == 0 else 1
    items, width = seqs // pair, pair * length
    wide = ff // nz if nz else 512
    tiles, chunks = ff // wide, n // chunk
    share = ff // chunks
    heads = Heads(feat)
    call = Call()
    at_once = lambda value: (value, RESIDENT)
    call.arg(tok=at_once(tokens.reshape(seqs, 1, length)), steps=at_once(timesteps.reshape(1, seqs)), char=at_once(char),
             g1=at_once(g1.reshape(1, count)), b1=at_once(b1.reshape(1, count)), g2=at_once(g2.reshape(1, count)),
             b2=at_once(b2.reshape(1, count)), time_w=at_once(time_w), w_qkv=at_once(w_qkv), w_out=at_once(w_out), w_up=at_once(w_up),
             w_down=at_once(w_down), cot=(cotangent, ANYWHERE))
    call.out(start_o=((feat, n), F32, ANYWHERE), mixed_o=((feat, n), BF16, ANYWHERE), project_o=((3 * feat, n), BF16, ANYWHERE),
             powers_o=((seqs, HEADS, length, length), BF16, ANYWHERE), inv=((seqs, HEADS, length), F32, RESIDENT),
             waves=((feat, 128), BF16, RESIDENT), grad_o=((feat, n), F32, ANYWHERE), ln=((2, feat, 128), F32, RESIDENT),
             d_down_o=((ff, feat), BF16, ANYWHERE), middle_o=((feat, n), F32, ANYWHERE), act_o=((ff, n), BF16, ANYWHERE),
             down_o=((feat, ff), BF16, ANYWHERE), d_out_o=((feat, feat), BF16, ANYWHERE))
    parts = 3
    vmem = lambda kind, *shape: pltpu.VMEM(shape, kind)
    if nz:
        per = feat // (nz * 8)
        blocks = lambda *tail: (nz,) + BLOCKS + tail
        landing = lambda *tail: vmem(BF16, *blocks(*tail))
        sems = Gather.scratch(nz)
        call.temp(first=landing(count, 128 + feat), first_sems=sems, out=landing(count, feat), out_sems=sems,
                  qkv=[landing(count, feat)] * parts, qkv_sems=[sems] * parts, ups=vmem(BF16, tiles, *blocks(count, wide)), up_sems=[sems] * tiles,
                  down=landing(*w_down.shape), down_sems=GatherLayers.scratch(nz), first_shard=vmem(BF16, count, 128 + feat),
                  mine=vmem(BF16, tiles, *blocks(per, wide)), sums=Scatter.scratch(nz, (per, wide)) * tiles)
        call.out(first_o=(blocks(count, 128 + feat), BF16, ANYWHERE), out_o=(blocks(count, feat), BF16, ANYWHERE),
                 qkv_o=(blocks(*w_qkv.shape), BF16, ANYWHERE), o_up=((per, ff), F32, RESIDENT))
    else:
        call.out(small=((count, 128), BF16, RESIDENT), d_up=((feat, ff), BF16, RESIDENT))
    call.temp(small_shard=vmem(BF16, count, 128), square=vmem(F32, 128, max(count, 128)), steps_row=vmem(F32, 1, 128),
              table=vmem(BF16, feat, 128), out_t=vmem(BF16, feat, feat), starts=vmem(F32, feat, n), mixed=vmem(BF16, feat, n),
              powers=vmem(BF16, 2, pair, HEADS, length, length), scores=vmem(F32, pair * HEADS, length, length),
              middle=vmem(F32, feat, n), low2=vmem(BF16, feat, n), cot_t=vmem(BF16, max(n, ff), feat), cot_f=vmem(BF16, feat, n),
              d_out=vmem(BF16, feat, feat), down_t=vmem(BF16, feat, ff), up=vmem(BF16, feat, ff), up_t=vmem(BF16, wide, feat),
              act=vmem(BF16, ff, n), gh=vmem(BF16, ff, n), gn=vmem(F32, feat, chunk), tile_down=vmem(BF16, wide, feat),
              sems=pltpu.SemaphoreType.DMA((15 + 2 * chunks,)))

    def kernel(r):
        proj, low = r.act.at[pl.ds(0, 3 * feat)], r.gh.at[pl.ds(0, feat)]
        stream = Stream(r.sems)
        if nz:
            z, x, y, c = place()
            first = Gather(nz, r.first_shard, r.first, r.first_sems)
            qkv = [Gather(nz, r.w_qkv.at[:, pl.ds(p * feat, feat)], r.qkv[p], r.qkv_sems[p]) for p in range(parts)]
            out = Gather(nz, r.w_out, r.out, r.out_sems)
            ups = [Gather(nz, r.w_up.at[:, pl.ds(j * wide, wide)], r.ups.at[j], r.up_sems[j]) for j in range(tiles)]
            down = GatherLayers(nz, r.w_down, r.down, r.down_sems)
            needs = [(ups[j], down.layer(j)) for j in range(tiles)]
            order = [ups[0], ups[1], needs[0][1], needs[1][1]] + [part for some in needs[2:] for part in some]
            groups = [Scatter(nz, r.mine.at[j], r.sums[5 * j:5 * j + 5]) for j in range(tiles)]

        def small():
            return flat(r.first, slice(0, 128)) if nz else r.small[...]

        def stamps(weights):
            stamp = dot(weights.T, r.waves[...])
            lane = lax.broadcasted_iota(jnp.int32, stamp.shape, 1)
            stamp = jnp.where(lane < seqs, stamp, 0.0)
            high = stamp.astype(BF16)
            rest = (stamp - high.astype(F32)).astype(BF16)
            shift = lambda value, by: jnp.concatenate([value[:, 128 - by:], value[:, :128 - by]], axis=1)
            chars_only = jnp.where(lane < chars, small(), jnp.zeros_like(high))
            r.table[...] = chars_only + shift(high, ITEM_HIGH) + shift(rest, ITEM_LOW)

        def begin(some):
            table = small()
            gain, bias = param(table, chars), param(table, chars + 1)
            for k in some:
                cols = pl.ds(k * length, length)
                start = dot(r.table[...], one_hot_of(r.tok[k], k))
                r.starts[:, cols] = start
                normed, _ = norm_rows(start)
                low[:, cols] = (normed * gain + bias).astype(BF16)

        def multiply(p, weights):
            proj[p * feat:(p + 1) * feat] = dot(weights.T, low[...]).astype(BF16)

        to_hbm = [(proj, r.project_o), (r.starts, r.start_o), (r.mixed, r.mixed_o), (r.middle, r.middle_o), (r.act, r.act_o), (r.down_t, r.down_o)]
        d_out_copy = (14 + 2 * chunks, r.d_out, r.d_out_o)
        if nz:
            every = (pl.ds(0, nz), slice(None), slice(None), slice(None), slice(None))
            to_hbm += [(r.first, r.first_o), (r.out, r.out_o)] + [(g.out, r.qkv_o.at[every + (pl.ds(p * feat, feat),)]) for p, g in enumerate(qkv)]
        cot_in = (11, r.cot, r.cot_t.at[pl.ds(0, n)])

        def leave(*numbers):
            for k in numbers:
                stream.start(k, *to_hbm[k])

        def left(*numbers):
            for k in numbers:
                stream.wait(k, *to_hbm[k])

        def powers_copy(i):
            return 12 + i % 2, r.powers.at[i % 2], r.powers_o.at[pl.ds(i * pair, pair)]

        def grad_copy(m):
            cols = block_at(m, chunk)
            return 14 + m, r.starts.at[:, cols], r.grad_o.at[:, cols]

        def d_down_copy(m):
            rows = block_at(m, share)
            return 14 + chunks + m, r.cot_t.at[rows], r.d_down_o.at[rows]

        def prelude():
            stream.start(*cot_in)
            r.ln[...] = jnp.zeros_like(r.ln)
            if not nz:
                fill_small(r, chars)
                r.small[...] = r.small_shard[...]
                fill_waves(r, feat)
                stamps(r.time_w[...])
                r.out_t[...] = r.w_out[...].T
                begin(range(seqs))
                for p in range(parts):
                    multiply(p, r.w_qkv[:, p * feat:(p + 1) * feat])
                leave(0, 1)
                stream.wait(*cot_in)
                r.cot_f[...] = r.cot_t[:n].T
                return
            greet(nz)
            fill_small(r, chars)
            q, k, v = qkv
            r.first_shard[:, :128] = r.small_shard[...]
            r.first_shard[:, 128:] = r.time_w[...]
            for g in (first, out, q, k, v, *ups, down):
                g.out[z, x, y, c] = g.shard[...]
            stream.wait(*cot_in)
            r.cot_f[...] = r.cot_t[:n].T
            greeted(nz)
            first.lines()
            q.lines()
            k.lines()
            fill_waves(r, feat)
            first.sides()
            v.lines()
            q.sides()
            out.lines()
            k.sides()
            ups[0].lines()
            v.sides()
            first.corners()
            ups[1].lines()
            q.corners()
            down.lines()
            k.corners()
            first.cores()
            first.whole()
            stamps(flat(r.first, slice(128, 128 + feat)))
            v.corners()
            out.sides()
            begin(range(0, seqs // 2))
            q.cores()
            ups[0].sides()
            begin(range(seqs // 2, seqs))
            k.cores()
            q.whole()
            multiply(0, flat(r.qkv[0]))
            v.cores()
            out.corners()
            ups[1].sides()
            for g in ups[2:]:
                g.lines()
            k.whole()
            multiply(1, flat(r.qkv[1]))
            down.arrived()
            needs[0][1].sides()
            v.whole()
            multiply(2, flat(r.qkv[2]))
            ups[0].corners()
            out.cores()
            leave(0, 1)

        def out_weights():
            out.whole()
            r.out_t[...] = flat(r.out).T
            leave(*range(6, 8 + parts))

        def item(i):
            views = []
            for k in range(pair):
                cols = block_at(i * pair + k, length)
                views.append((proj.at[:, cols], r.scores.at[pl.ds(k * HEADS, HEADS)], r.powers.at[i % 2, k], r.inv.at[i * pair + k], r.mixed.at[:, cols]))
            for project, scores, *_ in views:
                heads.scores(project, scores)
            for project, scores, powers, inverses, mixed in views:
                heads.softmax(scores, powers, inverses)
                heads.mix(project, powers, inverses, mixed)
            stream.start(*powers_copy(i))
            if nz:
                at_step(i, [[out_weights]])
            cols = block_at(i, width)
            table = small()
            middle = r.starts[:, cols] + dot(r.out_t[...], r.mixed[:, cols])
            r.middle[:, cols] = middle
            normed, _ = norm_rows(middle)
            r.low2[:, cols] = (normed * param(table, chars + 2) + param(table, chars + 3)).astype(BF16)

        def weights_step(step):
            if not nz:
                return []
            cores = lambda p: (1, 2, 2, 4)[p] if p < 4 else p // 2 + 3
            corners = lambda p: 0 if p < 3 else 3 if p < 5 else p // 4 + 3
            acts = [part.cores for p, part in enumerate(order) if cores(p) == step]
            acts += [part.corners for p, part in enumerate(order) if p > 0 and corners(p) == step]
            return acts + [part.sides for part in order[2 * step + 3:2 * step + 5]]

        def sums_step(step):
            if not nz:
                return []
            return [(g.corners, g.sides, g.lines)[step - j - 1] for j, g in enumerate(groups) if 0 <= step - j - 1 < 3]

        middles, ends = [], []
        if nz:
            middles = [[groups[-1].corners], [groups[-1].sides, groups[-3].lines]]
            ends = [[groups[-2].sides], [groups[-2].lines], [groups[-1].lines]]

        def tile(j):
            rows = block_at(j, wide)
            if nz:
                at_step(j, [[part.whole for part in some] for some in needs])
                r.up[:, rows] = flat(r.ups.at[j])
                r.tile_down[...] = flat(r.down.at[pl.ds(j, 1)])
            else:
                r.up[:, rows] = r.w_up[:, rows]
                r.tile_down[...] = r.w_down[rows, :]
            r.up_t[...] = r.up[:, rows].T
            r.down_t[:, rows] = r.tile_down[...].T
            for t in range(chunks):
                cols = pl.ds(t * chunk, chunk)
                for half in range(2):
                    some = pl.ds(half * wide // 2, wide // 2)
                    part = block_at(2 * j + half, wide // 2)
                    r.act[part, cols], r.gh[part, cols] = gelu_parts(
                        dot(r.up_t[some, :], r.low2[:, cols]), dot(r.tile_down[some, :], r.cot_f[:, cols]))
            at_step(j, [weights_step(items + k) + sums_step(k) for k in range(tiles)])
            d_up = dot_nt(r.low2[...], r.gh[rows, :]).astype(BF16)
            if nz:
                r.mine[j] = d_up.reshape(blocks(per, wide))
                at_step(j, [[g.cores] for g in groups])
            else:
                r.d_up[:, rows] = d_up

        def layer_back(m):
            cols, rows = block_at(m, chunk), block_at(m, share)
            r.gn[...] = dot(r.up[...], r.gh[:, cols])
            at_step(m, middles)
            r.cot_t[rows, :] = dot_nt(r.act[rows, :], r.cot_f[...]).astype(BF16)
            stream.start(*d_down_copy(m))
            normed, inverse = norm_rows(r.middle[:, cols])
            grad_normed = r.gn[...]
            grad = r.cot_f[:, cols].astype(F32) + norm_rows_back(grad_normed, param(small(), chars + 2), normed, inverse)
            r.starts[:, cols] = grad
            r.low2[:, cols] = grad.astype(BF16)
            r.ln[0] += fold(grad_normed * normed)
            r.ln[1] += fold(grad_normed)
            stream.start(*grad_copy(m))

        prelude()

        def items_loop(i, _):
            @pl.when(i >= 2)
            def _():
                stream.wait(*powers_copy(i - 2))
            item(i)
            at_step(i, [weights_step(k) for k in range(items)])
            return 0
        lax.fori_loop(0, items, items_loop, 0)
        left(0, 1)
        leave(2, 3)

        def tiles_loop(j, _):
            tile(j)
            return 0
        lax.fori_loop(0, tiles, tiles_loop, 0)
        leave(4, 5)

        def chunks_loop(m, _):
            layer_back(m)
            at_step(m, ends)
            return 0
        lax.fori_loop(0, chunks, chunks_loop, 0)
        r.d_out[...] = dot_nt(r.mixed[...], r.low2[...]).astype(BF16)
        stream.start(*d_out_copy)
        if nz:
            for g in (first, *qkv, out, *ups, down):
                g.finish()
            for j in range(tiles):
                r.o_up[:, j * wide:(j + 1) * wide] = groups[j].total()
        left(*range(2, len(to_hbm)))
        stream.wait(*d_out_copy)
        for i in range(max(items - 2, 0), items):
            stream.wait(*powers_copy(i))
        for m in range(chunks):
            stream.wait(*d_down_copy(m))
            stream.wait(*grad_copy(m))

    return call.run(kernel, "forward_and_ffn", None, 0 if nz else None)


def backward(nz, chars, tokens, small, w_qkv, w_out, saved, chunk=512):
    feat, n = saved.start_o.shape
    seqs = saved.powers_o.shape[0]
    ff = saved.act_o.shape[0]
    length = n // seqs
    pair = 2 if seqs % 2 == 0 else 1
    items, width, chunks = seqs // pair, pair * length, n // chunk
    heads = Heads(feat)
    vmem = lambda kind, *shape: pltpu.VMEM(shape, kind)
    there = lambda value: (value, ANYWHERE)
    call = Call()
    call.arg(tok=(tokens.reshape(seqs, 1, length), RESIDENT), waves=(saved.waves, RESIDENT), inv=(saved.inv, RESIDENT), small_i=there(small),
             qkv_i=there(w_qkv), out_i=there(w_out), start_i=there(saved.start_o), grad_i=there(saved.grad_o), project_i=there(saved.project_o),
             powers_i=there(saved.powers_o), mixed_i=there(saved.mixed_o), ln2_i=there(saved.ln),
             middle_i=there(saved.middle_o), act_i=there(saved.act_o), down_i=there(saved.down_o))
    call.out(d_in=((feat, n), F32, ANYWHERE), result=((feat, n), F32, ANYWHERE))
    call.temp(small=vmem(BF16, feat, 128), qkv=vmem(BF16, feat, 3 * feat), w_out=vmem(BF16, feat, feat), start=vmem(F32, feat, n),
              grad=vmem(F32, feat, n), project=vmem(BF16, 2, 3 * feat, width), powers=vmem(BF16, 2, pair, HEADS, length, length),
              mixed=vmem(BF16, feat, n), ln2=vmem(F32, 2, feat, 128), middle=vmem(F32, feat, n), act=vmem(BF16, 2, ff, chunk),
              down_t=vmem(BF16, feat, ff), ln1=vmem(F32, 2, feat, 128), d_char=vmem(F32, feat, 128), low_f=vmem(BF16, feat, n),
              gp_f=vmem(BF16, 3 * feat, n), scores=vmem(F32, pair * HEADS, length, length),
              grads=vmem(BF16, pair * HEADS, length, length), grad_mixed=vmem(F32, feat, width), scaled=vmem(BF16, feat, width),
              lean=vmem(F32, seqs, HEADS, length), gn=vmem(F32, feat, width), sems=pltpu.SemaphoreType.DMA((12 + 4 * items + chunks,)))
    parts = 4
    if nz:
        devices = nz * 8
        per, down_per = feat // devices, ff // devices
        blocks = (nz,) + BLOCKS
        call.arg(d_down=there(saved.d_down_o.reshape(blocks + (down_per, feat))), d_out_i=there(saved.d_out_o.reshape(blocks + (per, feat))))
        small_out = lambda *shape: (shape, F32, RESIDENT)
        call.out(o_out=small_out(per, feat), o_down=small_out(down_per, feat), o_qkv=small_out(per, 3 * feat), o_time=small_out(per, feat),
                 o_char=small_out(per, chars), o_ln=small_out(4, per))
        call.temp(down_sums=Scatter.scratch(nz, (down_per, feat)), rest_sums=Scatter.scratch(nz, (per, 128 + feat)),
                  at_sums=Scatter.scratch(nz, (per, feat)) * parts, kept=vmem(BF16, nz, 2, 2, down_per, feat),
                  d_at=[vmem(BF16, *blocks, per, feat)] * parts, d_rest=vmem(BF16, *blocks, per, 128 + feat))
    else:
        call.out(d_at=((feat, 3 * feat), BF16, RESIDENT), d_rest=((feat, 128 + feat), BF16, RESIDENT))

    def kernel(r):
        stream = Stream(r.sems)
        if nz:
            c = place()[3]
            down = Scatter(nz, r.d_down, r.down_sums, r.kept)
            *ats, out = [Scatter(nz, r.d_at[p], r.at_sums[5 * p:5 * p + 5]) for p in range(parts)]
            rest = Scatter(nz, r.d_rest, r.rest_sums)

        def tall(value):
            value = value.astype(BF16)
            return value.reshape(blocks + (per, value.shape[-1])) if nz else value

        def columns(i):
            return block_at(i, width)

        fixed = [(r.out_i, r.w_out), (r.small_i.at[:, pl.ds(0, 128)], r.small), (r.qkv_i, r.qkv), (r.ln2_i, r.ln2), (r.middle_i, r.middle),
                 (r.down_i, r.down_t)]
        if nz:
            fixed += [(r.d_down.at[pl.ds(0, nz), :, :, c], r.kept), (r.d_out_i, r.d_at[3])]

        def fetch(*numbers):
            for k in numbers:
                stream.start(k, *fixed[k])

        def fetched(*numbers):
            for k in numbers:
                stream.wait(k, *fixed[k])

        def item_copies(i):
            cols = columns(i)
            return [(12 + i, r.grad_i.at[:, cols], r.grad.at[:, cols]), (12 + items + i, r.start_i.at[:, cols], r.start.at[:, cols]),
                    (12 + 2 * items + i, r.mixed_i.at[:, cols], r.mixed.at[:, cols]), (8 + i % 2, r.project_i.at[:, cols], r.project.at[i % 2]),
                    (10 + i % 2, r.powers_i.at[pl.ds(i * pair, pair)], r.powers.at[i % 2])]

        def d_in_copy(i):
            return 12 + 3 * items + i, r.start.at[:, columns(i)], r.d_in.at[:, columns(i)]

        def act_copy(m):
            return 8 + m % 2, r.act_i.at[:, block_at(m, chunk)], r.act.at[m % 2]

        def result_copy(m):
            cols = block_at(m, chunk)
            return 12 + 4 * items + m, r.middle.at[:, cols], r.result.at[:, cols]

        def norm_again(i):
            normed, _ = norm_rows(r.start[:, columns(i)])
            r.low_f[:, columns(i)] = (normed * param(r.small[...], chars) + param(r.small[...], chars + 1)).astype(BF16)

        def product(p):
            value = tall(dot_nt(r.low_f[...], r.gp_f[p * feat:(p + 1) * feat, :]))
            if nz:
                r.d_at[p][...] = value
                ats[p].cores()
            else:
                r.d_at[:, p * feat:(p + 1) * feat] = value

        def layer_back(i):
            r.gn[...] = dot(r.qkv[...], r.gp_f[:, columns(i)])
            grad_normed = r.gn[...]
            normed, inverse = norm_rows(r.start[:, columns(i)])
            d_in = r.grad[:, columns(i)] + norm_rows_back(grad_normed, param(r.small[...], chars), normed, inverse)
            r.start[:, columns(i)] = d_in
            stream.start(*d_in_copy(i))
            r.ln1[0] += fold(grad_normed * normed)
            r.ln1[1] += fold(grad_normed)
            one_hot = jnp.concatenate([one_hot_of(r.tok[i * pair + k], i * pair + k) for k in range(pair)], axis=1)
            high = d_in.astype(BF16)
            low = (d_in - high.astype(F32)).astype(BF16)
            r.d_char[...] += dot_nt(high, one_hot) + dot_nt(low, one_hot)

        def rest_products():
            lane = lax.broadcasted_iota(jnp.int32, r.d_char.shape, 1)
            sums = r.d_char[...]
            table = jnp.where(lane < chars, sums, 0.0)
            for k, ref in enumerate((r.ln1.at[0], r.ln1.at[1], r.ln2.at[0], r.ln2.at[1])):
                table = jnp.where(lane == chars + k, jnp.sum(ref[...], axis=1, keepdims=True), table)
            stamps = jnp.concatenate([sums[:, ITEM_HIGH:], sums[:, :ITEM_HIGH]], axis=1)
            stamps = jnp.where(lane < seqs, stamps, 0.0).astype(BF16)
            r.d_rest[..., :128] = tall(table)
            r.d_rest[..., 128:] = tall(dot_nt(r.waves[...], stamps))

        def result(m):
            cols = block_at(m, chunk)
            stream.wait(*act_copy(m))
            r.middle[:, cols] = r.middle[:, cols] + dot(r.down_t[...], r.act[m % 2])
            stream.start(*result_copy(m))

            @pl.when(m + 2 < chunks)
            def _():
                stream.start(*act_copy(m + 2))

        def item(i):
            copies = item_copies(i)
            stream.wait(*copies[0])
            grad_low = r.grad[:, columns(i)].astype(BF16)
            r.grad_mixed[...] = dot(r.w_out[...], grad_low).astype(BF16).astype(F32)
            stream.wait(*copies[1])
            norm_again(i)
            for copy in copies[2:]:
                stream.wait(*copy)
            if nz:
                at_step(i, [[lambda: fetch(6, 7), lambda: greeted(nz), down.cores]])

            @pl.when(i + 1 < items)
            def _():
                for copy in item_copies(i + 1):
                    stream.start(*copy)
            views = []
            for k in range(pair):
                here, number = pl.ds(k * length, length), i * pair + k
                cols, group = block_at(number, length), pl.ds(k * HEADS, HEADS)
                views.append((r.project.at[i % 2, :, here], r.scaled.at[:, here], r.powers.at[i % 2, k], r.scores.at[group], r.grads.at[group], cols))
                heads.scale_grad(r.grad_mixed.at[:, here], r.inv.at[number], r.mixed.at[:, cols], r.scaled.at[:, here], r.lean.at[number])
            for project, scaled, powers, scores, grads, cols in views:
                heads.grad_probs(project, scaled, scores)
            for k, (project, scaled, powers, scores, grads, cols) in enumerate(views):
                heads.grad_scores(powers, scores, r.lean.at[i * pair + k], grads)
                heads.grad_project(project, scaled, powers, grads, r.gp_f, cols)

        if nz:
            greet(nz)
        fetch(0)
        first_copies = item_copies(0)
        stream.start(*first_copies[0])
        fetch(1)
        for copy in first_copies[1:]:
            stream.start(*copy)
        r.ln1[...] = jnp.zeros_like(r.ln1)
        r.d_char[...] = jnp.zeros_like(r.d_char)
        fetched(0, 1)

        def items_loop(i, _):
            item(i)
            if nz:
                at_step(i, [[lambda: fetched(6, 7), down.corners, out.cores], [out.corners], [down.sides, out.sides]])
            return 0
        lax.fori_loop(0, items, items_loop, 0)
        fetch(2, 3, 4, 5)
        for m in range(2):
            stream.start(*act_copy(m))
        product(0)
        product(1)
        if nz:
            ats[0].corners()
        fetched(2)

        def back_loop(i, _):
            layer_back(i)
            if nz:
                at_step(i, [[ats[1].corners, down.lines], [ats[0].sides, out.lines], [ats[1].sides], [ats[0].lines]])
            return 0
        lax.fori_loop(0, items, back_loop, 0)
        fetched(3)
        rest_products()
        fetched(4, 5)
        if nz:
            rest.cores()
        product(2)
        if nz:
            rest.corners()
            ats[1].lines()

        def result_loop(m, _):
            result(m)
            if nz:
                at_step(m, [[ats[2].corners]] + [[]] * (chunks - 4) + [[rest.sides], [ats[2].sides], [rest.lines]])
            return 0
        lax.fori_loop(0, chunks, result_loop, 0)
        if nz:
            r.o_down[...] = down.total()
            r.o_out[...] = out.total()
            for p in range(2):
                r.o_qkv[:, p * feat:(p + 1) * feat] = ats[p].total()
            ats[2].lines()
            total = rest.total()
            r.o_time[...] = total[:, 128:]
            r.o_char[...] = total[:, :chars]
            r.o_ln[...] = total[:, :128].T[chars:chars + 4]
            r.o_qkv[:, 2 * feat:] = ats[2].total()
        for i in range(items):
            stream.wait(*d_in_copy(i))
        for m in range(chunks):
            stream.wait(*result_copy(m))

    return call.run(kernel, "backward", None, 1 if nz else None)


def hand_over(result, d_in, ln, *others, width=1024):
    feat, n = d_in.shape
    call = Call()
    turned = ((n, feat), F32, pl.BlockSpec((width, feat), lambda i: (i, 0)))
    call.arg(result=(result, lanes(feat, width)), d_in=(d_in, lanes(feat, width)), ln=(ln, whole(ln.shape)))
    call.arg(**{f"a{k}": (value, whole(value.shape)) for k, value in enumerate(others)})
    call.out(o_result=turned, o_d_in=turned, **{f"l{k}": ((1, ln.shape[1]), F32, whole((1, ln.shape[1]))) for k in range(4)})
    call.out(**{f"o{k}": (value.shape, F32, whole(value.shape)) for k, value in enumerate(others)})

    def kernel(r):
        r.o_result[...] = r.result[...].T
        r.o_d_in[...] = r.d_in[...].T

        @pl.when(pl.program_id(0) == 0)
        def _():
            for k, ref in enumerate((r.l0, r.l1, r.l2, r.l3)):
                ref[...] = r.ln[k:k + 1]
            for k in range(len(others)):
                getattr(r, f"o{k}")[...] = getattr(r, f"a{k}")[...]

    got = call.run(kernel, "hand_over", n // width)
    return got.o_result, got.o_d_in, [getattr(got, f"l{k}") for k in range(4)], [getattr(got, f"o{k}") for k in range(len(others))]


def make_body(gx, gy):
    def gathered(*shards):
        return [lax.all_gather(s, AXES, axis=0, tiled=True) for s in shards]

    def summed(part):
        return lax.psum_scatter(part.astype(F32), AXES, scatter_dimension=0, tiled=True)

    def body(tokens, timesteps, cotangent, char_table, time_weight, ln1_gain, ln1_bias, w_qkv, w_attn_out, ln2_gain, ln2_bias, w_up, w_down):
        feat = time_weight.shape[1]
        chars = char_table.shape[0]
        per = feat // (gx * gy)
        nz = gx // 2 if gy == 4 and gx % 8 == 0 and per % 16 == 0 else 0
        shards = [char_table.T, ln1_gain, ln1_bias, ln2_gain, ln2_bias, time_weight, w_qkv, w_attn_out, w_up, w_down]
        if not nz:
            shards = gathered(*shards)
        saved = forward(nz, tokens, timesteps, cotangent, *shards)
        if nz:
            small, w_qkv, w_out = (value.reshape(feat, value.shape[-1]) for value in (saved.first_o, saved.qkv_o, saved.out_o))
            got = backward(nz, chars, tokens, small, w_qkv, w_out, saved)
            ln, sums = got.o_ln, (got.o_char, got.o_time, got.o_qkv, got.o_out, saved.o_up, got.o_down)
        else:
            got = backward(nz, chars, tokens, saved.small, *shards[6:8], saved)
            up, down, at, rest = (summed(p) for p in (saved.d_up, saved.d_down_o, got.d_at, got.d_rest))
            ln, sums = rest[:, chars:chars + 4].T, (rest[:, :chars], rest[:, 128:], at, summed(saved.d_out_o), up, down)
        result, d_in, lns, (char, time, qkv, out, up, down) = hand_over(got.result, got.d_in, ln, *sums)
        g1, b1, g2, b2 = (value.reshape(per) for value in lns)
        return result, d_in, char.T, time, g1, b1, qkv, out, g2, b2, up, down
    return body


def solution(mesh):
    every = P(AXES)
    rows, cols = P(AXES, None), P(None, AXES)
    return jax.shard_map(
        make_body(mesh.shape[AXES[0]], mesh.shape[AXES[1]]),
        mesh=mesh,
        in_specs=(every, every, rows, cols, rows, every, every, rows, rows, every, every, rows, rows),
        out_specs=(rows, rows, cols, rows, every, every, rows, rows, every, every, rows, rows),
        check_vma=False,
    )
```

```python
import math
import types

import jax
import jax.numpy as jnp
from jax import lax
from jax.experimental import pallas as pl
from jax.experimental.pallas import tpu as pltpu
from jax.sharding import PartitionSpec as P

F32, BF16 = jnp.float32, jnp.bfloat16
MESH = pl.DeviceIdType.MESH
AXES = ("gx", "gy")
HEADS = 8
EPSILON = 1e-05
VMEM_LIMIT = 63 * 2**20
BLOCKS = (2, 2, 2)
X, Y, CORE = range(3)


def place():
    gx, gy = lax.axis_index(AXES[0]), lax.axis_index(AXES[1])
    return gx // 2, gx % 2, gy // 2, gy % 2


def device(z, x, y, c):
    return (z * 2 + x, y * 2 + c)


def across(axis):
    z, x, y, c = place()
    return ((z, 1 - x, y, c), (z, x, 1 - y, c), (z, x, y, 1 - c))[axis]


def greet(nz):
    z, x, y, c = place()
    barrier = pltpu.get_barrier_semaphore()
    for where in [across(axis) for axis in (X, Y, CORE)] + [((z + d) % nz, x, y, c) for d in range(1, nz)]:
        pl.semaphore_signal(barrier, inc=1, device_id=device(*where), device_id_type=MESH)


def greeted(nz):
    pl.semaphore_wait(pltpu.get_barrier_semaphore(), 3 + nz - 1)


def halves(width):
    middle = width // 256 * 128
    return pl.ds(0, middle), pl.ds(middle, width - middle)


def blocks_of(out, number):
    if number % 4:
        return out.at[pl.ds(0, number), 0, 0, 0]
    return out.at[pl.ds(0, number // 4), :, :, 0]


class Gather:
    LINES, SIDES, CORNERS, CORES = range(4)

    @staticmethod
    def scratch(nz):
        return pltpu.SemaphoreType.DMA((2, 4))

    def __init__(self, nz, shard, out, sems):
        self.nz, self.shard, self.out, self.sems = nz, shard, out, sems
        self.zs, self.count, self.base, self.waits = pl.ds(0, nz), nz, 0, True

    def send(self, src, dst, sent, came, where):
        return pltpu.make_async_remote_copy(
            src_ref=src, dst_ref=dst, send_sem=self.sems.at[0, sent + (self.base if sent else 0)],
            recv_sem=self.sems.at[1, came + (self.base if came else 0)], device_id=device(*where), device_id_type=MESH)

    def some(self, number, stage):
        ref = blocks_of(self.out, number)
        return self.send(ref, ref, stage, stage, across(CORE))

    def pass_on(self, axis, a, b, sent, came, cut=None):
        c = place()[3]
        ref = self.out.at[self.zs, a, b, c]
        if cut is not None:
            ref = ref.at[:, :, cut]
        self.send(ref, ref, sent, came, across(axis)).start()

    def lines(self):
        z, x, y, c = place()
        for d in range(1, self.nz):
            self.send(self.shard, self.out.at[z, x, y, c], self.LINES, self.LINES, ((z + d) % self.nz, x, y, c)).start()

    def arrived(self):
        self.some(self.nz - 1, self.LINES).wait_recv()

    def sides(self):
        _, x, y, _ = place()
        if self.waits:
            self.arrived()
        self.pass_on(X, x, y, self.SIDES, self.SIDES)
        self.pass_on(Y, x, y, self.SIDES, self.SIDES)
        self.pass_on(CORE, x, y, self.SIDES, self.CORES)

    def corners(self):
        _, x, y, _ = place()
        lo, hi = halves(self.out.shape[-1])
        self.some(2 * self.count, self.SIDES).wait_recv()
        self.pass_on(X, x, 1 - y, self.CORNERS, self.CORNERS, lo)
        self.pass_on(Y, 1 - x, y, self.CORNERS, self.CORNERS, hi)
        self.pass_on(CORE, 1 - x, y, self.CORNERS, self.CORES)
        self.pass_on(CORE, x, 1 - y, self.CORNERS, self.CORES)

    def cores(self):
        _, x, y, _ = place()
        self.some(self.count, self.CORNERS).wait_recv()
        self.pass_on(CORE, 1 - x, 1 - y, self.CORES, self.CORES)

    def whole(self):
        self.some(4 * self.count, self.CORES).wait_recv()

    def sent(self):
        self.some(3 * self.count, self.SIDES).wait_send()
        self.some(3 * self.count, self.CORNERS).wait_send()
        self.some(self.count, self.CORES).wait_send()

    def finish(self):
        self.some(self.nz - 1, self.LINES).wait_send()
        self.sent()


class GatherLayers(Gather):
    @staticmethod
    def scratch(nz):
        return pltpu.SemaphoreType.DMA((2, 1 + 3 * nz))

    def layer(self, j):
        one = Gather(self.nz, self.shard, self.out, self.sems)
        one.zs, one.count, one.base, one.waits = pl.ds(j, 1), 1, 3 * j, False
        return one

    def sent(self):
        for j in range(self.nz):
            self.layer(j).sent()


class Scatter:
    @staticmethod
    def scratch(nz, tail):
        return [pltpu.VMEM((nz, 2, 2) + tail, BF16), pltpu.VMEM((nz,) + tail, BF16), pltpu.VMEM((2, nz) + tail, BF16),
                pltpu.VMEM((nz - 1,) + tail, BF16), pltpu.SemaphoreType.DMA((2, 4))]

    def __init__(self, nz, mine, temps, kept=None):
        self.nz, self.mine, self.kept = nz, mine, kept
        self.own, self.far, self.near, self.line, self.sems = temps
        self.width = self.own.shape[-1]

    def send(self, src, dst, stage, where):
        return pltpu.make_async_remote_copy(
            src_ref=src, dst_ref=dst, send_sem=self.sems.at[0, stage], recv_sem=self.sems.at[1, stage],
            device_id=device(*where), device_id_type=MESH)

    def done(self, ref, stage):
        self.send(ref, ref, stage, across(CORE)).wait()

    def add(self, a, b, cols, *values):
        spot = (slice(None), a, b, slice(None), cols)
        total = self.own[spot]
        for value in values:
            total = total + value
        self.own[spot] = total

    def cores(self):
        c = place()[3]
        self.send(self.mine.at[pl.ds(0, self.nz), :, :, 1 - c], self.own, 0, across(CORE)).start()

    def corners(self):
        _, x, y, c = place()
        every, all_z = pl.ds(0, self.width), pl.ds(0, self.nz)
        lo, hi = halves(self.width)
        self.done(self.own, 0)
        for number, (a, b) in enumerate(((1 - x, 1 - y), (1 - x, y), (x, 1 - y), (x, y))):
            self.add(a, b, every, self.mine[:, a, b, c] if self.kept is None else self.kept[:, a, b])
            if number == 0:
                self.send(self.own.at[all_z, 1 - x, 1 - y, :, lo], self.far.at[:, :, lo], 1, across(X)).start()
                self.send(self.own.at[all_z, 1 - x, 1 - y, :, hi], self.far.at[:, :, hi], 1, across(Y)).start()

    def sides(self):
        _, x, y, _ = place()
        all_z = pl.ds(0, self.nz)
        lo, hi = halves(self.width)
        self.done(self.far, 1)
        self.add(x, 1 - y, lo, self.far[:, :, lo])
        self.send(self.own.at[all_z, x, 1 - y], self.near.at[1], 2, across(Y)).start()
        self.add(1 - x, y, hi, self.far[:, :, hi])
        self.send(self.own.at[all_z, 1 - x, y], self.near.at[0], 2, across(X)).start()

    def lines(self):
        z, x, y, c = place()
        self.done(self.near, 2)
        self.add(x, y, pl.ds(0, self.width), self.near[0], self.near[1])
        for d in range(1, self.nz):
            to = (z + d) % self.nz
            self.send(self.own.at[to, x, y], self.line.at[d - 1], 3, (to, x, y, c)).start()

    def total(self):
        z, x, y, _ = place()
        self.done(self.line, 3)
        total = self.own[z, x, y].astype(F32)
        for d in range(1, self.nz):
            total = total + self.line[d - 1].astype(F32)
        return total


class Call:
    def __init__(self):
        self.ins, self.outs, self.temps = {}, {}, {}

    def arg(self, **named):
        self.ins.update(named)

    def out(self, **named):
        self.outs.update(named)

    def temp(self, **named):
        self.temps.update(named)

    def run(self, kernel, name, steps=None, collective=None):
        kinds = [k for kind in self.temps.values() for k in (kind if isinstance(kind, list) else [kind])]

        def body(*refs):
            refs = iter(refs)
            r = types.SimpleNamespace(**{n: next(refs) for n in [*self.ins, *self.outs]})
            for n, kind in self.temps.items():
                setattr(r, n, [next(refs) for _ in kind] if isinstance(kind, list) else next(refs))
            kernel(r)
        extra = {} if collective is None else dict(collective_id=collective, has_side_effects=True)
        got = pl.pallas_call(
            body, grid=() if steps is None else (steps,), in_specs=[spec for _, spec in self.ins.values()], out_specs=[spec for *_, spec in self.outs.values()],
            out_shape=[jax.ShapeDtypeStruct(shape, kind) for shape, kind, _ in self.outs.values()], scratch_shapes=kinds,
            compiler_params=pltpu.CompilerParams(vmem_limit_bytes=VMEM_LIMIT, **extra), name=name,
        )(*[array for array, _ in self.ins.values()])
        return types.SimpleNamespace(**dict(zip(self.outs, got)))


def whole(shape):
    return pl.BlockSpec(tuple(shape), lambda i: (0,) * len(shape))


def lanes(rows, width, at=lambda i: i):
    return pl.BlockSpec((rows, width), lambda i: (0, at(i)))


ANYWHERE = pl.BlockSpec(memory_space=pl.ANY)
RESIDENT = pl.BlockSpec(memory_space=pltpu.VMEM)


def at_step(i, table):
    for step, acts in enumerate(table):
        if acts:
            @pl.when(i == step)
            def _():
                for act in acts:
                    act()


def block_at(i, width):
    return pl.ds(i * width if isinstance(i, int) else pl.multiple_of(i * width, width), width)


def dot(left, right):
    return jnp.dot(left, right, preferred_element_type=F32)


def dot_nt(left, right):
    return lax.dot_general(left, right, (((1,), (1,)), ((), ())), preferred_element_type=F32)


def norm_rows(values):
    count = values.shape[0]
    shifted = values - jnp.sum(values, axis=0, keepdims=True) * (1.0 / count)
    inverse = lax.rsqrt(jnp.sum(shifted * shifted, axis=0, keepdims=True) * (1.0 / count) + EPSILON)
    return shifted * inverse, inverse


def norm_rows_back(grad, gain, normed, inverse):
    count = grad.shape[0]
    scaled = grad * gain
    lean = jnp.sum(scaled, axis=0, keepdims=True) * (1.0 / count)
    turn = jnp.sum(scaled * normed, axis=0, keepdims=True) * (1.0 / count)
    return inverse * (scaled - lean - normed * turn)


def fold(values):
    total = values[:, :128]
    for k in range(1, values.shape[1] // 128):
        total = total + values[:, 128 * k:128 * (k + 1)]
    return total


def flat(ref, cols=slice(None)):
    value = ref[(slice(None),) * (len(ref.shape) - 1) + (cols,)]
    return value.reshape(-1, value.shape[-1])


def param(table, column):
    return table[:, column:column + 1].astype(F32)


def gelu_parts(hidden, grad_active):
    cdf = 0.5 + 0.5 * lax.erf(hidden * math.sqrt(0.5))
    bell = jnp.exp2(hidden * hidden * (-0.5 * math.log2(math.e))) * (1.0 / math.sqrt(2.0 * math.pi))
    return (hidden * cdf).astype(BF16), (grad_active.astype(BF16).astype(F32) * (cdf + hidden * bell)).astype(BF16)


def fill_waves(r, feat):
    half = feat // 2
    r.steps_row[...] = jnp.zeros_like(r.steps_row)
    r.steps_row[:, :r.steps.shape[1]] = r.steps[...].astype(F32)
    rate = jnp.exp(lax.broadcasted_iota(jnp.int32, (half, 128), 0).astype(F32) * (-math.log(10000.0) / half))
    angles = rate * r.steps_row[...]
    r.waves[:half, :] = jnp.sin(angles).astype(BF16)
    r.waves[half:, :] = jnp.cos(angles).astype(BF16)


def fill_small(r, chars):
    count = r.char.shape[0]
    r.square[...] = jnp.zeros_like(r.square)
    for k, ref in enumerate((r.g1, r.b1, r.g2, r.b2)):
        r.square[chars + k:chars + k + 1, :count] = ref[...].astype(F32)
    r.small_shard[...] = r.square[...].T[:count].astype(BF16)
    r.small_shard[:, :chars] = r.char[...]


ITEM_HIGH, ITEM_LOW = 32, 64


def one_hot_of(tok, item):
    row = lax.broadcasted_iota(jnp.int32, (128, tok.shape[1]), 0)
    return ((row == tok) | (row == ITEM_HIGH + item) | (row == ITEM_LOW + item)).astype(BF16)


class Heads:
    def __init__(self, feat):
        self.size = feat // HEADS
        self.q, self.k, self.v = ([pl.ds(part * feat + h * self.size, self.size) for h in range(HEADS)] for part in range(3))

    def scores(self, project, scores):
        for h in range(HEADS):
            scores[h] = dot(project[self.k[h], :].T, project[self.q[h], :])

    def softmax(self, scores, powers, inverses):
        turn = math.log2(math.e) / math.sqrt(self.size)
        for h in range(HEADS):
            value = scores[h]
            power = jnp.exp2((value - jnp.max(value, axis=0, keepdims=True)) * turn)
            inverses[h:h + 1, :] = 1.0 / jnp.sum(power, axis=0, keepdims=True)
            powers[h] = power.astype(BF16)

    def mix(self, project, powers, inverses, mixed):
        for h in range(HEADS):
            mixed[self.q[h], :] = (dot(project[self.v[h], :], powers[h]) * inverses[h:h + 1, :]).astype(BF16)

    def scale_grad(self, grad_mixed, inverses, mixed, scaled, lean):
        for h in range(HEADS):
            value = grad_mixed[self.q[h], :] * inverses[h:h + 1, :]
            lean[h:h + 1, :] = jnp.sum(value * mixed[self.q[h], :].astype(F32), axis=0, keepdims=True)
            scaled[self.q[h], :] = value.astype(BF16)

    def grad_probs(self, project, scaled, scores):
        for h in range(HEADS):
            scores[h] = dot(project[self.v[h], :].T, scaled[self.q[h], :])

    def grad_scores(self, powers, scores, lean, grads):
        for h in range(HEADS):
            grads[h] = (powers[h].astype(F32) * (scores[h] - lean[h:h + 1, :])).astype(BF16)

    def grad_project(self, project, scaled, powers, grads, out, cols):
        scale = 1.0 / math.sqrt(self.size)
        for h in range(HEADS):
            out[self.v[h], cols] = dot_nt(scaled[self.q[h], :], powers[h]).astype(BF16)
            out[self.q[h], cols] = (dot(project[self.k[h], :], grads[h]) * scale).astype(BF16)
            out[self.k[h], cols] = (dot_nt(project[self.q[h], :], grads[h]) * scale).astype(BF16)


class Stream:
    def __init__(self, sems):
        self.sems = sems

    def start(self, number, src, dst):
        pltpu.make_async_copy(src, dst, self.sems.at[number]).start()

    def wait(self, number, src, dst):
        pltpu.make_async_copy(src, dst, self.sems.at[number]).wait()


def forward(nz, tokens, timesteps, cotangent, char, g1, b1, g2, b2, time_w, w_qkv, w_out, w_up, w_down, chunk=512):
    seqs = timesteps.shape[0]
    n = tokens.shape[0]
    length = n // seqs
    feat, ff = time_w.shape[1], w_up.shape[1]
    count, chars = char.shape
    pair = 2 if seqs % 2 == 0 else 1
    items, width = seqs // pair, pair * length
    wide = ff // nz if nz else 512
    tiles, chunks = ff // wide, n // chunk
    share = ff // chunks
    heads = Heads(feat)
    call = Call()
    at_once = lambda value: (value, RESIDENT)
    call.arg(tok=at_once(tokens.reshape(seqs, 1, length)), steps=at_once(timesteps.reshape(1, seqs)), char=at_once(char),
             g1=at_once(g1.reshape(1, count)), b1=at_once(b1.reshape(1, count)), g2=at_once(g2.reshape(1, count)),
             b2=at_once(b2.reshape(1, count)), time_w=at_once(time_w), w_qkv=at_once(w_qkv), w_out=at_once(w_out), w_up=at_once(w_up),
             w_down=at_once(w_down), cot=(cotangent, ANYWHERE))
    call.out(start_o=((feat, n), F32, ANYWHERE), mixed_o=((feat, n), BF16, ANYWHERE), project_o=((3 * feat, n), BF16, ANYWHERE),
             powers_o=((seqs, HEADS, length, length), BF16, ANYWHERE), inv=((seqs, HEADS, length), F32, RESIDENT),
             waves=((feat, 128), BF16, RESIDENT), grad_o=((feat, n), F32, ANYWHERE), ln_o=((2, feat, 128), F32, ANYWHERE),
             d_down_o=((ff, feat), BF16, ANYWHERE), middle_o=((feat, n), F32, ANYWHERE), act_o=((ff, n), BF16, ANYWHERE),
             down_o=((feat, ff), BF16, ANYWHERE), d_out_o=((feat, feat), BF16, ANYWHERE))
    parts = 3
    vmem = lambda kind, *shape: pltpu.VMEM(shape, kind)
    if nz:
        per = feat // (nz * 8)
        blocks = lambda *tail: (nz,) + BLOCKS + tail
        landing = lambda *tail: vmem(BF16, *blocks(*tail))
        sems = Gather.scratch(nz)
        call.temp(first=landing(count, 128 + feat), first_sems=sems, out=landing(count, feat), out_sems=sems,
                  qkv=[landing(count, feat)] * parts, qkv_sems=[sems] * parts, ups=vmem(BF16, tiles, *blocks(count, wide)), up_sems=[sems] * tiles,
                  down=landing(*w_down.shape), down_sems=GatherLayers.scratch(nz), first_shard=vmem(BF16, count, 128 + feat),
                  mine=vmem(BF16, tiles, *blocks(per, wide)), sums=Scatter.scratch(nz, (per, wide)) * tiles)
        call.out(first_o=(blocks(count, 128 + feat), BF16, ANYWHERE), out_o=(blocks(count, feat), BF16, ANYWHERE),
                 qkv_o=(blocks(*w_qkv.shape), BF16, ANYWHERE), o_up=((per, ff), F32, RESIDENT))
    else:
        call.out(small=((count, 128), BF16, RESIDENT), d_up=((feat, ff), BF16, RESIDENT))
    call.temp(ln=vmem(F32, 2, feat, 128), small_shard=vmem(BF16, count, 128), square=vmem(F32, 128, max(count, 128)), steps_row=vmem(F32, 1, 128),
              table=vmem(BF16, feat, 128), out_t=vmem(BF16, feat, feat), starts=vmem(F32, feat, n), mixed=vmem(BF16, feat, n),
              powers=vmem(BF16, 2, pair, HEADS, length, length), scores=vmem(F32, pair * HEADS, length, length),
              middle=vmem(F32, feat, n), low2=vmem(BF16, feat, n), cot_t=vmem(BF16, max(n, ff), feat), cot_f=vmem(BF16, feat, n),
              d_out=vmem(BF16, feat, feat), down_t=vmem(BF16, feat, ff), up=vmem(BF16, feat, ff), up_t=vmem(BF16, wide, feat),
              act=vmem(BF16, ff, n), gh=vmem(BF16, ff, n), gn=vmem(F32, feat, chunk), tile_down=vmem(BF16, wide, feat),
              sems=pltpu.SemaphoreType.DMA((16 + 2 * chunks,)))

    def kernel(r):
        proj, low = r.act.at[pl.ds(0, 3 * feat)], r.gh.at[pl.ds(0, feat)]
        stream = Stream(r.sems)
        if nz:
            z, x, y, c = place()
            first = Gather(nz, r.first_shard, r.first, r.first_sems)
            qkv = [Gather(nz, r.w_qkv.at[:, pl.ds(p * feat, feat)], r.qkv[p], r.qkv_sems[p]) for p in range(parts)]
            out = Gather(nz, r.w_out, r.out, r.out_sems)
            ups = [Gather(nz, r.w_up.at[:, pl.ds(j * wide, wide)], r.ups.at[j], r.up_sems[j]) for j in range(tiles)]
            down = GatherLayers(nz, r.w_down, r.down, r.down_sems)
            needs = [(ups[j], down.layer(j)) for j in range(tiles)]
            order = [ups[0], ups[1], needs[0][1], needs[1][1]] + [part for some in needs[2:] for part in some]
            groups = [Scatter(nz, r.mine.at[j], r.sums[5 * j:5 * j + 5]) for j in range(tiles)]

        def small():
            return flat(r.first, slice(0, 128)) if nz else r.small[...]

        def stamps(weights):
            stamp = dot(weights.T, r.waves[...])
            lane = lax.broadcasted_iota(jnp.int32, stamp.shape, 1)
            stamp = jnp.where(lane < seqs, stamp, 0.0)
            high = stamp.astype(BF16)
            rest = (stamp - high.astype(F32)).astype(BF16)
            shift = lambda value, by: jnp.concatenate([value[:, 128 - by:], value[:, :128 - by]], axis=1)
            chars_only = jnp.where(lane < chars, small(), jnp.zeros_like(high))
            r.table[...] = chars_only + shift(high, ITEM_HIGH) + shift(rest, ITEM_LOW)

        def begin(some):
            table = small()
            gain, bias = param(table, chars), param(table, chars + 1)
            for k in some:
                cols = pl.ds(k * length, length)
                start = dot(r.table[...], one_hot_of(r.tok[k], k))
                r.starts[:, cols] = start
                normed, _ = norm_rows(start)
                low[:, cols] = (normed * gain + bias).astype(BF16)

        def multiply(p, weights):
            proj[p * feat:(p + 1) * feat] = dot(weights.T, low[...]).astype(BF16)

        to_hbm = [(proj, r.project_o), (r.starts, r.start_o), (r.mixed, r.mixed_o), (r.middle, r.middle_o), (r.act, r.act_o), (r.down_t, r.down_o)]
        d_out_copy = (14 + 2 * chunks, r.d_out, r.d_out_o)
        ln_copy = (15 + 2 * chunks, r.ln, r.ln_o)
        if nz:
            every = (pl.ds(0, nz), slice(None), slice(None), slice(None), slice(None))
            to_hbm += [(r.first, r.first_o), (r.out, r.out_o)] + [(g.out, r.qkv_o.at[every + (pl.ds(p * feat, feat),)]) for p, g in enumerate(qkv)]
        cot_in = (11, r.cot, r.cot_t.at[pl.ds(0, n)])

        def leave(*numbers):
            for k in numbers:
                stream.start(k, *to_hbm[k])

        def left(*numbers):
            for k in numbers:
                stream.wait(k, *to_hbm[k])

        def powers_copy(i):
            return 12 + i % 2, r.powers.at[i % 2], r.powers_o.at[pl.ds(i * pair, pair)]

        def grad_copy(m):
            cols = block_at(m, chunk)
            return 14 + m, r.starts.at[:, cols], r.grad_o.at[:, cols]

        def d_down_copy(m):
            rows = block_at(m, share)
            return 14 + chunks + m, r.cot_t.at[rows], r.d_down_o.at[rows]

        def prelude():
            stream.start(*cot_in)
            r.ln[...] = jnp.zeros_like(r.ln)
            if not nz:
                fill_small(r, chars)
                r.small[...] = r.small_shard[...]
                fill_waves(r, feat)
                stamps(r.time_w[...])
                r.out_t[...] = r.w_out[...].T
                begin(range(seqs))
                for p in range(parts):
                    multiply(p, r.w_qkv[:, p * feat:(p + 1) * feat])
                leave(0, 1)
                stream.wait(*cot_in)
                r.cot_f[...] = r.cot_t[:n].T
                return
            greet(nz)
            fill_small(r, chars)
            q, k, v = qkv
            r.first_shard[:, :128] = r.small_shard[...]
            r.first_shard[:, 128:] = r.time_w[...]
            for g in (first, out, q, k, v, *ups, down):
                g.out[z, x, y, c] = g.shard[...]
            stream.wait(*cot_in)
            r.cot_f[...] = r.cot_t[:n].T
            greeted(nz)
            first.lines()
            q.lines()
            k.lines()
            fill_waves(r, feat)
            first.sides()
            v.lines()
            q.sides()
            out.lines()
            k.sides()
            ups[0].lines()
            v.sides()
            first.corners()
            ups[1].lines()
            q.corners()
            down.lines()
            k.corners()
            first.cores()
            first.whole()
            stamps(flat(r.first, slice(128, 128 + feat)))
            v.corners()
            out.sides()
            begin(range(0, seqs // 2))
            q.cores()
            ups[0].sides()
            begin(range(seqs // 2, seqs))
            k.cores()
            q.whole()
            multiply(0, flat(r.qkv[0]))
            v.cores()
            out.corners()
            ups[1].sides()
            for g in ups[2:]:
                g.lines()
            k.whole()
            multiply(1, flat(r.qkv[1]))
            down.arrived()
            needs[0][1].sides()
            v.whole()
            multiply(2, flat(r.qkv[2]))
            ups[0].corners()
            out.cores()
            leave(0, 1)

        def out_weights():
            out.whole()
            r.out_t[...] = flat(r.out).T
            leave(*range(6, 8 + parts))

        def item(i):
            views = []
            for k in range(pair):
                cols = block_at(i * pair + k, length)
                views.append((proj.at[:, cols], r.scores.at[pl.ds(k * HEADS, HEADS)], r.powers.at[i % 2, k], r.inv.at[i * pair + k], r.mixed.at[:, cols]))
            for project, scores, *_ in views:
                heads.scores(project, scores)
            for project, scores, powers, inverses, mixed in views:
                heads.softmax(scores, powers, inverses)
                heads.mix(project, powers, inverses, mixed)
            stream.start(*powers_copy(i))
            if nz:
                at_step(i, [[out_weights]])
            cols = block_at(i, width)
            table = small()
            middle = r.starts[:, cols] + dot(r.out_t[...], r.mixed[:, cols])
            r.middle[:, cols] = middle
            normed, _ = norm_rows(middle)
            r.low2[:, cols] = (normed * param(table, chars + 2) + param(table, chars + 3)).astype(BF16)

        def weights_step(step):
            if not nz:
                return []
            cores = lambda p: (1, 2, 2, 4)[p] if p < 4 else p // 2 + 3
            corners = lambda p: 0 if p < 3 else 3 if p < 5 else p // 4 + 3
            acts = [part.cores for p, part in enumerate(order) if cores(p) == step]
            acts += [part.corners for p, part in enumerate(order) if p > 0 and corners(p) == step]
            return acts + [part.sides for part in order[2 * step + 3:2 * step + 5]]

        def sums_step(step):
            if not nz:
                return []
            return [(g.corners, g.sides, g.lines)[step - j - 1] for j, g in enumerate(groups) if 0 <= step - j - 1 < 3]

        middles, ends = [], []
        if nz:
            middles = [[groups[-1].corners], [groups[-1].sides, groups[-3].lines]]
            ends = [[groups[-2].sides], [groups[-2].lines], [groups[-1].lines]]

        def tile(j):
            rows = block_at(j, wide)
            if nz:
                at_step(j, [[part.whole for part in some] for some in needs])
                r.up[:, rows] = flat(r.ups.at[j])
                r.tile_down[...] = flat(r.down.at[pl.ds(j, 1)])
            else:
                r.up[:, rows] = r.w_up[:, rows]
                r.tile_down[...] = r.w_down[rows, :]
            r.up_t[...] = r.up[:, rows].T
            r.down_t[:, rows] = r.tile_down[...].T
            for t in range(chunks):
                cols = pl.ds(t * chunk, chunk)
                for half in range(2):
                    some = pl.ds(half * wide // 2, wide // 2)
                    part = block_at(2 * j + half, wide // 2)
                    r.act[part, cols], r.gh[part, cols] = gelu_parts(
                        dot(r.up_t[some, :], r.low2[:, cols]), dot(r.tile_down[some, :], r.cot_f[:, cols]))
            at_step(j, [weights_step(items + k) + sums_step(k) for k in range(tiles)])
            d_up = dot_nt(r.low2[...], r.gh[rows, :]).astype(BF16)
            if nz:
                r.mine[j] = d_up.reshape(blocks(per, wide))
                at_step(j, [[g.cores] for g in groups])
            else:
                r.d_up[:, rows] = d_up

        def layer_back(m):
            cols, rows = block_at(m, chunk), block_at(m, share)
            r.gn[...] = dot(r.up[...], r.gh[:, cols])
            at_step(m, middles)
            r.cot_t[rows, :] = dot_nt(r.act[rows, :], r.cot_f[...]).astype(BF16)
            stream.start(*d_down_copy(m))
            normed, inverse = norm_rows(r.middle[:, cols])
            grad_normed = r.gn[...]
            grad = r.cot_f[:, cols].astype(F32) + norm_rows_back(grad_normed, param(small(), chars + 2), normed, inverse)
            r.starts[:, cols] = grad
            r.low2[:, cols] = grad.astype(BF16)
            r.ln[0] += fold(grad_normed * normed)
            r.ln[1] += fold(grad_normed)
            stream.start(*grad_copy(m))

        prelude()

        def items_loop(i, _):
            @pl.when(i >= 2)
            def _():
                stream.wait(*powers_copy(i - 2))
            item(i)
            at_step(i, [weights_step(k) for k in range(items)])
            return 0
        lax.fori_loop(0, items, items_loop, 0)
        left(0, 1)
        leave(2, 3)

        def tiles_loop(j, _):
            tile(j)
            return 0
        lax.fori_loop(0, tiles, tiles_loop, 0)
        leave(4, 5)

        def chunks_loop(m, _):
            layer_back(m)
            at_step(m, ends)
            return 0
        lax.fori_loop(0, chunks, chunks_loop, 0)
        stream.start(*ln_copy)
        r.d_out[...] = dot_nt(r.mixed[...], r.low2[...]).astype(BF16)
        stream.start(*d_out_copy)
        if nz:
            for g in (first, *qkv, out, *ups, down):
                g.finish()
            for j in range(tiles):
                r.o_up[:, j * wide:(j + 1) * wide] = groups[j].total()
        left(*range(2, len(to_hbm)))
        stream.wait(*d_out_copy)
        stream.wait(*ln_copy)
        for i in range(max(items - 2, 0), items):
            stream.wait(*powers_copy(i))
        for m in range(chunks):
            stream.wait(*d_down_copy(m))
            stream.wait(*grad_copy(m))

    return call.run(kernel, "forward_and_ffn", None, 0 if nz else None)


def backward(nz, chars, tokens, small, w_qkv, w_out, saved, chunk=512):
    feat, n = saved.start_o.shape
    seqs = saved.powers_o.shape[0]
    ff = saved.act_o.shape[0]
    length = n // seqs
    pair = 2 if seqs % 2 == 0 else 1
    items, width, chunks = seqs // pair, pair * length, n // chunk
    heads = Heads(feat)
    vmem = lambda kind, *shape: pltpu.VMEM(shape, kind)
    there = lambda value: (value, ANYWHERE)
    call = Call()
    call.arg(tok=(tokens.reshape(seqs, 1, length), RESIDENT), waves=(saved.waves, RESIDENT), inv=(saved.inv, RESIDENT), small_i=there(small),
             qkv_i=there(w_qkv), out_i=there(w_out), start_i=there(saved.start_o), grad_i=there(saved.grad_o), project_i=there(saved.project_o),
             powers_i=there(saved.powers_o), mixed_i=there(saved.mixed_o), ln2_i=there(saved.ln_o),
             middle_i=there(saved.middle_o), act_i=there(saved.act_o), down_i=there(saved.down_o))
    call.out(d_in=((feat, n), F32, ANYWHERE), result=((feat, n), F32, ANYWHERE))
    call.temp(small=vmem(BF16, feat, 128), qkv=vmem(BF16, feat, 3 * feat), w_out=vmem(BF16, feat, feat), start=vmem(F32, feat, n),
              grad=vmem(F32, feat, n), project=vmem(BF16, 2, 3 * feat, width), powers=vmem(BF16, 2, pair, HEADS, length, length),
              mixed=vmem(BF16, feat, n), ln2=vmem(F32, 2, feat, 128), middle=vmem(F32, feat, n), act=vmem(BF16, 2, ff, chunk),
              down_t=vmem(BF16, feat, ff), ln1=vmem(F32, 2, feat, 128), d_char=vmem(F32, feat, 128), low_f=vmem(BF16, feat, n),
              gp_f=vmem(BF16, 3 * feat, n), scores=vmem(F32, pair * HEADS, length, length),
              grads=vmem(BF16, pair * HEADS, length, length), grad_mixed=vmem(F32, feat, width), scaled=vmem(BF16, feat, width),
              lean=vmem(F32, seqs, HEADS, length), gn=vmem(F32, feat, width), sems=pltpu.SemaphoreType.DMA((12 + 4 * items + chunks,)))
    parts = 4
    if nz:
        devices = nz * 8
        per, down_per = feat // devices, ff // devices
        blocks = (nz,) + BLOCKS
        call.arg(d_down=there(saved.d_down_o.reshape(blocks + (down_per, feat))), d_out_i=there(saved.d_out_o.reshape(blocks + (per, feat))))
        small_out = lambda *shape: (shape, F32, RESIDENT)
        call.out(o_out=small_out(per, feat), o_down=small_out(down_per, feat), o_qkv=small_out(per, 3 * feat), o_time=small_out(per, feat),
                 o_char=small_out(per, chars), o_ln=small_out(4, per))
        call.temp(down_sums=Scatter.scratch(nz, (down_per, feat)), rest_sums=Scatter.scratch(nz, (per, 128 + feat)),
                  at_sums=Scatter.scratch(nz, (per, feat)) * parts, kept=vmem(BF16, nz, 2, 2, down_per, feat),
                  d_at=[vmem(BF16, *blocks, per, feat)] * parts, d_rest=vmem(BF16, *blocks, per, 128 + feat))
    else:
        call.out(d_at=((feat, 3 * feat), BF16, RESIDENT), d_rest=((feat, 128 + feat), BF16, RESIDENT))

    def kernel(r):
        stream = Stream(r.sems)
        if nz:
            c = place()[3]
            down = Scatter(nz, r.d_down, r.down_sums, r.kept)
            *ats, out = [Scatter(nz, r.d_at[p], r.at_sums[5 * p:5 * p + 5]) for p in range(parts)]
            rest = Scatter(nz, r.d_rest, r.rest_sums)

        def tall(value):
            value = value.astype(BF16)
            return value.reshape(blocks + (per, value.shape[-1])) if nz else value

        def columns(i):
            return block_at(i, width)

        fixed = [(r.out_i, r.w_out), (r.small_i.at[:, pl.ds(0, 128)], r.small), (r.qkv_i, r.qkv), (r.ln2_i, r.ln2), (r.middle_i, r.middle),
                 (r.down_i, r.down_t)]
        if nz:
            fixed += [(r.d_down.at[pl.ds(0, nz), :, :, c], r.kept), (r.d_out_i, r.d_at[3])]

        def fetch(*numbers):
            for k in numbers:
                stream.start(k, *fixed[k])

        def fetched(*numbers):
            for k in numbers:
                stream.wait(k, *fixed[k])

        def item_copies(i):
            cols = columns(i)
            return [(12 + i, r.grad_i.at[:, cols], r.grad.at[:, cols]), (12 + items + i, r.start_i.at[:, cols], r.start.at[:, cols]),
                    (12 + 2 * items + i, r.mixed_i.at[:, cols], r.mixed.at[:, cols]), (8 + i % 2, r.project_i.at[:, cols], r.project.at[i % 2]),
                    (10 + i % 2, r.powers_i.at[pl.ds(i * pair, pair)], r.powers.at[i % 2])]

        def d_in_copy(i):
            return 12 + 3 * items + i, r.start.at[:, columns(i)], r.d_in.at[:, columns(i)]

        def act_copy(m):
            return 8 + m % 2, r.act_i.at[:, block_at(m, chunk)], r.act.at[m % 2]

        def result_copy(m):
            cols = block_at(m, chunk)
            return 12 + 4 * items + m, r.middle.at[:, cols], r.result.at[:, cols]

        def norm_again(i):
            normed, _ = norm_rows(r.start[:, columns(i)])
            r.low_f[:, columns(i)] = (normed * param(r.small[...], chars) + param(r.small[...], chars + 1)).astype(BF16)

        def product(p):
            value = tall(dot_nt(r.low_f[...], r.gp_f[p * feat:(p + 1) * feat, :]))
            if nz:
                r.d_at[p][...] = value
                ats[p].cores()
            else:
                r.d_at[:, p * feat:(p + 1) * feat] = value

        def layer_back(i):
            r.gn[...] = dot(r.qkv[...], r.gp_f[:, columns(i)])
            grad_normed = r.gn[...]
            normed, inverse = norm_rows(r.start[:, columns(i)])
            d_in = r.grad[:, columns(i)] + norm_rows_back(grad_normed, param(r.small[...], chars), normed, inverse)
            r.start[:, columns(i)] = d_in
            stream.start(*d_in_copy(i))
            r.ln1[0] += fold(grad_normed * normed)
            r.ln1[1] += fold(grad_normed)
            one_hot = jnp.concatenate([one_hot_of(r.tok[i * pair + k], i * pair + k) for k in range(pair)], axis=1)
            high = d_in.astype(BF16)
            low = (d_in - high.astype(F32)).astype(BF16)
            r.d_char[...] += dot_nt(high, one_hot) + dot_nt(low, one_hot)

        def rest_products():
            lane = lax.broadcasted_iota(jnp.int32, r.d_char.shape, 1)
            sums = r.d_char[...]
            table = jnp.where(lane < chars, sums, 0.0)
            for k, ref in enumerate((r.ln1.at[0], r.ln1.at[1], r.ln2.at[0], r.ln2.at[1])):
                table = jnp.where(lane == chars + k, jnp.sum(ref[...], axis=1, keepdims=True), table)
            stamps = jnp.concatenate([sums[:, ITEM_HIGH:], sums[:, :ITEM_HIGH]], axis=1)
            stamps = jnp.where(lane < seqs, stamps, 0.0).astype(BF16)
            r.d_rest[..., :128] = tall(table)
            r.d_rest[..., 128:] = tall(dot_nt(r.waves[...], stamps))

        def result(m):
            cols = block_at(m, chunk)
            stream.wait(*act_copy(m))
            r.middle[:, cols] = r.middle[:, cols] + dot(r.down_t[...], r.act[m % 2])
            stream.start(*result_copy(m))

            @pl.when(m + 2 < chunks)
            def _():
                stream.start(*act_copy(m + 2))

        def item(i):
            copies = item_copies(i)
            stream.wait(*copies[0])
            grad_low = r.grad[:, columns(i)].astype(BF16)
            r.grad_mixed[...] = dot(r.w_out[...], grad_low).astype(BF16).astype(F32)
            stream.wait(*copies[1])
            at_step(i, [[lambda: fetched(1)]])
            norm_again(i)
            for copy in copies[2:]:
                stream.wait(*copy)
            if nz:
                at_step(i, [[lambda: fetch(6, 7), lambda: greeted(nz), down.cores]])

            @pl.when(i + 1 < items)
            def _():
                for copy in item_copies(i + 1):
                    stream.start(*copy)
            views = []
            for k in range(pair):
                here, number = pl.ds(k * length, length), i * pair + k
                cols, group = block_at(number, length), pl.ds(k * HEADS, HEADS)
                views.append((r.project.at[i % 2, :, here], r.scaled.at[:, here], r.powers.at[i % 2, k], r.scores.at[group], r.grads.at[group], cols))
                heads.scale_grad(r.grad_mixed.at[:, here], r.inv.at[number], r.mixed.at[:, cols], r.scaled.at[:, here], r.lean.at[number])
            for project, scaled, powers, scores, grads, cols in views:
                heads.grad_probs(project, scaled, scores)
            for k, (project, scaled, powers, scores, grads, cols) in enumerate(views):
                heads.grad_scores(powers, scores, r.lean.at[i * pair + k], grads)
                heads.grad_project(project, scaled, powers, grads, r.gp_f, cols)

        if nz:
            greet(nz)
        fetch(0)
        first_copies = item_copies(0)
        stream.start(*first_copies[0])
        fetch(1)
        for copy in first_copies[1:]:
            stream.start(*copy)
        r.ln1[...] = jnp.zeros_like(r.ln1)
        r.d_char[...] = jnp.zeros_like(r.d_char)
        fetched(0)

        def items_loop(i, _):
            item(i)
            if nz:
                at_step(i, [[lambda: fetched(6, 7), down.corners, out.cores], [out.corners], [down.sides, out.sides]])
            return 0
        lax.fori_loop(0, items, items_loop, 0)
        fetch(2, 3, 4, 5)
        for m in range(2):
            stream.start(*act_copy(m))
        product(0)
        product(1)
        if nz:
            ats[0].corners()
        fetched(2)

        def back_loop(i, _):
            layer_back(i)
            if nz:
                at_step(i, [[ats[1].corners, down.lines], [ats[0].sides, out.lines], [ats[1].sides], [ats[0].lines]])
            return 0
        lax.fori_loop(0, items, back_loop, 0)
        fetched(3)
        rest_products()
        fetched(4, 5)
        if nz:
            rest.cores()
        product(2)
        if nz:
            rest.corners()
            ats[1].lines()

        def result_loop(m, _):
            result(m)
            if nz:
                at_step(m, [[ats[2].corners]] + [[]] * (chunks - 4) + [[rest.sides], [ats[2].sides], [rest.lines]])
            return 0
        lax.fori_loop(0, chunks, result_loop, 0)
        if nz:
            r.o_down[...] = down.total()
            r.o_out[...] = out.total()
            for p in range(2):
                r.o_qkv[:, p * feat:(p + 1) * feat] = ats[p].total()
            ats[2].lines()
            total = rest.total()
            r.o_time[...] = total[:, 128:]
            r.o_char[...] = total[:, :chars]
            r.o_ln[...] = total[:, :128].T[chars:chars + 4]
            r.o_qkv[:, 2 * feat:] = ats[2].total()
        for i in range(items):
            stream.wait(*d_in_copy(i))
        for m in range(chunks):
            stream.wait(*result_copy(m))

    return call.run(kernel, "backward", None, 1 if nz else None)


def hand_over(result, d_in, ln, *others, width=1024):
    feat, n = d_in.shape
    call = Call()
    turned = ((n, feat), F32, pl.BlockSpec((width, feat), lambda i: (i, 0)))
    call.arg(result=(result, lanes(feat, width)), d_in=(d_in, lanes(feat, width)), ln=(ln, whole(ln.shape)))
    call.arg(**{f"a{k}": (value, whole(value.shape)) for k, value in enumerate(others)})
    call.out(o_result=turned, o_d_in=turned, **{f"l{k}": ((1, ln.shape[1]), F32, whole((1, ln.shape[1]))) for k in range(4)})
    call.out(**{f"o{k}": (value.shape, F32, whole(value.shape)) for k, value in enumerate(others)})

    def kernel(r):
        r.o_result[...] = r.result[...].T
        r.o_d_in[...] = r.d_in[...].T

        @pl.when(pl.program_id(0) == 0)
        def _():
            for k, ref in enumerate((r.l0, r.l1, r.l2, r.l3)):
                ref[...] = r.ln[k:k + 1]
            for k in range(len(others)):
                getattr(r, f"o{k}")[...] = getattr(r, f"a{k}")[...]

    got = call.run(kernel, "hand_over", n // width)
    return got.o_result, got.o_d_in, [getattr(got, f"l{k}") for k in range(4)], [getattr(got, f"o{k}") for k in range(len(others))]


def make_body(gx, gy):
    def gathered(*shards):
        return [lax.all_gather(s, AXES, axis=0, tiled=True) for s in shards]

    def summed(part):
        return lax.psum_scatter(part.astype(F32), AXES, scatter_dimension=0, tiled=True)

    def body(tokens, timesteps, cotangent, char_table, time_weight, ln1_gain, ln1_bias, w_qkv, w_attn_out, ln2_gain, ln2_bias, w_up, w_down):
        feat = time_weight.shape[1]
        chars = char_table.shape[0]
        per = feat // (gx * gy)
        nz = gx // 2 if gy == 4 and gx % 8 == 0 and per % 16 == 0 else 0
        shards = [char_table.T, ln1_gain, ln1_bias, ln2_gain, ln2_bias, time_weight, w_qkv, w_attn_out, w_up, w_down]
        if not nz:
            shards = gathered(*shards)
        saved = forward(nz, tokens, timesteps, cotangent, *shards)
        if nz:
            small, w_qkv, w_out = (value.reshape(feat, value.shape[-1]) for value in (saved.first_o, saved.qkv_o, saved.out_o))
            got = backward(nz, chars, tokens, small, w_qkv, w_out, saved)
            ln, sums = got.o_ln, (got.o_char, got.o_time, got.o_qkv, got.o_out, saved.o_up, got.o_down)
        else:
            got = backward(nz, chars, tokens, saved.small, *shards[6:8], saved)
            up, down, at, rest = (summed(p) for p in (saved.d_up, saved.d_down_o, got.d_at, got.d_rest))
            ln, sums = rest[:, chars:chars + 4].T, (rest[:, :chars], rest[:, 128:], at, summed(saved.d_out_o), up, down)
        result, d_in, lns, (char, time, qkv, out, up, down) = hand_over(got.result, got.d_in, ln, *sums)
        g1, b1, g2, b2 = (value.reshape(per) for value in lns)
        return result, d_in, char.T, time, g1, b1, qkv, out, g2, b2, up, down
    return body


def solution(mesh):
    every = P(AXES)
    rows, cols = P(AXES, None), P(None, AXES)
    return jax.shard_map(
        make_body(mesh.shape[AXES[0]], mesh.shape[AXES[1]]),
        mesh=mesh,
        in_specs=(every, every, rows, cols, rows, every, every, rows, rows, every, every, rows, rows),
        out_specs=(rows, rows, cols, rows, every, every, rows, rows, every, every, rows, rows),
        check_vma=False,
    )
```
